32 devices in a mesh: gx: 4 (over y, x), gy: 2 (over core), gz: 4 (over z).
Axes of the slice: x: 2, y: 2, z: 4, core: 2. Of those that a mesh axis runs over, the one named last changes fastest.
Arguments:
- cell_weight: float32 [16, 32, 512], P('gx', 'gy', 'gz'), may hold values from 0.3 to 3
- weight_grad: float32 [16, 32, 512], P('gx', 'gy', 'gz'), may hold values from -4 to 4
- material: int32 [16, 32, 512], P('gx', 'gy', 'gz'), may hold values from 0 to 7
- modulus: float32 [8], replicated, may hold values from 0.25 to 2
- node_mass: float32 [16, 32, 512], P('gx', 'gy', 'gz'), may hold values from 0.05 to 0.5
- pinned: int32 [16, 32, 512], P('gx', 'gy', 'gz'), may hold values 0 or 1
- positions: float32 [3, 16, 32, 512], P(None, 'gx', 'gy', 'gz'), may hold values from -6 to 6
- forces: float32 [3, 16, 32, 512], P(None, 'gx', 'gy', 'gz'), may hold values from -6 to 6
Outputs:
- iterate: float32 [3, 16, 32, 512], P(None, 'gx', 'gy', 'gz')
- level_one: float32 [27, 8, 16, 256], P(None, 'gx', 'gy', 'gz')
The draws below stay inside these ranges and needn't reach their ends.
All inputs are finite; a program needn't handle non-finite values. No bound on the sum of `pinned` on one device may be relied on, other than what follows from the above.
Results may differ from the reference program's by a relative error of at most 0.0065.
Values sent between devices are 32-bit elements; how exact they have to be, the bound alone decides.
No kernel may reach another device: no remote copies, remote signals or barrier semaphores. Data moves between devices by JAX's collectives and lax.ppermute only.
A program may use at most 64 MiB of HBM per device.

```python
import math
import jax
import jax.numpy as jnp
import numpy as np
from jax import lax

MATERIALS = 8
NX = 16
NY = 32
NZ = 512


def touch_ends(array, rng, least, high):
    place = [jax.random.randint(jax.random.fold_in(rng, axis), (), 0, length) for axis, length in enumerate(array.shape)]
    longest = array.shape.index(max(array.shape))
    next_to = place[:longest] + [(place[longest] + 1) % array.shape[longest]] + place[longest + 1:]
    return array.at[tuple(place)].set(least).at[tuple(next_to)].set(high)


def block_levels(stream_key, shape, pieces, smallest, largest):
    def one(axis_at, blocks):
        draws = jax.random.uniform(jax.random.fold_in(jax.random.fold_in(stream_key, 6), axis_at), (blocks,), jnp.float32, smallest / len(pieces), largest / len(pieces))
        return jnp.repeat(jnp.exp(draws), shape[axis_at] // blocks).reshape((-1,) + (1,) * (len(shape) - axis_at - 1))

    loudness = one(*pieces[0])
    for cut in pieces[1:]:
        loudness = loudness * one(*cut)
    return loudness


def normal_values(own_key, shape, deviation, reach, pieces=(), held_as=jnp.bfloat16):
    values = deviation * jax.random.normal(own_key, shape, jnp.float32)
    if pieces:
        values = values * block_levels(own_key, shape, pieces, -0.22, 0.18)
    return jnp.clip(values, -reach, reach).astype(held_as)


def setup_inputs(seed: int = 0) -> dict:
    arg_keys = jax.random.split(jax.random.key(seed), 9)
    return {
        "cell_weight": jnp.clip(jnp.exp(math.log(3.0) - 2.3025851 * jax.random.uniform(arg_keys[0], (NX, NY, NZ), jnp.float32) ** block_levels(arg_keys[0], (NX, NY, NZ), ((0, 4), (1, 2), (2, 4)), -0.2, 0.2)), 0.3, 3.0),
        "weight_grad": normal_values(arg_keys[1], (NX, NY, NZ), 1.0, 4.0, ((0, 4), (1, 2), (2, 4)), jnp.float32),
        "material": touch_ends(jax.random.randint(arg_keys[2], (NX, NY, NZ), 0, MATERIALS), jax.random.fold_in(arg_keys[2], 1), 0, MATERIALS - 1).astype(jnp.int32),
        "modulus": jnp.clip(jnp.exp(jax.random.uniform(arg_keys[3], (MATERIALS,), jnp.float32, math.log(0.25), math.log(2.0))), 0.25, 2.0),
        "node_mass": jnp.clip(jnp.exp(math.log(0.5) - 2.3025851 * jax.random.uniform(arg_keys[4], (NX, NY, NZ), jnp.float32) ** block_levels(arg_keys[4], (NX, NY, NZ), ((0, 4), (1, 2), (2, 4)), -0.2, 0.2)), 0.05, 0.5),
        "pinned": touch_ends((jax.random.randint(arg_keys[5], (NX, NY, NZ), 0, 16) < 1).astype(jnp.int32), jax.random.fold_in(arg_keys[5], 1), 0, 1),
        "positions": normal_values(arg_keys[6], (3, NX, NY, NZ), 1.0, 6.0, ((1, 4), (2, 2), (3, 4)), jnp.float32),
        "forces": normal_values(arg_keys[7], (3, NX, NY, NZ), 1.0, 6.0, ((1, 4), (2, 2), (3, 4)), jnp.float32),
    }


OMEGA = 0.6
LEARN_RATE = 0.5
PIN_WEIGHT = 4.0
ELEMENT_TERMS = (1.0 / 3.0, 0.0, -1.0 / 12.0, -1.0 / 12.0)


def offset_list():
    return [(shift_x, shift_y, shift_z) for shift_x in (-1, 0, 1) for shift_y in (-1, 0, 1) for shift_z in (-1, 0, 1)]


def corner_list():
    return [(bit_x, bit_y, bit_z) for bit_x in (0, 1) for bit_y in (0, 1) for bit_z in (0, 1)]


def hat_weight(distance):
    if distance == 0:
        return 1.0
    if abs(distance) == 1:
        return 0.5
    return 0.0


def galerkin_tables():
    offsets = offset_list()
    tables = np.zeros((27, 27, 27), np.float32)
    for slot_a, outer in enumerate(offsets):
        for slot_c, coarse in enumerate(offsets):
            for slot_f, inner in enumerate(offsets):
                factor = 1.0
                for axis_pos in range(3):
                    factor *= hat_weight(outer[axis_pos]) * hat_weight(2 * coarse[axis_pos] - outer[axis_pos] - inner[axis_pos])
                tables[slot_a, slot_c, slot_f] = factor
    return tables


def stiffness_of(cell_weight, weight_grad, material, modulus):
    lookup = jnp.zeros(cell_weight.shape, jnp.float32)
    for index in range(modulus.shape[0]):
        lookup = lookup + jnp.where(material == index, modulus[index], 0.0)
    return cell_weight * jnp.exp(-LEARN_RATE * weight_grad) * lookup


def assemble(cell_rim, node_mass, pinned_weight):
    node_shape = node_mass.shape
    rows_out = []
    for offset in offset_list():
        total = jnp.zeros(node_shape, jnp.float32)
        for corner in corner_list():
            if all(0 <= corner[axis_pos] + offset[axis_pos] <= 1 for axis_pos in range(3)):
                total = total + cell_rim[1 - corner[0]:1 - corner[0] + node_shape[0],
                                         1 - corner[1]:1 - corner[1] + node_shape[1],
                                         1 - corner[2]:1 - corner[2] + node_shape[2]]
        nonzero = sum(1 for axis_pos in range(3) if offset[axis_pos] != 0)
        entry = ELEMENT_TERMS[nonzero] * total
        if nonzero == 0:
            entry = entry + node_mass + PIN_WEIGHT * pinned_weight
        rows_out.append(entry)
    return jnp.stack(rows_out)


def galerkin(op_rim, coarse_shape):
    tables = jnp.asarray(galerkin_tables())
    result = None
    for slot_a, outer in enumerate(offset_list()):
        piece = op_rim[:, outer[0] + 1:outer[0] + 1 + 2 * coarse_shape[0]:2,
                       outer[1] + 1:outer[1] + 1 + 2 * coarse_shape[1]:2,
                       outer[2] + 1:outer[2] + 1 + 2 * coarse_shape[2]:2]
        term = jnp.einsum('pk,kxyz->pxyz', tables[slot_a], piece, precision=lax.Precision.HIGHEST)
        result = term if result is None else result + term
    return result


def stencil_apply(stencil, padded):
    node_shape = stencil.shape[1:]
    result = None
    for slot, offset in enumerate(offset_list()):
        window = padded[:, 1 + offset[0]:1 + offset[0] + node_shape[0],
                        1 + offset[1]:1 + offset[1] + node_shape[1],
                        1 + offset[2]:1 + offset[2] + node_shape[2]]
        term = stencil[slot][None] * window
        result = term if result is None else result + term
    return result


def relax(stencil, field, rhs_field, padded):
    return field + OMEGA * (rhs_field - stencil_apply(stencil, padded)) / stencil[13][None]


def restrict_axis(field, axis_pos, coarse_len):
    below = lax.slice_in_dim(field, 0, 2 * coarse_len - 1, 2, axis_pos)
    centre = lax.slice_in_dim(field, 1, 2 * coarse_len, 2, axis_pos)
    above = lax.slice_in_dim(field, 2, 2 * coarse_len + 1, 2, axis_pos)
    return 0.5 * below + centre + 0.5 * above


def restrict(rim_field, coarse_shape):
    field = rim_field
    for axis_pos in (1, 2, 3):
        field = restrict_axis(field, axis_pos, coarse_shape[axis_pos - 1])
    return field


def prolong_axis(field, axis_pos, coarse_len):
    lower = lax.slice_in_dim(field, 0, coarse_len, 1, axis_pos)
    upper = lax.slice_in_dim(field, 1, coarse_len + 1, 1, axis_pos)
    middle = 0.5 * (lower + upper)
    paired = jnp.stack([lower, middle], axis=axis_pos + 1)
    new_shape = list(lower.shape)
    new_shape[axis_pos] = 2 * coarse_len
    return paired.reshape(new_shape)


def prolong(rim_field, coarse_shape):
    field = rim_field
    for axis_pos in (1, 2, 3):
        field = prolong_axis(field, axis_pos, coarse_shape[axis_pos - 1])
    return field


def pad_lower(field):
    return jnp.pad(field, ((0, 0), (1, 0), (1, 0), (1, 0)))


def pad_upper(field):
    return jnp.pad(field, ((0, 0), (0, 1), (0, 1), (0, 1)))


def pad_both(field):
    return jnp.pad(field, ((0, 0), (1, 1), (1, 1), (1, 1)))


def reference(cell_weight, weight_grad, material, modulus, node_mass, pinned, positions, forces):
    stiffness = stiffness_of(cell_weight, weight_grad, material, modulus)
    fine_shape = node_mass.shape
    mid_shape = tuple(extent // 2 for extent in fine_shape)
    low_shape = tuple(extent // 4 for extent in fine_shape)
    level_zero = assemble(jnp.pad(stiffness, ((1, 0), (1, 0), (1, 0))), node_mass, pinned.astype(jnp.float32))
    level_one = galerkin(pad_lower(level_zero), mid_shape)
    level_two = galerkin(pad_lower(level_one), low_shape)
    iterate = positions
    for sweep in range(2):
        iterate = relax(level_zero, iterate, forces, pad_both(iterate))
    residual_zero = forces - stencil_apply(level_zero, pad_both(iterate))
    rhs_one = restrict(pad_lower(residual_zero), mid_shape)
    corr_one = OMEGA * rhs_one / level_one[13][None]
    corr_one = relax(level_one, corr_one, rhs_one, pad_both(corr_one))
    residual_one = rhs_one - stencil_apply(level_one, pad_both(corr_one))
    rhs_two = restrict(pad_lower(residual_one), low_shape)
    corr_two = OMEGA * rhs_two / level_two[13][None]
    for sweep in range(3):
        corr_two = relax(level_two, corr_two, rhs_two, pad_both(corr_two))
    corr_one = corr_one + prolong(pad_upper(corr_two), low_shape)
    for sweep in range(2):
        corr_one = relax(level_one, corr_one, rhs_one, pad_both(corr_one))
    iterate = iterate + prolong(pad_upper(corr_one), mid_shape)
    for sweep in range(2):
        iterate = relax(level_zero, iterate, forces, pad_both(iterate))
    return iterate, level_one
```

```python
import jax
import jax.numpy as jnp
import numpy as np
from jax import lax
from jax.experimental import pallas as pl
from jax.experimental.pallas import tpu as pltpu
from jax.sharding import PartitionSpec as P

OMEGA = 0.6
LEARN_RATE = 0.5
PIN_WEIGHT = 4.0
ELEMENT_TERMS = (1.0 / 3.0, 0.0, -1.0 / 12.0, -1.0 / 12.0)


def shifted(x, axis, by):
    peers = lax.axis_size(axis)
    pairs = [(i, i + by) for i in range(peers) if 0 <= i + by < peers]
    return lax.ppermute(x, axis, pairs)


def extended(block, sides, width):
    for axis, dim in sides:
        count = lax.axis_size(axis)
        forward = [(i, i + 1) for i in range(count - 1)]
        backward = [(target, source) for source, target in forward]
        low = lax.ppermute(
            lax.slice_in_dim(block, block.shape[dim] - width, None, axis=dim), axis, forward
        )
        high = lax.ppermute(lax.slice_in_dim(block, 0, width, axis=dim), axis, backward)
        block = jnp.concatenate([low, block, high], axis=dim)
    return block


def offset_list():
    return [
        (shift_x, shift_y, shift_z)
        for shift_x in (-1, 0, 1)
        for shift_y in (-1, 0, 1)
        for shift_z in (-1, 0, 1)
    ]


def corner_list():
    return [(bit_x, bit_y, bit_z) for bit_x in (0, 1) for bit_y in (0, 1) for bit_z in (0, 1)]


def hat_weight(distance):
    if distance == 0:
        return 1.0
    if abs(distance) == 1:
        return 0.5
    return 0.0


def galerkin_tables():
    offsets = offset_list()
    tables = np.zeros((27, 27, 27), np.float32)
    for slot_a, outer in enumerate(offsets):
        for slot_c, coarse in enumerate(offsets):
            for slot_f, inner in enumerate(offsets):
                factor = 1.0
                for axis_pos in range(3):
                    factor *= hat_weight(outer[axis_pos]) * hat_weight(
                        2 * coarse[axis_pos] - outer[axis_pos] - inner[axis_pos]
                    )
                tables[slot_a, slot_c, slot_f] = factor
    return tables


def stiffness_of(cell_weight, weight_grad, material, modulus):
    lookup = jnp.zeros(cell_weight.shape, jnp.float32)
    for index in range(modulus.shape[0]):
        lookup = lookup + jnp.where(material == index, modulus[index], 0.0)
    return cell_weight * jnp.exp(-LEARN_RATE * weight_grad) * lookup


def assemble(cell_rim, node_mass, pinned_weight):
    node_shape = node_mass.shape
    rows_out = []
    for offset in offset_list():
        total = jnp.zeros(node_shape, jnp.float32)
        for corner in corner_list():
            if all((0 <= corner[axis_pos] + offset[axis_pos] <= 1 for axis_pos in range(3))):
                total = (
                    total
                    + cell_rim[
                        1 - corner[0] : 1 - corner[0] + node_shape[0],
                        1 - corner[1] : 1 - corner[1] + node_shape[1],
                        1 - corner[2] : 1 - corner[2] + node_shape[2],
                    ]
                )
        nonzero = sum((1 for axis_pos in range(3) if offset[axis_pos] != 0))
        entry = ELEMENT_TERMS[nonzero] * total
        if nonzero == 0:
            entry = entry + node_mass + PIN_WEIGHT * pinned_weight
        rows_out.append(entry)
    return jnp.stack(rows_out)


def galerkin(op_rim, coarse_shape):
    tables = jnp.asarray(galerkin_tables())
    result = None
    for slot_a, outer in enumerate(offset_list()):
        piece = op_rim[
            :,
            outer[0] + 1 : outer[0] + 1 + 2 * coarse_shape[0] : 2,
            outer[1] + 1 : outer[1] + 1 + 2 * coarse_shape[1] : 2,
            outer[2] + 1 : outer[2] + 1 + 2 * coarse_shape[2] : 2,
        ]
        term = jnp.einsum("pk,kxyz->pxyz", tables[slot_a], piece, precision=lax.Precision.HIGHEST)
        result = term if result is None else result + term
    return result


def stencil_apply(stencil, padded):
    node_shape = stencil.shape[1:]
    result = None
    for slot, offset in enumerate(offset_list()):
        window = padded[
            :,
            1 + offset[0] : 1 + offset[0] + node_shape[0],
            1 + offset[1] : 1 + offset[1] + node_shape[1],
            1 + offset[2] : 1 + offset[2] + node_shape[2],
        ]
        term = stencil[slot][None] * window
        result = term if result is None else result + term
    return result


def relax(stencil, field, rhs_field, padded):
    return field + OMEGA * (rhs_field - stencil_apply(stencil, padded)) / stencil[13][None]


def restrict_axis(field, axis_pos, coarse_len):
    below = lax.slice_in_dim(field, 0, 2 * coarse_len - 1, 2, axis_pos)
    centre = lax.slice_in_dim(field, 1, 2 * coarse_len, 2, axis_pos)
    above = lax.slice_in_dim(field, 2, 2 * coarse_len + 1, 2, axis_pos)
    return 0.5 * below + centre + 0.5 * above


def restrict(rim_field, coarse_shape):
    field = rim_field
    for axis_pos in (1, 2, 3):
        field = restrict_axis(field, axis_pos, coarse_shape[axis_pos - 1])
    return field


def prolong_axis(field, axis_pos, coarse_len):
    lower = lax.slice_in_dim(field, 0, coarse_len, 1, axis_pos)
    upper = lax.slice_in_dim(field, 1, coarse_len + 1, 1, axis_pos)
    middle = 0.5 * (lower + upper)
    paired = jnp.stack([lower, middle], axis=axis_pos + 1)
    new_shape = list(lower.shape)
    new_shape[axis_pos] = 2 * coarse_len
    return paired.reshape(new_shape)


def prolong(rim_field, coarse_shape):
    field = rim_field
    for axis_pos in (1, 2, 3):
        field = prolong_axis(field, axis_pos, coarse_shape[axis_pos - 1])
    return field


def boundary_layer(field, axis_pos, forward):
    extent = field.shape[axis_pos]
    if forward:
        return lax.slice_in_dim(field, extent - 1, extent, 1, axis_pos)
    return lax.slice_in_dim(field, 0, 1, 1, axis_pos)


def attach(field, layer_in, axis_pos, forward):
    if forward:
        return jnp.concatenate([layer_in, field], axis=axis_pos)
    return jnp.concatenate([field, layer_in], axis=axis_pos)


def extend(field, leading, forward):
    step = 1 if forward else -1
    got_x = shifted(boundary_layer(field, leading, forward), "gx", step)
    field = attach(field, got_x, leading, forward)
    got_y = shifted(boundary_layer(field, leading + 1, forward), "gy", step)
    field = attach(field, got_y, leading + 1, forward)
    got_z = shifted(boundary_layer(field, leading + 2, forward), "gz", step)
    return attach(field, got_z, leading + 2, forward)


def faces(field):
    return extended(field, (("gx", 1), ("gy", 2), ("gz", 3)), 1)


def shards(cell_weight, weight_grad, material, modulus, node_mass, pinned, positions, forces):
    stiffness = stiffness_of(cell_weight, weight_grad, material, modulus)
    fine_shape = node_mass.shape
    mid_shape = tuple((extent // 2 for extent in fine_shape))
    low_shape = tuple((extent // 4 for extent in fine_shape))
    pinned_weight = pinned.astype(jnp.float32)
    level_zero = assemble(extend(stiffness, 0, True), node_mass, pinned_weight)
    zero_rim = extend(level_zero, 1, True)
    level_one = galerkin(zero_rim, mid_shape)
    level_two = galerkin(extend(level_one, 1, True), low_shape)
    iterate = positions
    for sweep in range(2):
        iterate = relax(level_zero, iterate, forces, faces(iterate))
    residual_zero = forces - stencil_apply(level_zero, faces(iterate))
    rhs_one = restrict(extend(residual_zero, 1, True), mid_shape)
    corr_one = OMEGA * rhs_one / level_one[13][None]
    corr_one = relax(level_one, corr_one, rhs_one, faces(corr_one))
    residual_one = rhs_one - stencil_apply(level_one, faces(corr_one))
    rhs_two = restrict(extend(residual_one, 1, True), low_shape)
    corr_two = OMEGA * rhs_two / level_two[13][None]
    for sweep in range(3):
        corr_two = relax(level_two, corr_two, rhs_two, faces(corr_two))
    corr_one = corr_one + prolong(extend(corr_two, 1, False), low_shape)
    for sweep in range(2):
        corr_one = relax(level_one, corr_one, rhs_one, faces(corr_one))
    iterate = iterate + prolong(extend(corr_one, 1, False), mid_shape)
    for sweep in range(2):
        iterate = relax(level_zero, iterate, forces, faces(iterate))
    return (iterate, level_one)


LANES = 128
ROWS = 8
TILE = (ROWS, LANES)
SNAKE = (0, 1, 3, 2)


def lane_roll(x, by):
    return pltpu.roll(x, by % LANES, x.ndim - 1)


def row_roll(x, by):
    return pltpu.roll(x, by % ROWS, x.ndim - 2)


def lane_ids(shape):
    return lax.broadcasted_iota(jnp.int32, shape, len(shape) - 1)


def row_ids(shape):
    return lax.broadcasted_iota(jnp.int32, shape, len(shape) - 2)


def x_below(x):
    return jnp.where(lane_ids(x.shape) >= 32, lane_roll(x, 32), 0.0)


def x_above(x):
    return jnp.where(lane_ids(x.shape) < 96, lane_roll(x, -32), 0.0)


def y_below(x):
    return jnp.where(row_ids(x.shape) >= 1, row_roll(x, 1), 0.0)


def y_above(x):
    return jnp.where(row_ids(x.shape) < ROWS - 1, row_roll(x, -1), 0.0)


def z_below(x):
    return lane_roll(x, 1)


def z_above(x):
    return lane_roll(x, -1)


def swap_groups(parts, unit):
    group = lane_ids(TILE) // unit
    parts = list(parts)
    for bit in (1, 2):
        low = (group & bit) == 0
        for i in range(4):
            if i & bit == 0:
                a, b = parts[i], parts[i + bit]
                parts[i] = jnp.where(low, a, lane_roll(b, unit * bit))
                parts[i + bit] = jnp.where(low, lane_roll(a, -unit * bit), b)
    return parts


def three_pieces(x):
    first = x.astype(jnp.bfloat16)
    rest = x - first.astype(jnp.float32)
    second = rest.astype(jnp.bfloat16)
    third = (rest - second.astype(jnp.float32)).astype(jnp.bfloat16)
    return first, second, third


def reorder(x, table):
    total = None
    for piece in three_pieces(x):
        term = jnp.dot(piece, table, preferred_element_type=jnp.float32)
        total = term if total is None else total + term
    return total


def pack_table():
    table = np.zeros((512, 512), np.float32)
    for xp in range(4):
        for z in range(128):
            t, q, p = z // 32, (z % 32) // 4, z % 4
            table[xp * 128 + z, t * 128 + xp * 32 + p * 8 + q] = 1.0
    return table


def coarse_table():
    table = np.zeros((512, 512), np.float32)
    for t in range(4):
        for o in range(4):
            for xp in range(2):
                for zp in range(2):
                    for zq in range(8):
                        src = t * 128 + o * 32 + xp * 16 + zp * 8 + zq
                        table[src, o * 128 + xp * 64 + 16 * t + 2 * zq + zp] = 1.0
    return table


def pack_kernel(mod_ref, cw_ref, wg_ref, mat_ref, mass_ref, pin_ref, pos_ref, force_ref, table_ref, out_ref):
    material = mat_ref[...]
    lookup = jnp.zeros(material.shape, jnp.float32)
    for index in range(mod_ref.shape[0]):
        lookup = jnp.where(material == index, mod_ref[index], lookup)
    stiff = cw_ref[...] * jnp.exp(-LEARN_RATE * wg_ref[...]) * lookup
    mass = mass_ref[...] + PIN_WEIGHT * pin_ref[...].astype(jnp.float32)
    fields = [stiff, mass] + [pos_ref[c] for c in range(3)] + [force_ref[c] for c in range(3)]
    rows = [jnp.concatenate([field[x] for x in range(4)], axis=-1) for field in fields]
    moved = reorder(jnp.concatenate(rows, axis=0), table_ref[...])
    for t in range(4):
        for f in range(8):
            out_ref[t, f] = moved[16 * f:16 * f + 16, 128 * t:128 * t + 128]


def unpack_kernel(idx_ref, own_ref, got_ref, table_ref, coarse_ref, iterate_ref, level_ref):
    take_own = idx_ref[0] == 1

    def block(t):
        j = idx_ref[1 + t]
        return jnp.where(take_own, own_ref[j], got_ref[j])

    whole = jnp.concatenate([block(t) for t in range(4)], axis=-1)
    fine = reorder(whole[:48], table_ref[...])
    for c in range(3):
        for x in range(4):
            iterate_ref[c, x] = fine[16 * c:16 * c + 16, 128 * x:128 * x + 128]
    coarse = reorder(whole[48:], coarse_ref[...])
    for o in range(27):
        for x in range(2):
            col = (o % 4) * 128 + x * 64
            level_ref[o, x] = coarse[8 * (o // 4):8 * (o // 4) + 8, col:col + 64]


def fill_low(ref, n):
    ref[0, 1:, 1:] = x_below(ref[n, 1:, 1:])
    ref[:, 0, 1:] = y_below(ref[:, n, 1:])
    ref[:, :, 0] = z_below(ref[:, :, n])


def fill_both(ref, n):
    mid = slice(1, n + 1)
    ref[0, mid, mid] = x_below(ref[n, mid, mid])
    ref[n + 1, mid, mid] = x_above(ref[1, mid, mid])
    ref[:, 0, mid] = y_below(ref[:, n, mid])
    ref[:, n + 1, mid] = y_above(ref[:, 1, mid])
    ref[:, :, 0] = z_below(ref[:, :, n])
    ref[:, :, n + 1] = z_above(ref[:, :, 1])


def coarsen(low, mid, high, low_before, mid_before, high_before):
    out = []
    for i in range(len(mid) // 2):
        if i:
            mid_b, high_b, low_b = mid[2 * i - 1], high[2 * i - 1], low[2 * i - 1]
        else:
            mid_b, high_b, low_b = mid_before, high_before, low_before
        down = 0.5 * (low[2 * i] + low_b) + 0.25 * mid_b
        here = mid[2 * i] + 0.5 * (low[2 * i] + high[2 * i] + low[2 * i + 1] + high_b) + 0.25 * (
            mid[2 * i + 1] + mid_b
        )
        up = 0.5 * (high[2 * i] + high[2 * i + 1]) + 0.25 * mid[2 * i + 1]
        out.append((down, here, up))
    return out


def triple_product(src, mid_a, mid_b, dst, n):
    half = n // 2

    def pass_x(j, carry):
        parts = [[src[9 * f + j, i] for i in range(n)] for f in range(3)]
        before = [x_below(part[n - 1]) for part in parts]
        for i, trio in enumerate(coarsen(*parts, *before)):
            for c in range(3):
                mid_a[9 * c + j, i] = trio[c]
        return carry

    lax.fori_loop(0, 9, pass_x, 0)

    def pass_y(j, carry):
        base = 9 * (j // 3) + j % 3
        parts = [[mid_a[base + 3 * f, :, i] for i in range(n)] for f in range(3)]
        before = [y_below(part[n - 1]) for part in parts]
        for i, trio in enumerate(coarsen(*parts, *before)):
            for c in range(3):
                mid_b[base + 3 * c, :, i] = trio[c]
        return carry

    lax.fori_loop(0, 9, pass_y, 0)

    def pass_z(j, carry):
        parts = [[mid_b[3 * j + f, :, :, i] for i in range(n)] for f in range(3)]
        before = [z_below(part[n - 1]) for part in parts]
        for i, trio in enumerate(coarsen(*parts, *before)):
            for c in range(3):
                dst[3 * j + c, :, :, i] = trio[c]
        return carry

    lax.fori_loop(0, 9, pass_z, 0)


def sweep(level, field, n, store, skip_faces):
    def body(step, carry):
        x, y = step // n, step % n
        sums = [[None] * n for _ in range(3)]
        for o0 in range(3):
            for o1 in range(3):
                columns = [[field[c, x + o0, y + o1, z] for z in range(n + 2)] for c in range(3)]
                for o2 in range(3):
                    if skip_faces and (o0 != 1) + (o1 != 1) + (o2 != 1) == 1:
                        continue
                    for z in range(n):
                        coef = level[9 * o0 + 3 * o1 + o2, x, y, z]
                        for c in range(3):
                            term = coef * columns[c][z + o2]
                            sums[c][z] = term if sums[c][z] is None else sums[c][z] + term
        for c in range(3):
            for z in range(n):
                store(c, x, y, z, sums[c][z])
        return carry

    if n == 1:
        body(0, 0)
    else:
        lax.fori_loop(0, n * n, body, 0)


def relax_into(level, weight, rhs, src, dst, n, skip_faces=False):
    def store(c, x, y, z, value):
        dst[c, 1 + x, 1 + y, 1 + z] = src[c, 1 + x, 1 + y, 1 + z] + weight[x, y, z] * (rhs[c, x, y, z] - value)

    sweep(level, src, n, store, skip_faces)


def residual_down(level, rhs, src, res, coarse_rhs, n, skip_faces=False):
    half = n // 2

    def store(c, x, y, z, value):
        res[c, 1 + x, 1 + y, 1 + z] = rhs[c, x, y, z] - value

    sweep(level, src, n, store, skip_faces)

    def body(c, carry):
        fill_low(res.at[c], n)
        for i in range(half):
            part = 0.5 * (res[c, 2 * i] + res[c, 2 * i + 2]) + res[c, 2 * i + 1]
            for j in range(half):
                line = 0.5 * (part[2 * j] + part[2 * j + 2]) + part[2 * j + 1]
                for k in range(half):
                    coarse_rhs[c, i, j, k] = 0.5 * (line[2 * k] + line[2 * k + 2]) + line[2 * k + 1]
        return carry

    lax.fori_loop(0, 3, body, 0)


def add_prolonged(coarse, fine, inside, half):
    def between(values):
        out = []
        for i in range(half):
            out += [values[i], 0.5 * (values[i] + values[i + 1])]
        return out

    def body(c, carry):
        planes = between([coarse[c, 1 + i, 1:, 1:] for i in range(half + 1)])
        for x, plane in enumerate(planes):
            for y, line in enumerate(between([plane[j] for j in range(half + 1)])):
                for z, value in enumerate(between([line[k] for k in range(half + 1)])):
                    fine[c, 1 + x, 1 + y, 1 + z] += jnp.where(inside, value, 0.0)
        return carry

    lax.fori_loop(0, 3, body, 0)


def fill_all(ref, n):
    def body(c, carry):
        fill_both(ref.at[c], n)
        return carry

    lax.fori_loop(0, 3, body, 0)


def cycle_kernel(
    idx_ref, prev_ref, own_ref, next_ref, out_ref,
    fields, cells, level_a, weight_a, mid_a, mid_b, level_b, weight_b, mid_c, mid_d, level_c, weight_c,
    va, va2, vb, vb2, vc, vc2, res_a, res_b, rhs_b, rhs_c,
):
    gx_prev, gx_own, gx_next = idx_ref[0], idx_ref[1], idx_ref[2]
    slab = (lane_ids(TILE) // 8) % 4
    inside = (slab == 1) | ((slab == 0) & (idx_ref[3] == 1)) | ((slab == 2) & (idx_ref[4] == 1))

    def arrange(step, carry):
        f = step
        for yp in range(4):
            by_source = []
            for source in range(4):
                tiles = [
                    ref[lax.bitwise_xor(gx, source), f, pl.ds(yp, ROWS, stride=4), :]
                    for ref, gx in ((prev_ref, gx_prev), (own_ref, gx_own), (next_ref, gx_next))
                ]
                by_source.append(swap_groups(tiles + [jnp.zeros(TILE, jnp.float32)], 8))
            for zp in range(4):
                moved = swap_groups([by_source[source][zp] for source in range(4)], 32)
                for xp in range(4):
                    fields[f, xp, yp, zp] = moved[xp]
        return carry

    lax.fori_loop(0, 8, arrange, 0)

    for x in range(4):
        cells[1 + x, 1:, 1:] = fields[0, x] * ELEMENT_TERMS[3]
    fill_low(cells, 4)

    def build(step, carry):
        x, y = step // 4, step % 4
        near = [[[cells[x + 1 - s0, y + 1 - s1, z] for z in range(5)] for s1 in (0, 1)] for s0 in (0, 1)]
        for z in range(4):
            for slot, offset in enumerate(offset_list()):
                nonzero = sum(1 for part in offset if part != 0)
                if nonzero == 1:
                    level_a[slot, x, y, z] = jnp.zeros(TILE, jnp.float32)
                    continue
                total = None
                for s in corner_list():
                    if all(0 <= s[d] + offset[d] <= 1 for d in range(3)):
                        term = near[s[0]][s[1]][z + 1 - s[2]]
                        total = term if total is None else total + term
                if nonzero == 0:
                    total = (ELEMENT_TERMS[0] / ELEMENT_TERMS[3]) * total + fields[1, x, y, z]
                    weight_a[x, y, z] = jnp.where(inside, OMEGA / jnp.where(inside, total, 1.0), 0.0)
                level_a[slot, x, y, z] = total
        return carry

    lax.fori_loop(0, 16, build, 0)

    triple_product(level_a, mid_a, mid_b, level_b, 4)
    weight_b[...] = jnp.where(inside, OMEGA / jnp.where(inside, level_b[13], 1.0), 0.0)
    triple_product(level_b, mid_c, mid_d, level_c, 2)
    weight_c[...] = jnp.where(inside, OMEGA / jnp.where(inside, level_c[13], 1.0), 0.0)

    position, force = fields.at[2:5], fields.at[5:8]

    def load(c, carry):
        for x in range(4):
            va[c, 1 + x, 1:5, 1:5] = position[c, x]
        return carry

    lax.fori_loop(0, 3, load, 0)
    fill_all(va, 4)
    relax_into(level_a, weight_a, force, va, va2, 4, True)
    fill_all(va2, 4)
    relax_into(level_a, weight_a, force, va2, va, 4, True)
    fill_all(va, 4)
    residual_down(level_a, force, va, res_a, rhs_b, 4, True)

    for c in range(3):
        for x in range(2):
            vb[c, 1 + x, 1:3, 1:3] = weight_b[x] * rhs_b[c, x]
    fill_all(vb, 2)
    relax_into(level_b, weight_b, rhs_b, vb, vb2, 2)
    fill_all(vb2, 2)
    residual_down(level_b, rhs_b, vb2, res_b, rhs_c, 2)

    for c in range(3):
        vc[c, 1, 1, 1] = weight_c[0, 0, 0] * rhs_c[c, 0, 0, 0]
    fill_all(vc, 1)
    relax_into(level_c, weight_c, rhs_c, vc, vc2, 1)
    fill_all(vc2, 1)
    relax_into(level_c, weight_c, rhs_c, vc2, vc, 1)
    fill_all(vc, 1)
    relax_into(level_c, weight_c, rhs_c, vc, vc2, 1)
    fill_all(vc2, 1)

    add_prolonged(vc2, vb2, inside, 1)
    fill_all(vb2, 2)
    relax_into(level_b, weight_b, rhs_b, vb2, vb, 2)
    fill_all(vb, 2)
    relax_into(level_b, weight_b, rhs_b, vb, vb2, 2)
    fill_all(vb2, 2)

    add_prolonged(vb2, va, inside, 2)
    fill_all(va, 4)
    relax_into(level_a, weight_a, force, va, va2, 4, True)
    fill_all(va2, 4)
    relax_into(level_a, weight_a, force, va2, va, 4, True)

    def own_slab(tiles):
        total = None
        for group, tile in enumerate(tiles):
            moved = lane_roll(tile, 8 * group - 8)
            total = moved if total is None else jnp.where(slab == group, moved, total)
        return total

    for c in range(3):
        for yp in range(4):
            lines = [own_slab([va[c, 1 + xp, 1 + yp, 1 + zp] for zp in range(4)]) for xp in range(4)]
            for dest, tile in enumerate(swap_groups(lines, 32)):
                out_ref[lax.bitwise_xor(gx_own, dest), pl.ds(32 * c + yp, ROWS, stride=4), :] = tile
    for g in range(7):
        for yp in range(2):
            lines = [
                own_slab([level_b[min(4 * g + o, 26), xp, yp, zp] for xp in range(2) for zp in range(2)])
                for o in range(4)
            ]
            for dest, tile in enumerate(swap_groups(lines, 32)):
                out_ref[lax.bitwise_xor(gx_own, dest), pl.ds(96 + 16 * g + yp, ROWS, stride=2), :] = tile


def slab_place(gx, gz):
    order = jnp.where(gx < 2, gx, 5 - gx)
    return jnp.where(gz % 2 == 0, order, 3 - order)


def slab_owner(place, gz):
    order = place if gz % 2 == 0 else 3 - place
    return SNAKE[order]


def vmem_specs(count):
    return [pl.BlockSpec(memory_space=pltpu.VMEM)] * count


def shards_by_slab(cell_weight, weight_grad, material, modulus, node_mass, pinned, positions, forces):
    table = pack_table()
    smem = pl.BlockSpec(memory_space=pltpu.SMEM)
    gx, gy, gz = lax.axis_index("gx"), lax.axis_index("gy"), lax.axis_index("gz")
    f32 = jnp.float32
    packed = pl.pallas_call(
        pack_kernel,
        out_shape=jax.ShapeDtypeStruct((4, 8, 16, LANES), f32),
        in_specs=[smem] + vmem_specs(8),
        out_specs=vmem_specs(1)[0],
        name="pack",
    )(modulus, cell_weight, weight_grad, material, node_mass, pinned, positions, forces,
      jnp.asarray(table, jnp.bfloat16))

    lower = lax.ppermute(packed, "gy", [(0, 1)])
    block = jnp.concatenate([lower, packed], axis=2)
    by_partner = [
        lax.dynamic_index_in_dim(block, slab_place(gx ^ j, gz), 0, keepdims=False) for j in range(4)
    ]
    own = [by_partner[0]]
    for j in range(1, 4):
        pairs = [(2 * i + 1, 2 * (i ^ j) + 1) for i in range(4)]
        own.append(lax.ppermute(by_partner[j], ("gx", "gy"), pairs))
    own = jnp.stack(own)

    chain = [(slab_owner(place, z) * 2 + 1) * 4 + z for z in range(4) for place in range(4)]
    ahead = list(zip(chain[:-1], chain[1:]))
    behind = [(b, a) for a, b in ahead]
    everywhere = ("gx", "gy", "gz")
    before = lax.ppermute(own, everywhere, ahead)
    after = lax.ppermute(own, everywhere, behind)

    place = slab_place(gx, gz)

    def owner_of(place, z):
        order = jnp.where(z % 2 == 0, place, 3 - place)
        return jnp.where(order < 2, order, 5 - order)

    index = 4 * gz + place
    gx_before = owner_of((index - 1) % 4, (index - 1) // 4)
    gx_after = owner_of((index + 1) % 4, (index + 1) // 4)
    scalars = jnp.stack(
        [gx_before, gx, gx_after, (index > 0).astype(jnp.int32), (index < 15).astype(jnp.int32)]
    ).astype(jnp.int32)

    def buf(*dims):
        return pltpu.VMEM(tuple(dims) + TILE, f32)

    message = pl.pallas_call(
        cycle_kernel,
        out_shape=jax.ShapeDtypeStruct((4, 208, LANES), f32),
        in_specs=[smem] + vmem_specs(3),
        out_specs=vmem_specs(1)[0],
        scratch_shapes=[
            buf(8, 4, 4, 4), buf(5, 5, 5), buf(27, 4, 4, 4), buf(4, 4, 4),
            buf(27, 2, 4, 4), buf(27, 2, 2, 4), buf(27, 2, 2, 2), buf(2, 2, 2),
            buf(27, 1, 2, 2), buf(27, 1, 1, 2), buf(27, 1, 1, 1), buf(1, 1, 1),
            buf(3, 6, 6, 6), buf(3, 6, 6, 6), buf(3, 4, 4, 4), buf(3, 4, 4, 4), buf(3, 3, 3, 3), buf(3, 3, 3, 3),
            buf(3, 5, 5, 5), buf(3, 3, 3, 3), buf(3, 2, 2, 2), buf(3, 1, 1, 1),
        ],
        compiler_params=pltpu.CompilerParams(vmem_limit_bytes=48 * 1024 * 1024),
        name="cycle",
    )(scalars, before, own, after)

    back = [message[0]]
    for j in range(1, 4):
        pairs = [(2 * i + 1, 2 * (i ^ j) + 1) for i in range(4)]
        back.append(lax.ppermute(message[j], ("gx", "gy"), pairs))
    back = jnp.stack(back)
    fine = back[:, :96].reshape(4, 3, 2, 16, LANES)
    coarse = back[:, 96:].reshape(4, 7, 2, 8, LANES)

    def half(side):
        return jnp.concatenate(
            [fine[:, :, side].reshape(4, 48, LANES), coarse[:, :, side].reshape(4, 56, LANES)], axis=1
        )

    got = lax.ppermute(half(0), "gy", [(1, 0)])
    scalars = jnp.stack([gy] + [gx ^ owner_of(t, gz) for t in range(4)]).astype(jnp.int32)
    return pl.pallas_call(
        unpack_kernel,
        out_shape=[
            jax.ShapeDtypeStruct(positions.shape, f32),
            jax.ShapeDtypeStruct((27, 2, 8, 64), f32),
        ],
        in_specs=[smem] + vmem_specs(4),
        out_specs=vmem_specs(2),
        name="unpack",
    )(scalars, half(1), got, jnp.asarray(unpack_table(), jnp.bfloat16), jnp.asarray(coarse_table(), jnp.bfloat16))


def unpack_table():
    return np.ascontiguousarray(pack_table().T)


def solution(mesh):
    placed = (
        P("gx", "gy", "gz"),
        P("gx", "gy", "gz"),
        P("gx", "gy", "gz"),
        P(),
        P("gx", "gy", "gz"),
        P("gx", "gy", "gz"),
        P(None, "gx", "gy", "gz"),
        P(None, "gx", "gy", "gz"),
    )
    sizes = tuple(mesh.shape[axis] for axis in ("gx", "gy", "gz"))

    def choose(cell_weight, *rest):
        fits = sizes == (4, 2, 4) and cell_weight.shape == (4, 16, 128)
        return (shards_by_slab if fits else shards)(cell_weight, *rest)

    return jax.shard_map(
        choose,
        mesh=mesh,
        in_specs=placed,
        out_specs=(P(None, "gx", "gy", "gz"), P(None, "gx", "gy", "gz")),
        check_vma=False,
    )
```

```python
import jax
import jax.numpy as jnp
import numpy as np
from jax import lax
from jax.experimental import pallas as pl
from jax.experimental.pallas import tpu as pltpu
from jax.sharding import PartitionSpec as P

OMEGA = 0.6
LEARN_RATE = 0.5
PIN_WEIGHT = 4.0
ELEMENT_TERMS = (1.0 / 3.0, 0.0, -1.0 / 12.0, -1.0 / 12.0)


def shifted(x, axis, by):
    peers = lax.axis_size(axis)
    pairs = [(i, i + by) for i in range(peers) if 0 <= i + by < peers]
    return lax.ppermute(x, axis, pairs)


def extended(block, sides, width):
    for axis, dim in sides:
        count = lax.axis_size(axis)
        forward = [(i, i + 1) for i in range(count - 1)]
        backward = [(target, source) for source, target in forward]
        low = lax.ppermute(
            lax.slice_in_dim(block, block.shape[dim] - width, None, axis=dim), axis, forward
        )
        high = lax.ppermute(lax.slice_in_dim(block, 0, width, axis=dim), axis, backward)
        block = jnp.concatenate([low, block, high], axis=dim)
    return block


def offset_list():
    return [
        (shift_x, shift_y, shift_z)
        for shift_x in (-1, 0, 1)
        for shift_y in (-1, 0, 1)
        for shift_z in (-1, 0, 1)
    ]


def corner_list():
    return [(bit_x, bit_y, bit_z) for bit_x in (0, 1) for bit_y in (0, 1) for bit_z in (0, 1)]


def hat_weight(distance):
    if distance == 0:
        return 1.0
    if abs(distance) == 1:
        return 0.5
    return 0.0


def galerkin_tables():
    offsets = offset_list()
    tables = np.zeros((27, 27, 27), np.float32)
    for slot_a, outer in enumerate(offsets):
        for slot_c, coarse in enumerate(offsets):
            for slot_f, inner in enumerate(offsets):
                factor = 1.0
                for axis_pos in range(3):
                    factor *= hat_weight(outer[axis_pos]) * hat_weight(
                        2 * coarse[axis_pos] - outer[axis_pos] - inner[axis_pos]
                    )
                tables[slot_a, slot_c, slot_f] = factor
    return tables


def stiffness_of(cell_weight, weight_grad, material, modulus):
    lookup = jnp.zeros(cell_weight.shape, jnp.float32)
    for index in range(modulus.shape[0]):
        lookup = lookup + jnp.where(material == index, modulus[index], 0.0)
    return cell_weight * jnp.exp(-LEARN_RATE * weight_grad) * lookup


def assemble(cell_rim, node_mass, pinned_weight):
    node_shape = node_mass.shape
    rows_out = []
    for offset in offset_list():
        total = jnp.zeros(node_shape, jnp.float32)
        for corner in corner_list():
            if all((0 <= corner[axis_pos] + offset[axis_pos] <= 1 for axis_pos in range(3))):
                total = (
                    total
                    + cell_rim[
                        1 - corner[0] : 1 - corner[0] + node_shape[0],
                        1 - corner[1] : 1 - corner[1] + node_shape[1],
                        1 - corner[2] : 1 - corner[2] + node_shape[2],
                    ]
                )
        nonzero = sum((1 for axis_pos in range(3) if offset[axis_pos] != 0))
        entry = ELEMENT_TERMS[nonzero] * total
        if nonzero == 0:
            entry = entry + node_mass + PIN_WEIGHT * pinned_weight
        rows_out.append(entry)
    return jnp.stack(rows_out)


def galerkin(op_rim, coarse_shape):
    tables = jnp.asarray(galerkin_tables())
    result = None
    for slot_a, outer in enumerate(offset_list()):
        piece = op_rim[
            :,
            outer[0] + 1 : outer[0] + 1 + 2 * coarse_shape[0] : 2,
            outer[1] + 1 : outer[1] + 1 + 2 * coarse_shape[1] : 2,
            outer[2] + 1 : outer[2] + 1 + 2 * coarse_shape[2] : 2,
        ]
        term = jnp.einsum("pk,kxyz->pxyz", tables[slot_a], piece, precision=lax.Precision.HIGHEST)
        result = term if result is None else result + term
    return result


def stencil_apply(stencil, padded):
    node_shape = stencil.shape[1:]
    result = None
    for slot, offset in enumerate(offset_list()):
        window = padded[
            :,
            1 + offset[0] : 1 + offset[0] + node_shape[0],
            1 + offset[1] : 1 + offset[1] + node_shape[1],
            1 + offset[2] : 1 + offset[2] + node_shape[2],
        ]
        term = stencil[slot][None] * window
        result = term if result is None else result + term
    return result


def relax(stencil, field, rhs_field, padded):
    return field + OMEGA * (rhs_field - stencil_apply(stencil, padded)) / stencil[13][None]


def restrict_axis(field, axis_pos, coarse_len):
    below = lax.slice_in_dim(field, 0, 2 * coarse_len - 1, 2, axis_pos)
    centre = lax.slice_in_dim(field, 1, 2 * coarse_len, 2, axis_pos)
    above = lax.slice_in_dim(field, 2, 2 * coarse_len + 1, 2, axis_pos)
    return 0.5 * below + centre + 0.5 * above


def restrict(rim_field, coarse_shape):
    field = rim_field
    for axis_pos in (1, 2, 3):
        field = restrict_axis(field, axis_pos, coarse_shape[axis_pos - 1])
    return field


def prolong_axis(field, axis_pos, coarse_len):
    lower = lax.slice_in_dim(field, 0, coarse_len, 1, axis_pos)
    upper = lax.slice_in_dim(field, 1, coarse_len + 1, 1, axis_pos)
    middle = 0.5 * (lower + upper)
    paired = jnp.stack([lower, middle], axis=axis_pos + 1)
    new_shape = list(lower.shape)
    new_shape[axis_pos] = 2 * coarse_len
    return paired.reshape(new_shape)


def prolong(rim_field, coarse_shape):
    field = rim_field
    for axis_pos in (1, 2, 3):
        field = prolong_axis(field, axis_pos, coarse_shape[axis_pos - 1])
    return field


def boundary_layer(field, axis_pos, forward):
    extent = field.shape[axis_pos]
    if forward:
        return lax.slice_in_dim(field, extent - 1, extent, 1, axis_pos)
    return lax.slice_in_dim(field, 0, 1, 1, axis_pos)


def attach(field, layer_in, axis_pos, forward):
    if forward:
        return jnp.concatenate([layer_in, field], axis=axis_pos)
    return jnp.concatenate([field, layer_in], axis=axis_pos)


def extend(field, leading, forward):
    step = 1 if forward else -1
    got_x = shifted(boundary_layer(field, leading, forward), "gx", step)
    field = attach(field, got_x, leading, forward)
    got_y = shifted(boundary_layer(field, leading + 1, forward), "gy", step)
    field = attach(field, got_y, leading + 1, forward)
    got_z = shifted(boundary_layer(field, leading + 2, forward), "gz", step)
    return attach(field, got_z, leading + 2, forward)


def faces(field):
    return extended(field, (("gx", 1), ("gy", 2), ("gz", 3)), 1)


def shards(cell_weight, weight_grad, material, modulus, node_mass, pinned, positions, forces):
    stiffness = stiffness_of(cell_weight, weight_grad, material, modulus)
    fine_shape = node_mass.shape
    mid_shape = tuple((extent // 2 for extent in fine_shape))
    low_shape = tuple((extent // 4 for extent in fine_shape))
    pinned_weight = pinned.astype(jnp.float32)
    level_zero = assemble(extend(stiffness, 0, True), node_mass, pinned_weight)
    zero_rim = extend(level_zero, 1, True)
    level_one = galerkin(zero_rim, mid_shape)
    level_two = galerkin(extend(level_one, 1, True), low_shape)
    iterate = positions
    for sweep in range(2):
        iterate = relax(level_zero, iterate, forces, faces(iterate))
    residual_zero = forces - stencil_apply(level_zero, faces(iterate))
    rhs_one = restrict(extend(residual_zero, 1, True), mid_shape)
    corr_one = OMEGA * rhs_one / level_one[13][None]
    corr_one = relax(level_one, corr_one, rhs_one, faces(corr_one))
    residual_one = rhs_one - stencil_apply(level_one, faces(corr_one))
    rhs_two = restrict(extend(residual_one, 1, True), low_shape)
    corr_two = OMEGA * rhs_two / level_two[13][None]
    for sweep in range(3):
        corr_two = relax(level_two, corr_two, rhs_two, faces(corr_two))
    corr_one = corr_one + prolong(extend(corr_two, 1, False), low_shape)
    for sweep in range(2):
        corr_one = relax(level_one, corr_one, rhs_one, faces(corr_one))
    iterate = iterate + prolong(extend(corr_one, 1, False), mid_shape)
    for sweep in range(2):
        iterate = relax(level_zero, iterate, forces, faces(iterate))
    return (iterate, level_one)


LANES = 128
ROWS = 8
TILE = (ROWS, LANES)
SNAKE = (0, 1, 3, 2)


def lane_roll(x, by):
    return pltpu.roll(x, by % LANES, x.ndim - 1)


def row_roll(x, by):
    return pltpu.roll(x, by % ROWS, x.ndim - 2)


def lane_ids(shape):
    return lax.broadcasted_iota(jnp.int32, shape, len(shape) - 1)


def row_ids(shape):
    return lax.broadcasted_iota(jnp.int32, shape, len(shape) - 2)


def x_below(x):
    return jnp.where(lane_ids(x.shape) >= 32, lane_roll(x, 32), 0.0)


def x_above(x):
    return jnp.where(lane_ids(x.shape) < 96, lane_roll(x, -32), 0.0)


def y_below(x):
    return jnp.where(row_ids(x.shape) >= 1, row_roll(x, 1), 0.0)


def y_above(x):
    return jnp.where(row_ids(x.shape) < ROWS - 1, row_roll(x, -1), 0.0)


def z_below(x):
    return lane_roll(x, 1)


def z_above(x):
    return lane_roll(x, -1)


def swap_groups(parts, unit):
    group = lane_ids(TILE) // unit
    parts = list(parts)
    for bit in (1, 2):
        low = (group & bit) == 0
        for i in range(4):
            if i & bit == 0:
                a, b = parts[i], parts[i + bit]
                parts[i] = jnp.where(low, a, lane_roll(b, unit * bit))
                parts[i + bit] = jnp.where(low, lane_roll(a, -unit * bit), b)
    return parts


def three_pieces(x):
    first = x.astype(jnp.bfloat16)
    rest = x - first.astype(jnp.float32)
    second = rest.astype(jnp.bfloat16)
    third = (rest - second.astype(jnp.float32)).astype(jnp.bfloat16)
    return first, second, third


def reorder(x, table):
    total = None
    for piece in three_pieces(x):
        term = jnp.dot(piece, table, preferred_element_type=jnp.float32)
        total = term if total is None else total + term
    return total


def pack_table():
    table = np.zeros((512, 512), np.float32)
    for xp in range(4):
        for z in range(128):
            t, q, p = z // 32, (z % 32) // 4, z % 4
            table[xp * 128 + z, t * 128 + xp * 32 + p * 8 + q] = 1.0
    return table


def coarse_table():
    table = np.zeros((512, 512), np.float32)
    for t in range(4):
        for o in range(4):
            for xp in range(2):
                for zp in range(2):
                    for zq in range(8):
                        src = t * 128 + o * 32 + xp * 16 + zp * 8 + zq
                        table[src, o * 128 + xp * 64 + 16 * t + 2 * zq + zp] = 1.0
    return table


def pack_kernel(mod_ref, cw_ref, wg_ref, mat_ref, mass_ref, pin_ref, pos_ref, force_ref, table_ref, out_ref):
    material = mat_ref[...]
    lookup = jnp.zeros(material.shape, jnp.float32)
    for index in range(mod_ref.shape[0]):
        lookup = jnp.where(material == index, mod_ref[index], lookup)
    stiff = cw_ref[...] * jnp.exp(-LEARN_RATE * wg_ref[...]) * lookup
    mass = mass_ref[...] + PIN_WEIGHT * pin_ref[...].astype(jnp.float32)
    fields = [stiff, mass] + [pos_ref[c] for c in range(3)] + [force_ref[c] for c in range(3)]
    rows = [jnp.concatenate([field[x] for x in range(4)], axis=-1) for field in fields]
    moved = reorder(jnp.concatenate(rows, axis=0), table_ref[...])
    for t in range(4):
        for f in range(8):
            out_ref[t, f] = moved[16 * f:16 * f + 16, 128 * t:128 * t + 128]


def unpack_kernel(idx_ref, in_ref, table_ref, coarse_ref, iterate_ref, level_ref):
    whole = jnp.concatenate([in_ref[idx_ref[t]] for t in range(4)], axis=-1)
    fine = reorder(whole[:48], table_ref[...])
    for c in range(3):
        for x in range(4):
            iterate_ref[c, x] = fine[16 * c:16 * c + 16, 128 * x:128 * x + 128]
    coarse = reorder(whole[48:], coarse_ref[...])
    for o in range(27):
        for x in range(2):
            col = (o % 4) * 128 + x * 64
            level_ref[o, x] = coarse[8 * (o // 4):8 * (o // 4) + 8, col:col + 64]


def fill_low(ref, n):
    ref[0, 1:, 1:] = x_below(ref[n, 1:, 1:])
    ref[:, 0, 1:] = y_below(ref[:, n, 1:])
    ref[:, :, 0] = z_below(ref[:, :, n])


def fill_both(ref, n):
    mid = slice(1, n + 1)
    ref[0, mid, mid] = x_below(ref[n, mid, mid])
    ref[n + 1, mid, mid] = x_above(ref[1, mid, mid])
    ref[:, 0, mid] = y_below(ref[:, n, mid])
    ref[:, n + 1, mid] = y_above(ref[:, 1, mid])
    ref[:, :, 0] = z_below(ref[:, :, n])
    ref[:, :, n + 1] = z_above(ref[:, :, 1])


def coarsen(low, mid, high, low_before, mid_before, high_before):
    out = []
    for i in range(len(mid) // 2):
        if i:
            mid_b, high_b, low_b = mid[2 * i - 1], high[2 * i - 1], low[2 * i - 1]
        else:
            mid_b, high_b, low_b = mid_before, high_before, low_before
        down = 0.5 * (low[2 * i] + low_b) + 0.25 * mid_b
        here = mid[2 * i] + 0.5 * (low[2 * i] + high[2 * i] + low[2 * i + 1] + high_b) + 0.25 * (
            mid[2 * i + 1] + mid_b
        )
        up = 0.5 * (high[2 * i] + high[2 * i + 1]) + 0.25 * mid[2 * i + 1]
        out.append((down, here, up))
    return out


def triple_product(src, mid_a, mid_b, dst, n):
    unroll = n == 2

    def pass_x(j, carry):
        parts = [[src[9 * f + j, i] for i in range(n)] for f in range(3)]
        before = [x_below(part[n - 1]) for part in parts]
        for i, trio in enumerate(coarsen(*parts, *before)):
            for c in range(3):
                mid_a[9 * c + j, i] = trio[c]
        return carry

    lax.fori_loop(0, 9, pass_x, 0, unroll=unroll)

    def pass_y(j, carry):
        base = 9 * (j // 3) + j % 3
        parts = [[mid_a[base + 3 * f, :, i] for i in range(n)] for f in range(3)]
        before = [y_below(part[n - 1]) for part in parts]
        for i, trio in enumerate(coarsen(*parts, *before)):
            for c in range(3):
                mid_b[base + 3 * c, :, i] = trio[c]
        return carry

    lax.fori_loop(0, 9, pass_y, 0, unroll=unroll)

    def pass_z(j, carry):
        parts = [[mid_b[3 * j + f, :, :, i] for i in range(n)] for f in range(3)]
        before = [z_below(part[n - 1]) for part in parts]
        for i, trio in enumerate(coarsen(*parts, *before)):
            for c in range(3):
                dst[3 * j + c, :, :, i] = trio[c]
        return carry

    lax.fori_loop(0, 9, pass_z, 0, unroll=unroll)


def sweep(level, field, n, store, skip_faces):
    def body(step, carry):
        x, y = step // n, step % n
        sums = [[None] * n for _ in range(3)]
        for o0 in range(3):
            for o1 in range(3):
                columns = [[field[c, x + o0, y + o1, z] for z in range(n + 2)] for c in range(3)]
                for o2 in range(3):
                    if skip_faces and (o0 != 1) + (o1 != 1) + (o2 != 1) == 1:
                        continue
                    for z in range(n):
                        coef = level[9 * o0 + 3 * o1 + o2, x, y, z]
                        for c in range(3):
                            term = coef * columns[c][z + o2]
                            sums[c][z] = term if sums[c][z] is None else sums[c][z] + term
        for c in range(3):
            for z in range(n):
                store(c, x, y, z, sums[c][z])
        return carry

    lax.fori_loop(0, n * n, body, 0, unroll=n < 4)


def relax_into(level, weight, rhs, src, dst, n, skip_faces=False):
    def store(c, x, y, z, value):
        dst[c, 1 + x, 1 + y, 1 + z] = src[c, 1 + x, 1 + y, 1 + z] + weight[x, y, z] * (rhs[c, x, y, z] - value)

    sweep(level, src, n, store, skip_faces)


def residual_down(level, rhs, src, res, coarse_rhs, n, skip_faces=False):
    half = n // 2

    def store(c, x, y, z, value):
        res[c, 1 + x, 1 + y, 1 + z] = rhs[c, x, y, z] - value

    sweep(level, src, n, store, skip_faces)

    def body(c, carry):
        fill_low(res.at[c], n)
        for i in range(half):
            part = 0.5 * (res[c, 2 * i] + res[c, 2 * i + 2]) + res[c, 2 * i + 1]
            for j in range(half):
                line = 0.5 * (part[2 * j] + part[2 * j + 2]) + part[2 * j + 1]
                for k in range(half):
                    coarse_rhs[c, i, j, k] = 0.5 * (line[2 * k] + line[2 * k + 2]) + line[2 * k + 1]
        return carry

    lax.fori_loop(0, 3, body, 0, unroll=n < 4)


def add_prolonged(coarse, fine, inside, half):
    def between(values):
        out = []
        for i in range(half):
            out += [values[i], 0.5 * (values[i] + values[i + 1])]
        return out

    def body(c, carry):
        planes = between([coarse[c, 1 + i, 1:, 1:] for i in range(half + 1)])
        for x, plane in enumerate(planes):
            for y, line in enumerate(between([plane[j] for j in range(half + 1)])):
                for z, value in enumerate(between([line[k] for k in range(half + 1)])):
                    fine[c, 1 + x, 1 + y, 1 + z] += jnp.where(inside, value, 0.0)
        return carry

    lax.fori_loop(0, 3, body, 0, unroll=half < 2)


def fill_all(ref, n):
    def body(c, carry):
        fill_both(ref.at[c], n)
        return carry

    lax.fori_loop(0, 3, body, 0, unroll=n < 4)


def cycle_kernel(
    idx_ref, prev_ref, own_ref, next_ref, out_ref,
    fields, cells, level_a, weight_a, mid_a, mid_b, level_b, weight_b, mid_c, mid_d, level_c, weight_c,
    va, va2, vb, vb2, vc, vc2, res_a, res_b, rhs_b, rhs_c,
):
    gx_prev, gx_own, gx_next = idx_ref[0], idx_ref[1], idx_ref[2]
    slab = (lane_ids(TILE) // 8) % 4
    inside = (slab == 1) | ((slab == 0) & (idx_ref[3] == 1)) | ((slab == 2) & (idx_ref[4] == 1))

    def arrange(step, carry):
        f = step
        for yp in range(4):
            by_source = []
            for source in range(4):
                tiles = [
                    ref[lax.bitwise_xor(gx, source), f, pl.ds(yp, ROWS, stride=4), :]
                    for ref, gx in ((prev_ref, gx_prev), (own_ref, gx_own), (next_ref, gx_next))
                ]
                by_source.append(swap_groups(tiles + [jnp.zeros(TILE, jnp.float32)], 8))
            for zp in range(4):
                moved = swap_groups([by_source[source][zp] for source in range(4)], 32)
                for xp in range(4):
                    fields[f, xp, yp, zp] = moved[xp]
        return carry

    lax.fori_loop(0, 8, arrange, 0)

    for x in range(4):
        cells[1 + x, 1:, 1:] = fields[0, x] * ELEMENT_TERMS[3]
    fill_low(cells, 4)

    def build(step, carry):
        x, y = step // 4, step % 4
        near = [[[cells[x + 1 - s0, y + 1 - s1, z] for z in range(5)] for s1 in (0, 1)] for s0 in (0, 1)]
        for z in range(4):
            for slot, offset in enumerate(offset_list()):
                nonzero = sum(1 for part in offset if part != 0)
                if nonzero == 1:
                    level_a[slot, x, y, z] = jnp.zeros(TILE, jnp.float32)
                    continue
                total = None
                for s in corner_list():
                    if all(0 <= s[d] + offset[d] <= 1 for d in range(3)):
                        term = near[s[0]][s[1]][z + 1 - s[2]]
                        total = term if total is None else total + term
                if nonzero == 0:
                    total = (ELEMENT_TERMS[0] / ELEMENT_TERMS[3]) * total + fields[1, x, y, z]
                    weight_a[x, y, z] = jnp.where(inside, OMEGA / jnp.where(inside, total, 1.0), 0.0)
                level_a[slot, x, y, z] = total
        return carry

    lax.fori_loop(0, 16, build, 0)

    triple_product(level_a, mid_a, mid_b, level_b, 4)
    weight_b[...] = jnp.where(inside, OMEGA / jnp.where(inside, level_b[13], 1.0), 0.0)
    triple_product(level_b, mid_c, mid_d, level_c, 2)
    weight_c[...] = jnp.where(inside, OMEGA / jnp.where(inside, level_c[13], 1.0), 0.0)

    position, force = fields.at[2:5], fields.at[5:8]

    def load(c, carry):
        for x in range(4):
            va[c, 1 + x, 1:5, 1:5] = position[c, x]
        return carry

    lax.fori_loop(0, 3, load, 0)
    fill_all(va, 4)
    relax_into(level_a, weight_a, force, va, va2, 4, True)
    fill_all(va2, 4)
    relax_into(level_a, weight_a, force, va2, va, 4, True)
    fill_all(va, 4)
    residual_down(level_a, force, va, res_a, rhs_b, 4, True)

    for c in range(3):
        for x in range(2):
            vb[c, 1 + x, 1:3, 1:3] = weight_b[x] * rhs_b[c, x]
    fill_all(vb, 2)
    relax_into(level_b, weight_b, rhs_b, vb, vb2, 2)
    fill_all(vb2, 2)
    residual_down(level_b, rhs_b, vb2, res_b, rhs_c, 2)

    for c in range(3):
        vc[c, 1, 1, 1] = weight_c[0, 0, 0] * rhs_c[c, 0, 0, 0]
    fill_all(vc, 1)
    relax_into(level_c, weight_c, rhs_c, vc, vc2, 1)
    fill_all(vc2, 1)
    relax_into(level_c, weight_c, rhs_c, vc2, vc, 1)
    fill_all(vc, 1)
    relax_into(level_c, weight_c, rhs_c, vc, vc2, 1)
    fill_all(vc2, 1)

    add_prolonged(vc2, vb2, inside, 1)
    fill_all(vb2, 2)
    relax_into(level_b, weight_b, rhs_b, vb2, vb, 2)
    fill_all(vb, 2)
    relax_into(level_b, weight_b, rhs_b, vb, vb2, 2)
    fill_all(vb2, 2)

    add_prolonged(vb2, va, inside, 2)
    fill_all(va, 4)
    relax_into(level_a, weight_a, force, va, va2, 4, True)
    fill_all(va2, 4)
    relax_into(level_a, weight_a, force, va2, va, 4, True)

    def own_slab(tiles):
        total = None
        for group, tile in enumerate(tiles):
            moved = lane_roll(tile, 8 * group - 8)
            total = moved if total is None else jnp.where(slab == group, moved, total)
        return total

    for c in range(3):
        for yp in range(4):
            lines = [own_slab([va[c, 1 + xp, 1 + yp, 1 + zp] for zp in range(4)]) for xp in range(4)]
            for dest, tile in enumerate(swap_groups(lines, 32)):
                out_ref[lax.bitwise_xor(gx_own, dest), pl.ds(32 * c + yp, ROWS, stride=4), :] = tile
    for g in range(7):
        for yp in range(2):
            lines = [
                own_slab([level_b[min(4 * g + o, 26), xp, yp, zp] for xp in range(2) for zp in range(2)])
                for o in range(4)
            ]
            for dest, tile in enumerate(swap_groups(lines, 32)):
                out_ref[lax.bitwise_xor(gx_own, dest), pl.ds(96 + 16 * g + yp, ROWS, stride=2), :] = tile


def slab_place(gx, gz):
    order = jnp.where(gx < 2, gx, 5 - gx)
    return jnp.where(gz % 2 == 0, order, 3 - order)


def slab_owner(place, gz):
    order = place if gz % 2 == 0 else 3 - place
    return SNAKE[order]


def vmem_specs(count):
    return [pl.BlockSpec(memory_space=pltpu.VMEM)] * count


def shards_by_slab(cell_weight, weight_grad, material, modulus, node_mass, pinned, positions, forces):
    table = pack_table()
    smem = pl.BlockSpec(memory_space=pltpu.SMEM)
    gx, gy, gz = lax.axis_index("gx"), lax.axis_index("gy"), lax.axis_index("gz")
    f32 = jnp.float32
    packed = pl.pallas_call(
        pack_kernel,
        out_shape=jax.ShapeDtypeStruct((4, 8, 16, LANES), f32),
        in_specs=[smem] + vmem_specs(8),
        out_specs=vmem_specs(1)[0],
        name="pack",
    )(modulus, cell_weight, weight_grad, material, node_mass, pinned, positions, forces,
      jnp.asarray(table, jnp.bfloat16))

    place = slab_place(gx, gz)
    index = 4 * gz + place
    mine = [lax.dynamic_index_in_dim(packed, slab_place(gx ^ j, gz), 0, keepdims=False) for j in range(4)]
    for j in range(1, 4):
        mine[j] = lax.ppermute(mine[j], "gx", [(i, i ^ j) for i in range(4)])
    mine = jnp.stack(mine)

    def swap_in_chain(first):
        pairs = []
        for core in range(2):
            chain = [(slab_owner(at, z) * 2 + core) * 4 + z for z in range(4) for at in range(4)]
            for at in range(first, 15, 2):
                pairs += [(chain[at], chain[at + 1]), (chain[at + 1], chain[at])]
            if first:
                pairs += [(chain[end], chain[end] ^ 4) for end in (0, 15)]
        return lax.ppermute(mine, ("gx", "gy", "gz"), pairs)

    even, odd = swap_in_chain(0), swap_in_chain(1)

    def both_halves(half, present):
        other = lax.ppermute(half, "gy", [(0, 1), (1, 0)])
        rows = jnp.concatenate([jnp.where(gy == 0, half, other), jnp.where(gy == 0, other, half)], axis=2)
        return jnp.where(present, rows, 0.0)

    odd_place = index % 2 == 1
    own = both_halves(mine, True)
    even = both_halves(even, True)
    odd = both_halves(odd, (index > 0) & (index < 15))
    before = jnp.where(odd_place, even, odd)
    after = jnp.where(odd_place, odd, even)

    def owner_of(place, z):
        order = jnp.where(z % 2 == 0, place, 3 - place)
        return jnp.where(order < 2, order, 5 - order)

    gx_before = owner_of((index - 1) % 4, (index - 1) // 4)
    gx_after = owner_of((index + 1) % 4, (index + 1) // 4)
    scalars = jnp.stack(
        [gx_before, gx, gx_after, (index > 0).astype(jnp.int32), (index < 15).astype(jnp.int32)]
    ).astype(jnp.int32)

    def buf(*dims):
        return pltpu.VMEM(tuple(dims) + TILE, f32)

    message = pl.pallas_call(
        cycle_kernel,
        out_shape=jax.ShapeDtypeStruct((4, 208, LANES), f32),
        in_specs=[smem] + vmem_specs(3),
        out_specs=vmem_specs(1)[0],
        scratch_shapes=[
            buf(8, 4, 4, 4), buf(5, 5, 5), buf(27, 4, 4, 4), buf(4, 4, 4),
            buf(27, 2, 4, 4), buf(27, 2, 2, 4), buf(27, 2, 2, 2), buf(2, 2, 2),
            buf(27, 1, 2, 2), buf(27, 1, 1, 2), buf(27, 1, 1, 1), buf(1, 1, 1),
            buf(3, 6, 6, 6), buf(3, 6, 6, 6), buf(3, 4, 4, 4), buf(3, 4, 4, 4), buf(3, 3, 3, 3), buf(3, 3, 3, 3),
            buf(3, 5, 5, 5), buf(3, 3, 3, 3), buf(3, 2, 2, 2), buf(3, 1, 1, 1),
        ],
        compiler_params=pltpu.CompilerParams(vmem_limit_bytes=48 * 1024 * 1024),
        name="cycle",
    )(scalars, before, own, after)

    fine = message[:, :96].reshape(4, 3, 2, 16, LANES)
    coarse = message[:, 96:].reshape(4, 7, 2, 8, LANES)

    def half(side):
        return jnp.concatenate(
            [fine[:, :, side].reshape(4, 48, LANES), coarse[:, :, side].reshape(4, 56, LANES)], axis=1
        )

    message = jnp.where(gy == 0, half(0), half(1))
    back = [message[0]]
    for j in range(1, 4):
        back.append(lax.ppermute(message[j], "gx", [(i, i ^ j) for i in range(4)]))
    scalars = jnp.stack([gx ^ owner_of(t, gz) for t in range(4)]).astype(jnp.int32)
    return pl.pallas_call(
        unpack_kernel,
        out_shape=[
            jax.ShapeDtypeStruct(positions.shape, f32),
            jax.ShapeDtypeStruct((27, 2, 8, 64), f32),
        ],
        in_specs=[smem] + vmem_specs(3),
        out_specs=vmem_specs(2),
        name="unpack",
    )(scalars, jnp.stack(back), jnp.asarray(unpack_table(), jnp.bfloat16), jnp.asarray(coarse_table(), jnp.bfloat16))


def unpack_table():
    return np.ascontiguousarray(pack_table().T)


def solution(mesh):
    placed = (
        P("gx", "gy", "gz"),
        P("gx", "gy", "gz"),
        P("gx", "gy", "gz"),
        P(),
        P("gx", "gy", "gz"),
        P("gx", "gy", "gz"),
        P(None, "gx", "gy", "gz"),
        P(None, "gx", "gy", "gz"),
    )
    sizes = tuple(mesh.shape[axis] for axis in ("gx", "gy", "gz"))

    def choose(cell_weight, *rest):
        fits = sizes == (4, 2, 4) and cell_weight.shape == (4, 16, 128)
        return (shards_by_slab if fits else shards)(cell_weight, *rest)

    return jax.shard_map(
        choose,
        mesh=mesh,
        in_specs=placed,
        out_specs=(P(None, "gx", "gy", "gz"), P(None, "gx", "gy", "gz")),
        check_vma=False,
    )
```

```python
import jax
import jax.numpy as jnp
import numpy as np
from jax import lax
from jax.experimental import pallas as pl
from jax.experimental.pallas import tpu as pltpu
from jax.sharding import PartitionSpec as P

OMEGA = 0.6
LEARN_RATE = 0.5
PIN_WEIGHT = 4.0
ELEMENT_TERMS = (1.0 / 3.0, 0.0, -1.0 / 12.0, -1.0 / 12.0)


def shifted(x, axis, by):
    peers = lax.axis_size(axis)
    pairs = [(i, i + by) for i in range(peers) if 0 <= i + by < peers]
    return lax.ppermute(x, axis, pairs)


def extended(block, sides, width):
    for axis, dim in sides:
        count = lax.axis_size(axis)
        forward = [(i, i + 1) for i in range(count - 1)]
        backward = [(target, source) for source, target in forward]
        low = lax.ppermute(
            lax.slice_in_dim(block, block.shape[dim] - width, None, axis=dim), axis, forward
        )
        high = lax.ppermute(lax.slice_in_dim(block, 0, width, axis=dim), axis, backward)
        block = jnp.concatenate([low, block, high], axis=dim)
    return block


def offset_list():
    return [
        (shift_x, shift_y, shift_z)
        for shift_x in (-1, 0, 1)
        for shift_y in (-1, 0, 1)
        for shift_z in (-1, 0, 1)
    ]


def corner_list():
    return [(bit_x, bit_y, bit_z) for bit_x in (0, 1) for bit_y in (0, 1) for bit_z in (0, 1)]


def hat_weight(distance):
    if distance == 0:
        return 1.0
    if abs(distance) == 1:
        return 0.5
    return 0.0


def galerkin_tables():
    offsets = offset_list()
    tables = np.zeros((27, 27, 27), np.float32)
    for slot_a, outer in enumerate(offsets):
        for slot_c, coarse in enumerate(offsets):
            for slot_f, inner in enumerate(offsets):
                factor = 1.0
                for axis_pos in range(3):
                    factor *= hat_weight(outer[axis_pos]) * hat_weight(
                        2 * coarse[axis_pos] - outer[axis_pos] - inner[axis_pos]
                    )
                tables[slot_a, slot_c, slot_f] = factor
    return tables


def stiffness_of(cell_weight, weight_grad, material, modulus):
    lookup = jnp.zeros(cell_weight.shape, jnp.float32)
    for index in range(modulus.shape[0]):
        lookup = lookup + jnp.where(material == index, modulus[index], 0.0)
    return cell_weight * jnp.exp(-LEARN_RATE * weight_grad) * lookup


def assemble(cell_rim, node_mass, pinned_weight):
    node_shape = node_mass.shape
    rows_out = []
    for offset in offset_list():
        total = jnp.zeros(node_shape, jnp.float32)
        for corner in corner_list():
            if all((0 <= corner[axis_pos] + offset[axis_pos] <= 1 for axis_pos in range(3))):
                total = (
                    total
                    + cell_rim[
                        1 - corner[0] : 1 - corner[0] + node_shape[0],
                        1 - corner[1] : 1 - corner[1] + node_shape[1],
                        1 - corner[2] : 1 - corner[2] + node_shape[2],
                    ]
                )
        nonzero = sum((1 for axis_pos in range(3) if offset[axis_pos] != 0))
        entry = ELEMENT_TERMS[nonzero] * total
        if nonzero == 0:
            entry = entry + node_mass + PIN_WEIGHT * pinned_weight
        rows_out.append(entry)
    return jnp.stack(rows_out)


def galerkin(op_rim, coarse_shape):
    tables = jnp.asarray(galerkin_tables())
    result = None
    for slot_a, outer in enumerate(offset_list()):
        piece = op_rim[
            :,
            outer[0] + 1 : outer[0] + 1 + 2 * coarse_shape[0] : 2,
            outer[1] + 1 : outer[1] + 1 + 2 * coarse_shape[1] : 2,
            outer[2] + 1 : outer[2] + 1 + 2 * coarse_shape[2] : 2,
        ]
        term = jnp.einsum("pk,kxyz->pxyz", tables[slot_a], piece, precision=lax.Precision.HIGHEST)
        result = term if result is None else result + term
    return result


def stencil_apply(stencil, padded):
    node_shape = stencil.shape[1:]
    result = None
    for slot, offset in enumerate(offset_list()):
        window = padded[
            :,
            1 + offset[0] : 1 + offset[0] + node_shape[0],
            1 + offset[1] : 1 + offset[1] + node_shape[1],
            1 + offset[2] : 1 + offset[2] + node_shape[2],
        ]
        term = stencil[slot][None] * window
        result = term if result is None else result + term
    return result


def relax(stencil, field, rhs_field, padded):
    return field + OMEGA * (rhs_field - stencil_apply(stencil, padded)) / stencil[13][None]


def restrict_axis(field, axis_pos, coarse_len):
    below = lax.slice_in_dim(field, 0, 2 * coarse_len - 1, 2, axis_pos)
    centre = lax.slice_in_dim(field, 1, 2 * coarse_len, 2, axis_pos)
    above = lax.slice_in_dim(field, 2, 2 * coarse_len + 1, 2, axis_pos)
    return 0.5 * below + centre + 0.5 * above


def restrict(rim_field, coarse_shape):
    field = rim_field
    for axis_pos in (1, 2, 3):
        field = restrict_axis(field, axis_pos, coarse_shape[axis_pos - 1])
    return field


def prolong_axis(field, axis_pos, coarse_len):
    lower = lax.slice_in_dim(field, 0, coarse_len, 1, axis_pos)
    upper = lax.slice_in_dim(field, 1, coarse_len + 1, 1, axis_pos)
    middle = 0.5 * (lower + upper)
    paired = jnp.stack([lower, middle], axis=axis_pos + 1)
    new_shape = list(lower.shape)
    new_shape[axis_pos] = 2 * coarse_len
    return paired.reshape(new_shape)


def prolong(rim_field, coarse_shape):
    field = rim_field
    for axis_pos in (1, 2, 3):
        field = prolong_axis(field, axis_pos, coarse_shape[axis_pos - 1])
    return field


def boundary_layer(field, axis_pos, forward):
    extent = field.shape[axis_pos]
    if forward:
        return lax.slice_in_dim(field, extent - 1, extent, 1, axis_pos)
    return lax.slice_in_dim(field, 0, 1, 1, axis_pos)


def attach(field, layer_in, axis_pos, forward):
    if forward:
        return jnp.concatenate([layer_in, field], axis=axis_pos)
    return jnp.concatenate([field, layer_in], axis=axis_pos)


def extend(field, leading, forward):
    step = 1 if forward else -1
    got_x = shifted(boundary_layer(field, leading, forward), "gx", step)
    field = attach(field, got_x, leading, forward)
    got_y = shifted(boundary_layer(field, leading + 1, forward), "gy", step)
    field = attach(field, got_y, leading + 1, forward)
    got_z = shifted(boundary_layer(field, leading + 2, forward), "gz", step)
    return attach(field, got_z, leading + 2, forward)


def faces(field):
    return extended(field, (("gx", 1), ("gy", 2), ("gz", 3)), 1)


def shards(cell_weight, weight_grad, material, modulus, node_mass, pinned, positions, forces):
    stiffness = stiffness_of(cell_weight, weight_grad, material, modulus)
    fine_shape = node_mass.shape
    mid_shape = tuple((extent // 2 for extent in fine_shape))
    low_shape = tuple((extent // 4 for extent in fine_shape))
    pinned_weight = pinned.astype(jnp.float32)
    level_zero = assemble(extend(stiffness, 0, True), node_mass, pinned_weight)
    zero_rim = extend(level_zero, 1, True)
    level_one = galerkin(zero_rim, mid_shape)
    level_two = galerkin(extend(level_one, 1, True), low_shape)
    iterate = positions
    for sweep in range(2):
        iterate = relax(level_zero, iterate, forces, faces(iterate))
    residual_zero = forces - stencil_apply(level_zero, faces(iterate))
    rhs_one = restrict(extend(residual_zero, 1, True), mid_shape)
    corr_one = OMEGA * rhs_one / level_one[13][None]
    corr_one = relax(level_one, corr_one, rhs_one, faces(corr_one))
    residual_one = rhs_one - stencil_apply(level_one, faces(corr_one))
    rhs_two = restrict(extend(residual_one, 1, True), low_shape)
    corr_two = OMEGA * rhs_two / level_two[13][None]
    for sweep in range(3):
        corr_two = relax(level_two, corr_two, rhs_two, faces(corr_two))
    corr_one = corr_one + prolong(extend(corr_two, 1, False), low_shape)
    for sweep in range(2):
        corr_one = relax(level_one, corr_one, rhs_one, faces(corr_one))
    iterate = iterate + prolong(extend(corr_one, 1, False), mid_shape)
    for sweep in range(2):
        iterate = relax(level_zero, iterate, forces, faces(iterate))
    return (iterate, level_one)


LANES = 128
ROWS = 8
TILE = (ROWS, LANES)
SNAKE = (0, 1, 3, 2)


def lane_roll(x, by):
    return pltpu.roll(x, by % LANES, x.ndim - 1)


def row_roll(x, by):
    return pltpu.roll(x, by % ROWS, x.ndim - 2)


def lane_ids(shape):
    return lax.broadcasted_iota(jnp.int32, shape, len(shape) - 1)


def row_ids(shape):
    return lax.broadcasted_iota(jnp.int32, shape, len(shape) - 2)


def x_below(x):
    return jnp.where(lane_ids(x.shape) >= 32, lane_roll(x, 32), 0.0)


def x_above(x):
    return jnp.where(lane_ids(x.shape) < 96, lane_roll(x, -32), 0.0)


def y_below(x):
    return jnp.where(row_ids(x.shape) >= 1, row_roll(x, 1), 0.0)


def y_above(x):
    return jnp.where(row_ids(x.shape) < ROWS - 1, row_roll(x, -1), 0.0)


def z_below(x):
    return lane_roll(x, 1)


def z_above(x):
    return lane_roll(x, -1)


def swap_groups(parts, unit):
    group = lane_ids(parts[0].shape) // unit
    parts = list(parts)
    for bit in (1, 2):
        low = (group & bit) == 0
        for i in range(4):
            if i & bit == 0:
                a, b = parts[i], parts[i + bit]
                parts[i] = jnp.where(low, a, lane_roll(b, unit * bit))
                parts[i + bit] = jnp.where(low, lane_roll(a, -unit * bit), b)
    return parts


def pick_lanes(x, source):
    return jnp.take_along_axis(x, jnp.broadcast_to(source, x.shape), axis=-1)


def pack_kernel(place_ref, mod_ref, cw_ref, wg_ref, mat_ref, mass_ref, pin_ref, pos_ref, force_ref, out_ref):
    material = mat_ref[...]
    lookup = jnp.zeros(material.shape, jnp.float32)
    for index in range(mod_ref.shape[0]):
        lookup = jnp.where(material == index, mod_ref[index], lookup)
    stiff = cw_ref[...] * jnp.exp(-LEARN_RATE * wg_ref[...]) * lookup
    mass = mass_ref[...] + PIN_WEIGHT * pin_ref[...].astype(jnp.float32)
    fields = [stiff, mass] + [pos_ref[c] for c in range(3)] + [force_ref[c] for c in range(3)]
    lane = lane_ids((16, LANES))
    source = (lane // 32) * 32 + (lane % 8) * 4 + (lane % 32) // 8
    for f, field in enumerate(fields):
        moved = swap_groups([pick_lanes(field[x], source) for x in range(4)], 32)
        for t in range(4):
            out_ref[place_ref[t], f] = moved[t]


def unpack_kernel(place_ref, own_ref, one_ref, two_ref, three_ref, iterate_ref, level_ref, hold):
    for j, ref in enumerate((own_ref, one_ref, two_ref, three_ref)):
        hold[j] = ref[...]
    blocks = [place_ref[t] for t in range(4)]
    lane = lane_ids((16, LANES))
    source = (lane // 32) * 32 + (lane % 4) * 8 + (lane % 32) // 4
    for c in range(3):
        moved = swap_groups([hold[j, 16 * c:16 * c + 16] for j in blocks], 32)
        for x in range(4):
            iterate_ref[c, x] = pick_lanes(moved[x], source)
    lane = lane_ids(TILE)
    source = ((lane % 64) // 16) * 32 + (lane % 2) * 8 + (lane % 16) // 2
    for g in range(7):
        moved = swap_groups([hold[j, 48 + 8 * g:56 + 8 * g] for j in blocks], 32)
        for o in range(4):
            if 4 * g + o < 27:
                for x in range(2):
                    level_ref[4 * g + o, x] = pick_lanes(moved[o], source + 16 * x)[:, :64]


def fill_low(ref, n):
    ref[0, 1:, 1:] = x_below(ref[n, 1:, 1:])
    ref[:, 0, 1:] = y_below(ref[:, n, 1:])
    ref[:, :, 0] = z_below(ref[:, :, n])


def fill_both(ref, n):
    mid = slice(1, n + 1)
    ref[0, mid, mid] = x_below(ref[n, mid, mid])
    ref[n + 1, mid, mid] = x_above(ref[1, mid, mid])
    ref[:, 0, mid] = y_below(ref[:, n, mid])
    ref[:, n + 1, mid] = y_above(ref[:, 1, mid])
    ref[:, :, 0] = z_below(ref[:, :, n])
    ref[:, :, n + 1] = z_above(ref[:, :, 1])


def coarsen(low, mid, high, low_before, mid_before, high_before):
    out = []
    for i in range(len(mid) // 2):
        if i:
            mid_b, high_b, low_b = mid[2 * i - 1], high[2 * i - 1], low[2 * i - 1]
        else:
            mid_b, high_b, low_b = mid_before, high_before, low_before
        down = 0.5 * (low[2 * i] + low_b) + 0.25 * mid_b
        here = mid[2 * i] + 0.5 * (low[2 * i] + high[2 * i] + low[2 * i + 1] + high_b) + 0.25 * (
            mid[2 * i + 1] + mid_b
        )
        up = 0.5 * (high[2 * i] + high[2 * i + 1]) + 0.25 * mid[2 * i + 1]
        out.append((down, here, up))
    return out


def triple_product(src, mid_a, mid_b, dst, n):
    unroll = n == 2

    def pass_x(j, carry):
        parts = [[src[9 * f + j, i] for i in range(n)] for f in range(3)]
        before = [x_below(part[n - 1]) for part in parts]
        for i, trio in enumerate(coarsen(*parts, *before)):
            for c in range(3):
                mid_a[9 * c + j, i] = trio[c]
        return carry

    lax.fori_loop(0, 9, pass_x, 0, unroll=unroll)

    def pass_y(j, carry):
        base = 9 * (j // 3) + j % 3
        parts = [[mid_a[base + 3 * f, :, i] for i in range(n)] for f in range(3)]
        before = [y_below(part[n - 1]) for part in parts]
        for i, trio in enumerate(coarsen(*parts, *before)):
            for c in range(3):
                mid_b[base + 3 * c, :, i] = trio[c]
        return carry

    lax.fori_loop(0, 9, pass_y, 0, unroll=unroll)

    def pass_z(j, carry):
        parts = [[mid_b[3 * j + f, :, :, i] for i in range(n)] for f in range(3)]
        before = [z_below(part[n - 1]) for part in parts]
        for i, trio in enumerate(coarsen(*parts, *before)):
            for c in range(3):
                dst[3 * j + c, :, :, i] = trio[c]
        return carry

    lax.fori_loop(0, 9, pass_z, 0, unroll=unroll)


def sweep(level, field, n, store, skip_faces):
    def body(step, carry):
        x, y = step // n, step % n
        sums = [[None] * n for _ in range(3)]
        for o0 in range(3):
            for o1 in range(3):
                columns = [[field[c, x + o0, y + o1, z] for z in range(n + 2)] for c in range(3)]
                for o2 in range(3):
                    if skip_faces and (o0 != 1) + (o1 != 1) + (o2 != 1) == 1:
                        continue
                    for z in range(n):
                        coef = level[9 * o0 + 3 * o1 + o2, x, y, z]
                        for c in range(3):
                            term = coef * columns[c][z + o2]
                            sums[c][z] = term if sums[c][z] is None else sums[c][z] + term
        for c in range(3):
            for z in range(n):
                store(c, x, y, z, sums[c][z])
        return carry

    lax.fori_loop(0, n * n, body, 0, unroll=True)


def relax_into(level, weight, rhs, src, dst, n, skip_faces=False):
    def store(c, x, y, z, value):
        dst[c, 1 + x, 1 + y, 1 + z] = src[c, 1 + x, 1 + y, 1 + z] + weight[x, y, z] * (rhs[c, x, y, z] - value)

    sweep(level, src, n, store, skip_faces)


def residual_down(level, rhs, src, res, coarse_rhs, n, skip_faces=False):
    half = n // 2

    def store(c, x, y, z, value):
        res[c, 1 + x, 1 + y, 1 + z] = rhs[c, x, y, z] - value

    sweep(level, src, n, store, skip_faces)

    def body(c, carry):
        fill_low(res.at[c], n)
        for i in range(half):
            part = 0.5 * (res[c, 2 * i] + res[c, 2 * i + 2]) + res[c, 2 * i + 1]
            for j in range(half):
                line = 0.5 * (part[2 * j] + part[2 * j + 2]) + part[2 * j + 1]
                for k in range(half):
                    coarse_rhs[c, i, j, k] = 0.5 * (line[2 * k] + line[2 * k + 2]) + line[2 * k + 1]
        return carry

    lax.fori_loop(0, 3, body, 0, unroll=n < 4)


def add_prolonged(coarse, fine, inside, half):
    def between(values):
        out = []
        for i in range(half):
            out += [values[i], 0.5 * (values[i] + values[i + 1])]
        return out

    def body(c, carry):
        planes = between([coarse[c, 1 + i, 1:, 1:] for i in range(half + 1)])
        for x, plane in enumerate(planes):
            for y, line in enumerate(between([plane[j] for j in range(half + 1)])):
                for z, value in enumerate(between([line[k] for k in range(half + 1)])):
                    fine[c, 1 + x, 1 + y, 1 + z] += jnp.where(inside, value, 0.0)
        return carry

    lax.fori_loop(0, 3, body, 0, unroll=half < 2)


def fill_all(ref, n):
    def body(c, carry):
        fill_both(ref.at[c], n)
        return carry

    lax.fori_loop(0, 3, body, 0, unroll=n < 4)


def cycle_kernel(
    idx_ref, prev_ref, own_ref, next_ref, out_own, out_one, out_two, out_three,
    fields, cells, level_a, weight_a, mid_a, mid_b, level_b, weight_b, mid_c, mid_d, level_c, weight_c,
    va, va2, vb, vb2, vc, vc2, res_a, res_b, rhs_b, rhs_c, out_ref,
):
    gx_prev, gx_own, gx_next = idx_ref[0], idx_ref[1], idx_ref[2]
    slab = (lane_ids(TILE) // 8) % 4
    inside = (slab == 1) | ((slab == 0) & (idx_ref[3] == 1)) | ((slab == 2) & (idx_ref[4] == 1))

    def arrange(step, carry):
        f = step
        for yp in range(4):
            by_source = []
            for source in range(4):
                tiles = [
                    ref[lax.bitwise_xor(gx, source), f, pl.ds(yp, ROWS, stride=4), :]
                    for ref, gx in ((prev_ref, gx_prev), (own_ref, gx_own), (next_ref, gx_next))
                ]
                by_source.append(swap_groups(tiles + [jnp.zeros(TILE, jnp.float32)], 8))
            for zp in range(4):
                moved = swap_groups([by_source[source][zp] for source in range(4)], 32)
                for xp in range(4):
                    fields[f, xp, yp, zp] = moved[xp]
        return carry

    lax.fori_loop(0, 8, arrange, 0)

    for x in range(4):
        cells[1 + x, 1:, 1:] = fields[0, x] * ELEMENT_TERMS[3]
    fill_low(cells, 4)

    def build(step, carry):
        x, y = step // 4, step % 4
        near = [[[cells[x + 1 - s0, y + 1 - s1, z] for z in range(5)] for s1 in (0, 1)] for s0 in (0, 1)]
        for z in range(4):
            for slot, offset in enumerate(offset_list()):
                nonzero = sum(1 for part in offset if part != 0)
                if nonzero == 1:
                    level_a[slot, x, y, z] = jnp.zeros(TILE, jnp.float32)
                    continue
                total = None
                for s in corner_list():
                    if all(0 <= s[d] + offset[d] <= 1 for d in range(3)):
                        term = near[s[0]][s[1]][z + 1 - s[2]]
                        total = term if total is None else total + term
                if nonzero == 0:
                    total = (ELEMENT_TERMS[0] / ELEMENT_TERMS[3]) * total + fields[1, x, y, z]
                    weight_a[x, y, z] = jnp.where(inside, OMEGA / jnp.where(inside, total, 1.0), 0.0)
                level_a[slot, x, y, z] = total
        return carry

    lax.fori_loop(0, 16, build, 0)

    triple_product(level_a, mid_a, mid_b, level_b, 4)
    weight_b[...] = jnp.where(inside, OMEGA / jnp.where(inside, level_b[13], 1.0), 0.0)
    triple_product(level_b, mid_c, mid_d, level_c, 2)
    weight_c[...] = jnp.where(inside, OMEGA / jnp.where(inside, level_c[13], 1.0), 0.0)

    position, force = fields.at[2:5], fields.at[5:8]

    def load(c, carry):
        for x in range(4):
            va[c, 1 + x, 1:5, 1:5] = position[c, x]
        return carry

    lax.fori_loop(0, 3, load, 0)
    fill_all(va, 4)
    relax_into(level_a, weight_a, force, va, va2, 4, True)
    fill_all(va2, 4)
    relax_into(level_a, weight_a, force, va2, va, 4, True)
    fill_all(va, 4)
    residual_down(level_a, force, va, res_a, rhs_b, 4, True)

    for c in range(3):
        for x in range(2):
            vb[c, 1 + x, 1:3, 1:3] = weight_b[x] * rhs_b[c, x]
    fill_all(vb, 2)
    relax_into(level_b, weight_b, rhs_b, vb, vb2, 2)
    fill_all(vb2, 2)
    residual_down(level_b, rhs_b, vb2, res_b, rhs_c, 2)

    for c in range(3):
        vc[c, 1, 1, 1] = weight_c[0, 0, 0] * rhs_c[c, 0, 0, 0]
    fill_all(vc, 1)
    relax_into(level_c, weight_c, rhs_c, vc, vc2, 1)
    fill_all(vc2, 1)
    relax_into(level_c, weight_c, rhs_c, vc2, vc, 1)
    fill_all(vc, 1)
    relax_into(level_c, weight_c, rhs_c, vc, vc2, 1)
    fill_all(vc2, 1)

    add_prolonged(vc2, vb2, inside, 1)
    fill_all(vb2, 2)
    relax_into(level_b, weight_b, rhs_b, vb2, vb, 2)
    fill_all(vb, 2)
    relax_into(level_b, weight_b, rhs_b, vb, vb2, 2)
    fill_all(vb2, 2)

    add_prolonged(vb2, va, inside, 2)
    fill_all(va, 4)
    relax_into(level_a, weight_a, force, va, va2, 4, True)
    fill_all(va2, 4)
    relax_into(level_a, weight_a, force, va2, va, 4, True)

    def own_slab(tiles):
        total = None
        for group, tile in enumerate(tiles):
            moved = lane_roll(tile, 8 * group - 8)
            total = moved if total is None else jnp.where(slab == group, moved, total)
        return total

    for c in range(3):
        for yp in range(4):
            lines = [own_slab([va[c, 1 + xp, 1 + yp, 1 + zp] for zp in range(4)]) for xp in range(4)]
            for dest, tile in enumerate(swap_groups(lines, 32)):
                out_ref[lax.bitwise_xor(gx_own, dest), pl.ds(32 * c + yp, ROWS, stride=4), :] = tile
    for g in range(7):
        for yp in range(2):
            lines = [
                own_slab([level_b[min(4 * g + o, 26), xp, yp, zp] for xp in range(2) for zp in range(2)])
                for o in range(4)
            ]
            for dest, tile in enumerate(swap_groups(lines, 32)):
                out_ref[lax.bitwise_xor(gx_own, dest), pl.ds(96 + 16 * g + yp, ROWS, stride=2), :] = tile

    side = idx_ref[5]
    for j, ref in enumerate((out_own, out_one, out_two, out_three)):
        for c in range(3):
            ref[16 * c:16 * c + 16] = out_ref[j, pl.ds(pl.multiple_of(32 * c + 16 * side, 16), 16), :]
        for g in range(7):
            ref[48 + 8 * g:56 + 8 * g] = out_ref[j, pl.ds(pl.multiple_of(96 + 16 * g + 8 * side, 8), 8), :]


def slab_place(gx, gz):
    order = jnp.where(gx < 2, gx, 5 - gx)
    return jnp.where(gz % 2 == 0, order, 3 - order)


def slab_owner(place, gz):
    order = place if gz % 2 == 0 else 3 - place
    return SNAKE[order]


def vmem_specs(count):
    return [pl.BlockSpec(memory_space=pltpu.VMEM)] * count


def shards_by_slab(cell_weight, weight_grad, material, modulus, node_mass, pinned, positions, forces):
    smem = pl.BlockSpec(memory_space=pltpu.SMEM)
    gx, gy, gz = lax.axis_index("gx"), lax.axis_index("gy"), lax.axis_index("gz")
    f32 = jnp.float32
    place = slab_place(gx, gz)
    index = 4 * gz + place

    def owner_of(place, z):
        order = jnp.where(z % 2 == 0, place, 3 - place)
        return jnp.where(order < 2, order, 5 - order)

    partner = jnp.stack([gx ^ owner_of(t, gz) for t in range(4)]).astype(jnp.int32)
    packed = pl.pallas_call(
        pack_kernel,
        out_shape=jax.ShapeDtypeStruct((4, 8, 16, LANES), f32),
        in_specs=[smem, smem] + vmem_specs(7),
        out_specs=vmem_specs(1)[0],
        name="pack",
    )(partner, modulus, cell_weight, weight_grad, material, node_mass, pinned, positions, forces)

    mine = [packed[0]]
    for j in range(1, 4):
        mine.append(lax.ppermute(packed[j], "gx", [(i, i ^ j) for i in range(4)]))
    mine = jnp.stack(mine)

    def swap_in_chain(first):
        pairs = []
        for core in range(2):
            chain = [(slab_owner(at, z) * 2 + core) * 4 + z for z in range(4) for at in range(4)]
            for at in range(first, 15, 2):
                pairs += [(chain[at], chain[at + 1]), (chain[at + 1], chain[at])]
            if first:
                pairs += [(chain[end], chain[end] ^ 4) for end in (0, 15)]
        return lax.ppermute(mine, ("gx", "gy", "gz"), pairs)

    even, odd = swap_in_chain(0), swap_in_chain(1)

    def both_halves(half, present):
        other = lax.ppermute(half, "gy", [(0, 1), (1, 0)])
        rows = jnp.concatenate([jnp.where(gy == 0, half, other), jnp.where(gy == 0, other, half)], axis=2)
        return jnp.where(present, rows, 0.0)

    odd_place = index % 2 == 1
    own = both_halves(mine, True)
    even = both_halves(even, True)
    odd = both_halves(odd, (index > 0) & (index < 15))
    before = jnp.where(odd_place, even, odd)
    after = jnp.where(odd_place, odd, even)

    gx_before = owner_of((index - 1) % 4, (index - 1) // 4)
    gx_after = owner_of((index + 1) % 4, (index + 1) // 4)
    scalars = jnp.stack(
        [gx_before, gx, gx_after, (index > 0).astype(jnp.int32), (index < 15).astype(jnp.int32), gy]
    ).astype(jnp.int32)

    def buf(*dims):
        return pltpu.VMEM(tuple(dims) + TILE, f32)

    message = pl.pallas_call(
        cycle_kernel,
        out_shape=[jax.ShapeDtypeStruct((104, LANES), f32)] * 4,
        in_specs=[smem] + vmem_specs(3),
        out_specs=vmem_specs(4),
        scratch_shapes=[
            buf(8, 4, 4, 4), buf(5, 5, 5), buf(27, 4, 4, 4), buf(4, 4, 4),
            buf(27, 2, 4, 4), buf(27, 2, 2, 4), buf(27, 2, 2, 2), buf(2, 2, 2),
            buf(27, 1, 2, 2), buf(27, 1, 1, 2), buf(27, 1, 1, 1), buf(1, 1, 1),
            buf(3, 6, 6, 6), buf(3, 6, 6, 6), buf(3, 4, 4, 4), buf(3, 4, 4, 4), buf(3, 3, 3, 3), buf(3, 3, 3, 3),
            buf(3, 5, 5, 5), buf(3, 3, 3, 3), buf(3, 2, 2, 2), buf(3, 1, 1, 1),
            pltpu.VMEM((4, 208, LANES), f32),
        ],
        compiler_params=pltpu.CompilerParams(vmem_limit_bytes=48 * 1024 * 1024),
        name="cycle",
    )(scalars, before, own, after)

    back = [message[0]]
    for j in range(1, 4):
        back.append(lax.ppermute(message[j], "gx", [(i, i ^ j) for i in range(4)]))
    return pl.pallas_call(
        unpack_kernel,
        out_shape=[
            jax.ShapeDtypeStruct(positions.shape, f32),
            jax.ShapeDtypeStruct((27, 2, 8, 64), f32),
        ],
        in_specs=[smem] + vmem_specs(4),
        out_specs=vmem_specs(2),
        scratch_shapes=[pltpu.VMEM((4, 104, LANES), f32)],
        name="unpack",
    )(partner, *back)


def solution(mesh):
    placed = (
        P("gx", "gy", "gz"),
        P("gx", "gy", "gz"),
        P("gx", "gy", "gz"),
        P(),
        P("gx", "gy", "gz"),
        P("gx", "gy", "gz"),
        P(None, "gx", "gy", "gz"),
        P(None, "gx", "gy", "gz"),
    )
    sizes = tuple(mesh.shape[axis] for axis in ("gx", "gy", "gz"))

    def choose(cell_weight, *rest):
        fits = sizes == (4, 2, 4) and cell_weight.shape == (4, 16, 128)
        return (shards_by_slab if fits else shards)(cell_weight, *rest)

    return jax.shard_map(
        choose,
        mesh=mesh,
        in_specs=placed,
        out_specs=(P(None, "gx", "gy", "gz"), P(None, "gx", "gy", "gz")),
        check_vma=False,
    )
```

```python
import jax
import jax.numpy as jnp
import numpy as np
from jax import lax
from jax.experimental import pallas as pl
from jax.experimental.pallas import tpu as pltpu
from jax.sharding import PartitionSpec as P

OMEGA = 0.6
LEARN_RATE = 0.5
PIN_WEIGHT = 4.0
ELEMENT_TERMS = (1.0 / 3.0, 0.0, -1.0 / 12.0, -1.0 / 12.0)


def shifted(x, axis, by):
    peers = lax.axis_size(axis)
    pairs = [(i, i + by) for i in range(peers) if 0 <= i + by < peers]
    return lax.ppermute(x, axis, pairs)


def extended(block, sides, width):
    for axis, dim in sides:
        count = lax.axis_size(axis)
        forward = [(i, i + 1) for i in range(count - 1)]
        backward = [(target, source) for source, target in forward]
        low = lax.ppermute(
            lax.slice_in_dim(block, block.shape[dim] - width, None, axis=dim), axis, forward
        )
        high = lax.ppermute(lax.slice_in_dim(block, 0, width, axis=dim), axis, backward)
        block = jnp.concatenate([low, block, high], axis=dim)
    return block


def offset_list():
    return [
        (shift_x, shift_y, shift_z)
        for shift_x in (-1, 0, 1)
        for shift_y in (-1, 0, 1)
        for shift_z in (-1, 0, 1)
    ]


def corner_list():
    return [(bit_x, bit_y, bit_z) for bit_x in (0, 1) for bit_y in (0, 1) for bit_z in (0, 1)]


def hat_weight(distance):
    if distance == 0:
        return 1.0
    if abs(distance) == 1:
        return 0.5
    return 0.0


def galerkin_tables():
    offsets = offset_list()
    tables = np.zeros((27, 27, 27), np.float32)
    for slot_a, outer in enumerate(offsets):
        for slot_c, coarse in enumerate(offsets):
            for slot_f, inner in enumerate(offsets):
                factor = 1.0
                for axis_pos in range(3):
                    factor *= hat_weight(outer[axis_pos]) * hat_weight(
                        2 * coarse[axis_pos] - outer[axis_pos] - inner[axis_pos]
                    )
                tables[slot_a, slot_c, slot_f] = factor
    return tables


def stiffness_of(cell_weight, weight_grad, material, modulus):
    lookup = jnp.zeros(cell_weight.shape, jnp.float32)
    for index in range(modulus.shape[0]):
        lookup = lookup + jnp.where(material == index, modulus[index], 0.0)
    return cell_weight * jnp.exp(-LEARN_RATE * weight_grad) * lookup


def assemble(cell_rim, node_mass, pinned_weight):
    node_shape = node_mass.shape
    rows_out = []
    for offset in offset_list():
        total = jnp.zeros(node_shape, jnp.float32)
        for corner in corner_list():
            if all((0 <= corner[axis_pos] + offset[axis_pos] <= 1 for axis_pos in range(3))):
                total = (
                    total
                    + cell_rim[
                        1 - corner[0] : 1 - corner[0] + node_shape[0],
                        1 - corner[1] : 1 - corner[1] + node_shape[1],
                        1 - corner[2] : 1 - corner[2] + node_shape[2],
                    ]
                )
        nonzero = sum((1 for axis_pos in range(3) if offset[axis_pos] != 0))
        entry = ELEMENT_TERMS[nonzero] * total
        if nonzero == 0:
            entry = entry + node_mass + PIN_WEIGHT * pinned_weight
        rows_out.append(entry)
    return jnp.stack(rows_out)


def galerkin(op_rim, coarse_shape):
    tables = jnp.asarray(galerkin_tables())
    result = None
    for slot_a, outer in enumerate(offset_list()):
        piece = op_rim[
            :,
            outer[0] + 1 : outer[0] + 1 + 2 * coarse_shape[0] : 2,
            outer[1] + 1 : outer[1] + 1 + 2 * coarse_shape[1] : 2,
            outer[2] + 1 : outer[2] + 1 + 2 * coarse_shape[2] : 2,
        ]
        term = jnp.einsum("pk,kxyz->pxyz", tables[slot_a], piece, precision=lax.Precision.HIGHEST)
        result = term if result is None else result + term
    return result


def stencil_apply(stencil, padded):
    node_shape = stencil.shape[1:]
    result = None
    for slot, offset in enumerate(offset_list()):
        window = padded[
            :,
            1 + offset[0] : 1 + offset[0] + node_shape[0],
            1 + offset[1] : 1 + offset[1] + node_shape[1],
            1 + offset[2] : 1 + offset[2] + node_shape[2],
        ]
        term = stencil[slot][None] * window
        result = term if result is None else result + term
    return result


def relax(stencil, field, rhs_field, padded):
    return field + OMEGA * (rhs_field - stencil_apply(stencil, padded)) / stencil[13][None]


def restrict_axis(field, axis_pos, coarse_len):
    below = lax.slice_in_dim(field, 0, 2 * coarse_len - 1, 2, axis_pos)
    centre = lax.slice_in_dim(field, 1, 2 * coarse_len, 2, axis_pos)
    above = lax.slice_in_dim(field, 2, 2 * coarse_len + 1, 2, axis_pos)
    return 0.5 * below + centre + 0.5 * above


def restrict(rim_field, coarse_shape):
    field = rim_field
    for axis_pos in (1, 2, 3):
        field = restrict_axis(field, axis_pos, coarse_shape[axis_pos - 1])
    return field


def prolong_axis(field, axis_pos, coarse_len):
    lower = lax.slice_in_dim(field, 0, coarse_len, 1, axis_pos)
    upper = lax.slice_in_dim(field, 1, coarse_len + 1, 1, axis_pos)
    middle = 0.5 * (lower + upper)
    paired = jnp.stack([lower, middle], axis=axis_pos + 1)
    new_shape = list(lower.shape)
    new_shape[axis_pos] = 2 * coarse_len
    return paired.reshape(new_shape)


def prolong(rim_field, coarse_shape):
    field = rim_field
    for axis_pos in (1, 2, 3):
        field = prolong_axis(field, axis_pos, coarse_shape[axis_pos - 1])
    return field


def boundary_layer(field, axis_pos, forward):
    extent = field.shape[axis_pos]
    if forward:
        return lax.slice_in_dim(field, extent - 1, extent, 1, axis_pos)
    return lax.slice_in_dim(field, 0, 1, 1, axis_pos)


def attach(field, layer_in, axis_pos, forward):
    if forward:
        return jnp.concatenate([layer_in, field], axis=axis_pos)
    return jnp.concatenate([field, layer_in], axis=axis_pos)


def extend(field, leading, forward):
    step = 1 if forward else -1
    got_x = shifted(boundary_layer(field, leading, forward), "gx", step)
    field = attach(field, got_x, leading, forward)
    got_y = shifted(boundary_layer(field, leading + 1, forward), "gy", step)
    field = attach(field, got_y, leading + 1, forward)
    got_z = shifted(boundary_layer(field, leading + 2, forward), "gz", step)
    return attach(field, got_z, leading + 2, forward)


def faces(field):
    return extended(field, (("gx", 1), ("gy", 2), ("gz", 3)), 1)


def shards(cell_weight, weight_grad, material, modulus, node_mass, pinned, positions, forces):
    stiffness = stiffness_of(cell_weight, weight_grad, material, modulus)
    fine_shape = node_mass.shape
    mid_shape = tuple((extent // 2 for extent in fine_shape))
    low_shape = tuple((extent // 4 for extent in fine_shape))
    pinned_weight = pinned.astype(jnp.float32)
    level_zero = assemble(extend(stiffness, 0, True), node_mass, pinned_weight)
    zero_rim = extend(level_zero, 1, True)
    level_one = galerkin(zero_rim, mid_shape)
    level_two = galerkin(extend(level_one, 1, True), low_shape)
    iterate = positions
    for sweep in range(2):
        iterate = relax(level_zero, iterate, forces, faces(iterate))
    residual_zero = forces - stencil_apply(level_zero, faces(iterate))
    rhs_one = restrict(extend(residual_zero, 1, True), mid_shape)
    corr_one = OMEGA * rhs_one / level_one[13][None]
    corr_one = relax(level_one, corr_one, rhs_one, faces(corr_one))
    residual_one = rhs_one - stencil_apply(level_one, faces(corr_one))
    rhs_two = restrict(extend(residual_one, 1, True), low_shape)
    corr_two = OMEGA * rhs_two / level_two[13][None]
    for sweep in range(3):
        corr_two = relax(level_two, corr_two, rhs_two, faces(corr_two))
    corr_one = corr_one + prolong(extend(corr_two, 1, False), low_shape)
    for sweep in range(2):
        corr_one = relax(level_one, corr_one, rhs_one, faces(corr_one))
    iterate = iterate + prolong(extend(corr_one, 1, False), mid_shape)
    for sweep in range(2):
        iterate = relax(level_zero, iterate, forces, faces(iterate))
    return (iterate, level_one)


LANES = 128
ROWS = 8
TILE = (ROWS, LANES)
SNAKE = (0, 1, 3, 2)


def lane_roll(x, by):
    return pltpu.roll(x, by % LANES, x.ndim - 1)


def row_roll(x, by):
    return pltpu.roll(x, by % ROWS, x.ndim - 2)


def lane_ids(shape):
    return lax.broadcasted_iota(jnp.int32, shape, len(shape) - 1)


def row_ids(shape):
    return lax.broadcasted_iota(jnp.int32, shape, len(shape) - 2)


def x_below(x):
    return jnp.where(lane_ids(x.shape) >= 32, lane_roll(x, 32), 0.0)


def x_above(x):
    return jnp.where(lane_ids(x.shape) < 96, lane_roll(x, -32), 0.0)


def y_below(x):
    return jnp.where(row_ids(x.shape) >= 1, row_roll(x, 1), 0.0)


def y_above(x):
    return jnp.where(row_ids(x.shape) < ROWS - 1, row_roll(x, -1), 0.0)


def z_below(x):
    return lane_roll(x, 1)


def z_above(x):
    return lane_roll(x, -1)


def swap_groups(parts, unit):
    group = lane_ids(parts[0].shape) // unit
    parts = list(parts)
    for bit in (1, 2):
        low = (group & bit) == 0
        for i in range(4):
            if i & bit == 0:
                a, b = parts[i], parts[i + bit]
                parts[i] = jnp.where(low, a, lane_roll(b, unit * bit))
                parts[i + bit] = jnp.where(low, lane_roll(a, -unit * bit), b)
    return parts


def pick_lanes(x, source):
    return jnp.take_along_axis(x, jnp.broadcast_to(source, x.shape), axis=-1)


def pack_kernel(place_ref, mod_ref, cw_ref, wg_ref, mat_ref, mass_ref, pin_ref, pos_ref, force_ref, out_ref):
    material = mat_ref[...]
    lookup = jnp.zeros(material.shape, jnp.float32)
    for index in range(mod_ref.shape[0]):
        lookup = jnp.where(material == index, mod_ref[index], lookup)
    stiff = cw_ref[...] * jnp.exp(-LEARN_RATE * wg_ref[...]) * lookup
    mass = mass_ref[...] + PIN_WEIGHT * pin_ref[...].astype(jnp.float32)
    fields = [stiff, mass] + [pos_ref[c] for c in range(3)] + [force_ref[c] for c in range(3)]
    lane = lane_ids((16, LANES))
    source = (lane // 32) * 32 + (lane % 8) * 4 + (lane % 32) // 8
    for f, field in enumerate(fields):
        moved = swap_groups([pick_lanes(field[x], source) for x in range(4)], 32)
        for t in range(4):
            out_ref[place_ref[t], f] = moved[t]


def unpack_kernel(place_ref, own_ref, one_ref, two_ref, three_ref, iterate_ref, level_ref, hold):
    for j, ref in enumerate((own_ref, one_ref, two_ref, three_ref)):
        hold[j] = ref[...]
    blocks = [place_ref[t] for t in range(4)]
    lane = lane_ids((16, LANES))
    source = (lane // 32) * 32 + (lane % 4) * 8 + (lane % 32) // 4
    for c in range(3):
        moved = swap_groups([hold[j, 16 * c:16 * c + 16] for j in blocks], 32)
        for x in range(4):
            iterate_ref[c, x] = pick_lanes(moved[x], source)
    lane = lane_ids(TILE)
    source = ((lane % 64) // 16) * 32 + (lane % 2) * 8 + (lane % 16) // 2
    for g in range(7):
        moved = swap_groups([hold[j, 48 + 8 * g:56 + 8 * g] for j in blocks], 32)
        for o in range(4):
            if 4 * g + o < 27:
                for x in range(2):
                    level_ref[4 * g + o, x] = pick_lanes(moved[o], source + 16 * x)[:, :64]


def fill_low(ref, n):
    ref[0, 1:, 1:] = x_below(ref[n, 1:, 1:])
    ref[:, 0, 1:] = y_below(ref[:, n, 1:])
    ref[:, :, 0] = z_below(ref[:, :, n])


def fill_both(ref, n):
    mid = slice(1, n + 1)
    ref[0, mid, mid] = x_below(ref[n, mid, mid])
    ref[n + 1, mid, mid] = x_above(ref[1, mid, mid])
    ref[:, 0, mid] = y_below(ref[:, n, mid])
    ref[:, n + 1, mid] = y_above(ref[:, 1, mid])
    ref[:, :, 0] = z_below(ref[:, :, n])
    ref[:, :, n + 1] = z_above(ref[:, :, 1])


def add(*terms):
    total = None
    for term in terms:
        if term is not None:
            total = term if total is None else total + term
    return total


def coarsen(low, mid, high, before, count):
    def scaled(x, factor):
        return None if x is None else factor * x

    leads = []
    for i in range(count):
        half = scaled(mid(2 * i + 1), 0.5)
        leads.append((add(low(2 * i + 1), half), add(high(2 * i + 1), half)))
    wrapped = tuple(None if x is None else before(x) for x in leads[-1])
    out = []
    for i in range(count):
        to_low, to_high = leads[i]
        from_low, from_high = leads[i - 1] if i else wrapped
        here = add(scaled(mid(2 * i), 2.0), low(2 * i), high(2 * i), to_low, from_high)
        out.append((add(low(2 * i), from_low), here, add(high(2 * i), to_high)))
    return out


def triple_product(src, mid_a, mid_b, dst, n, faces):
    half = n // 2
    looped = n == 4

    def pass_x(j, y, skip):
        def part(f):
            return lambda i: None if f in skip else src[9 * f + j, i, y]

        for i, trio in enumerate(coarsen(part(0), part(1), part(2), x_below, half)):
            for c in range(3):
                mid_a[9 * c + j, i, y] = trio[c]

    def all_x(y, carry):
        for j in range(9):
            crossed = (j // 3 != 1) + (j % 3 != 1)
            skip = () if not faces or crossed == 2 else ((1,) if crossed == 1 else (0, 2))
            pass_x(j, y, skip)
        return carry

    lax.fori_loop(0, n, all_x, 0, unroll=not looped)

    def pass_y(j, carry):
        base = 9 * (j // 3) + j % 3

        def part(f):
            return lambda i: mid_a[base + 3 * f, :, i]

        for i, trio in enumerate(coarsen(part(0), part(1), part(2), y_below, half)):
            for c in range(3):
                mid_b[base + 3 * c, :, i] = trio[c]
        return carry

    lax.fori_loop(0, 9, pass_y, 0, unroll=not looped)

    def pass_z(j, carry):
        def part(f):
            return lambda i: mid_b[3 * j + f, :, :, i]

        for i, trio in enumerate(coarsen(part(0), part(1), part(2), z_below, half)):
            for c in range(3):
                dst[3 * j + c, :, :, i] = 0.125 * trio[c]
        return carry

    lax.fori_loop(0, 9, pass_z, 0, unroll=not looped)


def sweep(level, field, n, store):
    def body(step, carry):
        x, y = step // n, step % n
        sums = [[None] * n for _ in range(3)]
        for o0 in range(3):
            for o1 in range(3):
                columns = [[field[c, x + o0, y + o1, z] for z in range(n + 2)] for c in range(3)]
                for o2 in range(3):
                    for z in range(n):
                        coef = level[9 * o0 + 3 * o1 + o2, x, y, z]
                        for c in range(3):
                            term = coef * columns[c][z + o2]
                            sums[c][z] = term if sums[c][z] is None else sums[c][z] + term
        for c in range(3):
            for z in range(n):
                store(c, x, y, z, sums[c][z])
        return carry

    lax.fori_loop(0, n * n, body, 0, unroll=True)


def cell_sweep(parts, field, store):
    cells, edge_x, edge_y, edge_z, diag, sums = parts

    def gather(c, carry):
        for x in range(4):
            pair = [[field[c, 1 + x, 1 + y, 1 + z] + field[c, 2 + x, 1 + y, 1 + z] for z in range(5)] for y in range(5)]
            for y in range(4):
                quad = [pair[y][z] + pair[y + 1][z] for z in range(5)]
                for z in range(4):
                    sums[c, 1 + x, 1 + y, 1 + z] = cells[1 + x, 1 + y, 1 + z] * (quad[z] + quad[z + 1])
        fill_low(sums.at[c], 4)
        return carry

    lax.fori_loop(0, 3, gather, 0, unroll=True)

    for x in range(4):
        for y in range(4):
            for c in range(3):
                near = [
                    (sums[c, x, y, z] + sums[c, x, y + 1, z]) + (sums[c, x + 1, y, z] + sums[c, x + 1, y + 1, z])
                    for z in range(5)
                ]
                line = [field[c, 1 + x, 1 + y, z] for z in range(6)]
                for z in range(4):
                    value = diag[x, y, z] * line[1 + z] + (near[z] + near[z + 1])
                    value = value - edge_x[x, y, z] * field[c, x, 1 + y, 1 + z]
                    value = value - edge_x[x + 1, y, z] * field[c, x + 2, 1 + y, 1 + z]
                    value = value - edge_y[x, y, z] * field[c, 1 + x, y, 1 + z]
                    value = value - edge_y[x, y + 1, z] * field[c, 1 + x, y + 2, 1 + z]
                    value = value - edge_z[x, y, z] * line[z]
                    value = value - edge_z[x, y, z + 1] * line[z + 2]
                    store(c, x, y, z, value)


def apply_level(level, field, n, store):
    if n == 4:
        cell_sweep(level, field, store)
    else:
        sweep(level, field, n, store)


def relax_into(level, weight, rhs, src, dst, n):
    def store(c, x, y, z, value):
        dst[c, 1 + x, 1 + y, 1 + z] = src[c, 1 + x, 1 + y, 1 + z] + weight[x, y, z] * (rhs[c, x, y, z] - value)

    apply_level(level, src, n, store)


def residual_down(level, rhs, src, res, coarse_rhs, n):
    half = n // 2

    def store(c, x, y, z, value):
        res[c, 1 + x, 1 + y, 1 + z] = rhs[c, x, y, z] - value

    apply_level(level, src, n, store)

    def body(c, carry):
        fill_low(res.at[c], n)
        for i in range(half):
            part = 0.5 * (res[c, 2 * i] + res[c, 2 * i + 2]) + res[c, 2 * i + 1]
            for j in range(half):
                line = 0.5 * (part[2 * j] + part[2 * j + 2]) + part[2 * j + 1]
                for k in range(half):
                    coarse_rhs[c, i, j, k] = 0.5 * (line[2 * k] + line[2 * k + 2]) + line[2 * k + 1]
        return carry

    lax.fori_loop(0, 3, body, 0, unroll=n < 4)


def add_prolonged(coarse, fine, inside, half):
    def between(values):
        out = []
        for i in range(half):
            out += [values[i], 0.5 * (values[i] + values[i + 1])]
        return out

    def body(c, carry):
        planes = between([coarse[c, 1 + i, 1:, 1:] for i in range(half + 1)])
        for x, plane in enumerate(planes):
            for y, line in enumerate(between([plane[j] for j in range(half + 1)])):
                for z, value in enumerate(between([line[k] for k in range(half + 1)])):
                    fine[c, 1 + x, 1 + y, 1 + z] += jnp.where(inside, value, 0.0)
        return carry

    lax.fori_loop(0, 3, body, 0, unroll=half < 2)


def fill_all(ref, n):
    def body(c, carry):
        fill_both(ref.at[c], n)
        return carry

    lax.fori_loop(0, 3, body, 0, unroll=n < 4)


def cycle_kernel(
    idx_ref, prev_ref, own_ref, next_ref, out_own, out_one, out_two, out_three,
    fields, cells, level_a, weight_a, mid_a, mid_b, level_b, weight_b, mid_c, mid_d, level_c, weight_c,
    va, va2, vb, vb2, vc, vc2, res_a, res_b, rhs_b, rhs_c, out_ref,
    edge_x, edge_y, edge_z, diag, sums,
):
    gx_prev, gx_own, gx_next = idx_ref[0], idx_ref[1], idx_ref[2]
    slab = (lane_ids(TILE) // 8) % 4
    inside = (slab == 1) | ((slab == 0) & (idx_ref[3] == 1)) | ((slab == 2) & (idx_ref[4] == 1))

    def arrange(step, carry):
        f = step
        for yp in range(4):
            by_source = []
            for source in range(4):
                tiles = [
                    ref[lax.bitwise_xor(gx, source), f, pl.ds(yp, ROWS, stride=4), :]
                    for ref, gx in ((prev_ref, gx_prev), (own_ref, gx_own), (next_ref, gx_next))
                ]
                by_source.append(swap_groups(tiles + [jnp.zeros(TILE, jnp.float32)], 8))
            for zp in range(4):
                moved = swap_groups([by_source[source][zp] for source in range(4)], 32)
                for xp in range(4):
                    fields[f, xp, yp, zp] = moved[xp]
        return carry

    lax.fori_loop(0, 8, arrange, 0)

    for x in range(4):
        cells[1 + x, 1:, 1:] = fields[0, x] * ELEMENT_TERMS[3]
    fill_low(cells, 4)

    def build(step, carry):
        x, y = step // 4, step % 4
        near = [[[cells[x + 1 - s0, y + 1 - s1, z] for z in range(5)] for s1 in (0, 1)] for s0 in (0, 1)]
        for z in range(4):
            for slot, offset in enumerate(offset_list()):
                nonzero = sum(1 for part in offset if part != 0)
                if nonzero == 1:
                    continue
                total = None
                for s in corner_list():
                    if all(0 <= s[d] + offset[d] <= 1 for d in range(3)):
                        term = near[s[0]][s[1]][z + 1 - s[2]]
                        total = term if total is None else total + term
                if nonzero == 0:
                    mass = fields[1, x, y, z]
                    diag[x, y, z] = ((ELEMENT_TERMS[0] - ELEMENT_TERMS[3]) / ELEMENT_TERMS[3]) * total + mass
                    total = (ELEMENT_TERMS[0] / ELEMENT_TERMS[3]) * total + mass
                    weight_a[x, y, z] = jnp.where(inside, OMEGA / jnp.where(inside, total, 1.0), 0.0)
                level_a[slot, x, y, z] = total
        return carry

    lax.fori_loop(0, 16, build, 0)

    edge_z[...] = (cells[1:, 1:] + cells[:4, 1:]) + (cells[1:, :4] + cells[:4, :4])
    over_z = cells[:, :, 1:] + cells[:, :, :4]
    edge_x[...] = over_z[:, 1:] + over_z[:, :4]
    edge_y[...] = over_z[1:] + over_z[:4]
    fine = (cells, edge_x, edge_y, edge_z, diag, sums)

    triple_product(level_a, mid_a, mid_b, level_b, 4, True)
    weight_b[...] = jnp.where(inside, OMEGA / jnp.where(inside, level_b[13], 1.0), 0.0)
    triple_product(level_b, mid_c, mid_d, level_c, 2, False)
    weight_c[...] = jnp.where(inside, OMEGA / jnp.where(inside, level_c[13], 1.0), 0.0)

    position, force = fields.at[2:5], fields.at[5:8]

    def load(c, carry):
        for x in range(4):
            va[c, 1 + x, 1:5, 1:5] = position[c, x]
        return carry

    lax.fori_loop(0, 3, load, 0)
    fill_all(va, 4)
    relax_into(fine, weight_a, force, va, va2, 4)
    fill_all(va2, 4)
    relax_into(fine, weight_a, force, va2, va, 4)
    fill_all(va, 4)
    residual_down(fine, force, va, res_a, rhs_b, 4)

    for c in range(3):
        for x in range(2):
            vb[c, 1 + x, 1:3, 1:3] = weight_b[x] * rhs_b[c, x]
    fill_all(vb, 2)
    relax_into(level_b, weight_b, rhs_b, vb, vb2, 2)
    fill_all(vb2, 2)
    residual_down(level_b, rhs_b, vb2, res_b, rhs_c, 2)

    for c in range(3):
        vc[c, 1, 1, 1] = weight_c[0, 0, 0] * rhs_c[c, 0, 0, 0]
    fill_all(vc, 1)
    relax_into(level_c, weight_c, rhs_c, vc, vc2, 1)
    fill_all(vc2, 1)
    relax_into(level_c, weight_c, rhs_c, vc2, vc, 1)
    fill_all(vc, 1)
    relax_into(level_c, weight_c, rhs_c, vc, vc2, 1)
    fill_all(vc2, 1)

    add_prolonged(vc2, vb2, inside, 1)
    fill_all(vb2, 2)
    relax_into(level_b, weight_b, rhs_b, vb2, vb, 2)
    fill_all(vb, 2)
    relax_into(level_b, weight_b, rhs_b, vb, vb2, 2)
    fill_all(vb2, 2)

    add_prolonged(vb2, va, inside, 2)
    fill_all(va, 4)
    relax_into(fine, weight_a, force, va, va2, 4)
    fill_all(va2, 4)
    relax_into(fine, weight_a, force, va2, va, 4)

    def own_slab(tiles):
        total = None
        for group, tile in enumerate(tiles):
            moved = lane_roll(tile, 8 * group - 8)
            total = moved if total is None else jnp.where(slab == group, moved, total)
        return total

    def send_field(c, carry):
        for yp in range(4):
            lines = [own_slab([va[c, 1 + xp, 1 + yp, 1 + zp] for zp in range(4)]) for xp in range(4)]
            for dest, tile in enumerate(swap_groups(lines, 32)):
                out_ref[lax.bitwise_xor(gx_own, dest), pl.ds(32 * c + yp, ROWS, stride=4), :] = tile
        return carry

    lax.fori_loop(0, 3, send_field, 0)

    for g in range(7):
        for yp in range(2):
            lines = [
                own_slab([level_b[min(4 * g + o, 26), xp, yp, zp] for xp in range(2) for zp in range(2)])
                for o in range(4)
            ]
            for dest, tile in enumerate(swap_groups(lines, 32)):
                out_ref[lax.bitwise_xor(gx_own, dest), pl.ds(96 + 16 * g + yp, ROWS, stride=2), :] = tile

    side = idx_ref[5]
    for j, ref in enumerate((out_own, out_one, out_two, out_three)):
        for c in range(3):
            ref[16 * c:16 * c + 16] = out_ref[j, pl.ds(pl.multiple_of(32 * c + 16 * side, 16), 16), :]
        for g in range(7):
            ref[48 + 8 * g:56 + 8 * g] = out_ref[j, pl.ds(pl.multiple_of(96 + 16 * g + 8 * side, 8), 8), :]


def slab_place(gx, gz):
    order = jnp.where(gx < 2, gx, 5 - gx)
    return jnp.where(gz % 2 == 0, order, 3 - order)


def slab_owner(place, gz):
    order = place if gz % 2 == 0 else 3 - place
    return SNAKE[order]


def vmem_specs(count):
    return [pl.BlockSpec(memory_space=pltpu.VMEM)] * count


def shards_by_slab(cell_weight, weight_grad, material, modulus, node_mass, pinned, positions, forces):
    smem = pl.BlockSpec(memory_space=pltpu.SMEM)
    gx, gy, gz = lax.axis_index("gx"), lax.axis_index("gy"), lax.axis_index("gz")
    f32 = jnp.float32
    place = slab_place(gx, gz)
    index = 4 * gz + place

    def owner_of(place, z):
        order = jnp.where(z % 2 == 0, place, 3 - place)
        return jnp.where(order < 2, order, 5 - order)

    partner = jnp.stack([gx ^ owner_of(t, gz) for t in range(4)]).astype(jnp.int32)
    packed = pl.pallas_call(
        pack_kernel,
        out_shape=jax.ShapeDtypeStruct((4, 8, 16, LANES), f32),
        in_specs=[smem, smem] + vmem_specs(7),
        out_specs=vmem_specs(1)[0],
        name="pack",
    )(partner, modulus, cell_weight, weight_grad, material, node_mass, pinned, positions, forces)

    mine = [packed[0]]
    for j in range(1, 4):
        mine.append(lax.ppermute(packed[j], "gx", [(i, i ^ j) for i in range(4)]))
    mine = jnp.stack(mine)

    def swap_in_chain(first):
        pairs = []
        for core in range(2):
            chain = [(slab_owner(at, z) * 2 + core) * 4 + z for z in range(4) for at in range(4)]
            for at in range(first, 15, 2):
                pairs += [(chain[at], chain[at + 1]), (chain[at + 1], chain[at])]
            if first:
                pairs += [(chain[end], chain[end] ^ 4) for end in (0, 15)]
        return lax.ppermute(mine, ("gx", "gy", "gz"), pairs)

    even, odd = swap_in_chain(0), swap_in_chain(1)

    def both_halves(half, present):
        other = lax.ppermute(half, "gy", [(0, 1), (1, 0)])
        rows = jnp.concatenate([jnp.where(gy == 0, half, other), jnp.where(gy == 0, other, half)], axis=2)
        return jnp.where(present, rows, 0.0)

    odd_place = index % 2 == 1
    own = both_halves(mine, True)
    even = both_halves(even, True)
    odd = both_halves(odd, (index > 0) & (index < 15))
    before = jnp.where(odd_place, even, odd)
    after = jnp.where(odd_place, odd, even)

    gx_before = owner_of((index - 1) % 4, (index - 1) // 4)
    gx_after = owner_of((index + 1) % 4, (index + 1) // 4)
    scalars = jnp.stack(
        [gx_before, gx, gx_after, (index > 0).astype(jnp.int32), (index < 15).astype(jnp.int32), gy]
    ).astype(jnp.int32)

    def buf(*dims):
        return pltpu.VMEM(tuple(dims) + TILE, f32)

    message = pl.pallas_call(
        cycle_kernel,
        out_shape=[jax.ShapeDtypeStruct((104, LANES), f32)] * 4,
        in_specs=[smem] + vmem_specs(3),
        out_specs=vmem_specs(4),
        scratch_shapes=[
            buf(8, 4, 4, 4), buf(5, 5, 5), buf(27, 4, 4, 4), buf(4, 4, 4),
            buf(27, 2, 4, 4), buf(27, 2, 2, 4), buf(27, 2, 2, 2), buf(2, 2, 2),
            buf(27, 1, 2, 2), buf(27, 1, 1, 2), buf(27, 1, 1, 1), buf(1, 1, 1),
            buf(3, 6, 6, 6), buf(3, 6, 6, 6), buf(3, 4, 4, 4), buf(3, 4, 4, 4), buf(3, 3, 3, 3), buf(3, 3, 3, 3),
            buf(3, 5, 5, 5), buf(3, 3, 3, 3), buf(3, 2, 2, 2), buf(3, 1, 1, 1),
            pltpu.VMEM((4, 208, LANES), f32),
            buf(5, 4, 4), buf(4, 5, 4), buf(4, 4, 5), buf(4, 4, 4), buf(3, 5, 5, 5),
        ],
        compiler_params=pltpu.CompilerParams(vmem_limit_bytes=48 * 1024 * 1024),
        name="cycle",
    )(scalars, before, own, after)

    back = [message[0]]
    for j in range(1, 4):
        back.append(lax.ppermute(message[j], "gx", [(i, i ^ j) for i in range(4)]))
    return pl.pallas_call(
        unpack_kernel,
        out_shape=[
            jax.ShapeDtypeStruct(positions.shape, f32),
            jax.ShapeDtypeStruct((27, 2, 8, 64), f32),
        ],
        in_specs=[smem] + vmem_specs(4),
        out_specs=vmem_specs(2),
        scratch_shapes=[pltpu.VMEM((4, 104, LANES), f32)],
        name="unpack",
    )(partner, *back)


def solution(mesh):
    placed = (
        P("gx", "gy", "gz"),
        P("gx", "gy", "gz"),
        P("gx", "gy", "gz"),
        P(),
        P("gx", "gy", "gz"),
        P("gx", "gy", "gz"),
        P(None, "gx", "gy", "gz"),
        P(None, "gx", "gy", "gz"),
    )
    sizes = tuple(mesh.shape[axis] for axis in ("gx", "gy", "gz"))

    def choose(cell_weight, *rest):
        fits = sizes == (4, 2, 4) and cell_weight.shape == (4, 16, 128)
        return (shards_by_slab if fits else shards)(cell_weight, *rest)

    return jax.shard_map(
        choose,
        mesh=mesh,
        in_specs=placed,
        out_specs=(P(None, "gx", "gy", "gz"), P(None, "gx", "gy", "gz")),
        check_vma=False,
    )
```

```python
import jax
import jax.numpy as jnp
import numpy as np
from jax import lax
from jax.experimental import pallas as pl
from jax.experimental.pallas import tpu as pltpu
from jax.sharding import PartitionSpec as P

OMEGA = 0.6
LEARN_RATE = 0.5
PIN_WEIGHT = 4.0
ELEMENT_TERMS = (1.0 / 3.0, 0.0, -1.0 / 12.0, -1.0 / 12.0)


def shifted(x, axis, by):
    peers = lax.axis_size(axis)
    pairs = [(i, i + by) for i in range(peers) if 0 <= i + by < peers]
    return lax.ppermute(x, axis, pairs)


def extended(block, sides, width):
    for axis, dim in sides:
        count = lax.axis_size(axis)
        forward = [(i, i + 1) for i in range(count - 1)]
        backward = [(target, source) for source, target in forward]
        low = lax.ppermute(
            lax.slice_in_dim(block, block.shape[dim] - width, None, axis=dim), axis, forward
        )
        high = lax.ppermute(lax.slice_in_dim(block, 0, width, axis=dim), axis, backward)
        block = jnp.concatenate([low, block, high], axis=dim)
    return block


def offset_list():
    return [
        (shift_x, shift_y, shift_z)
        for shift_x in (-1, 0, 1)
        for shift_y in (-1, 0, 1)
        for shift_z in (-1, 0, 1)
    ]


def corner_list():
    return [(bit_x, bit_y, bit_z) for bit_x in (0, 1) for bit_y in (0, 1) for bit_z in (0, 1)]


def hat_weight(distance):
    if distance == 0:
        return 1.0
    if abs(distance) == 1:
        return 0.5
    return 0.0


def galerkin_tables():
    offsets = offset_list()
    tables = np.zeros((27, 27, 27), np.float32)
    for slot_a, outer in enumerate(offsets):
        for slot_c, coarse in enumerate(offsets):
            for slot_f, inner in enumerate(offsets):
                factor = 1.0
                for axis_pos in range(3):
                    factor *= hat_weight(outer[axis_pos]) * hat_weight(
                        2 * coarse[axis_pos] - outer[axis_pos] - inner[axis_pos]
                    )
                tables[slot_a, slot_c, slot_f] = factor
    return tables


def stiffness_of(cell_weight, weight_grad, material, modulus):
    lookup = jnp.zeros(cell_weight.shape, jnp.float32)
    for index in range(modulus.shape[0]):
        lookup = lookup + jnp.where(material == index, modulus[index], 0.0)
    return cell_weight * jnp.exp(-LEARN_RATE * weight_grad) * lookup


def assemble(cell_rim, node_mass, pinned_weight):
    node_shape = node_mass.shape
    rows_out = []
    for offset in offset_list():
        total = jnp.zeros(node_shape, jnp.float32)
        for corner in corner_list():
            if all((0 <= corner[axis_pos] + offset[axis_pos] <= 1 for axis_pos in range(3))):
                total = (
                    total
                    + cell_rim[
                        1 - corner[0] : 1 - corner[0] + node_shape[0],
                        1 - corner[1] : 1 - corner[1] + node_shape[1],
                        1 - corner[2] : 1 - corner[2] + node_shape[2],
                    ]
                )
        nonzero = sum((1 for axis_pos in range(3) if offset[axis_pos] != 0))
        entry = ELEMENT_TERMS[nonzero] * total
        if nonzero == 0:
            entry = entry + node_mass + PIN_WEIGHT * pinned_weight
        rows_out.append(entry)
    return jnp.stack(rows_out)


def galerkin(op_rim, coarse_shape):
    tables = jnp.asarray(galerkin_tables())
    result = None
    for slot_a, outer in enumerate(offset_list()):
        piece = op_rim[
            :,
            outer[0] + 1 : outer[0] + 1 + 2 * coarse_shape[0] : 2,
            outer[1] + 1 : outer[1] + 1 + 2 * coarse_shape[1] : 2,
            outer[2] + 1 : outer[2] + 1 + 2 * coarse_shape[2] : 2,
        ]
        term = jnp.einsum("pk,kxyz->pxyz", tables[slot_a], piece, precision=lax.Precision.HIGHEST)
        result = term if result is None else result + term
    return result


def stencil_apply(stencil, padded):
    node_shape = stencil.shape[1:]
    result = None
    for slot, offset in enumerate(offset_list()):
        window = padded[
            :,
            1 + offset[0] : 1 + offset[0] + node_shape[0],
            1 + offset[1] : 1 + offset[1] + node_shape[1],
            1 + offset[2] : 1 + offset[2] + node_shape[2],
        ]
        term = stencil[slot][None] * window
        result = term if result is None else result + term
    return result


def relax(stencil, field, rhs_field, padded):
    return field + OMEGA * (rhs_field - stencil_apply(stencil, padded)) / stencil[13][None]


def restrict_axis(field, axis_pos, coarse_len):
    below = lax.slice_in_dim(field, 0, 2 * coarse_len - 1, 2, axis_pos)
    centre = lax.slice_in_dim(field, 1, 2 * coarse_len, 2, axis_pos)
    above = lax.slice_in_dim(field, 2, 2 * coarse_len + 1, 2, axis_pos)
    return 0.5 * below + centre + 0.5 * above


def restrict(rim_field, coarse_shape):
    field = rim_field
    for axis_pos in (1, 2, 3):
        field = restrict_axis(field, axis_pos, coarse_shape[axis_pos - 1])
    return field


def prolong_axis(field, axis_pos, coarse_len):
    lower = lax.slice_in_dim(field, 0, coarse_len, 1, axis_pos)
    upper = lax.slice_in_dim(field, 1, coarse_len + 1, 1, axis_pos)
    middle = 0.5 * (lower + upper)
    paired = jnp.stack([lower, middle], axis=axis_pos + 1)
    new_shape = list(lower.shape)
    new_shape[axis_pos] = 2 * coarse_len
    return paired.reshape(new_shape)


def prolong(rim_field, coarse_shape):
    field = rim_field
    for axis_pos in (1, 2, 3):
        field = prolong_axis(field, axis_pos, coarse_shape[axis_pos - 1])
    return field


def boundary_layer(field, axis_pos, forward):
    extent = field.shape[axis_pos]
    if forward:
        return lax.slice_in_dim(field, extent - 1, extent, 1, axis_pos)
    return lax.slice_in_dim(field, 0, 1, 1, axis_pos)


def attach(field, layer_in, axis_pos, forward):
    if forward:
        return jnp.concatenate([layer_in, field], axis=axis_pos)
    return jnp.concatenate([field, layer_in], axis=axis_pos)


def extend(field, leading, forward):
    step = 1 if forward else -1
    got_x = shifted(boundary_layer(field, leading, forward), "gx", step)
    field = attach(field, got_x, leading, forward)
    got_y = shifted(boundary_layer(field, leading + 1, forward), "gy", step)
    field = attach(field, got_y, leading + 1, forward)
    got_z = shifted(boundary_layer(field, leading + 2, forward), "gz", step)
    return attach(field, got_z, leading + 2, forward)


def faces(field):
    return extended(field, (("gx", 1), ("gy", 2), ("gz", 3)), 1)


def shards(cell_weight, weight_grad, material, modulus, node_mass, pinned, positions, forces):
    stiffness = stiffness_of(cell_weight, weight_grad, material, modulus)
    fine_shape = node_mass.shape
    mid_shape = tuple((extent // 2 for extent in fine_shape))
    low_shape = tuple((extent // 4 for extent in fine_shape))
    pinned_weight = pinned.astype(jnp.float32)
    level_zero = assemble(extend(stiffness, 0, True), node_mass, pinned_weight)
    zero_rim = extend(level_zero, 1, True)
    level_one = galerkin(zero_rim, mid_shape)
    level_two = galerkin(extend(level_one, 1, True), low_shape)
    iterate = positions
    for sweep in range(2):
        iterate = relax(level_zero, iterate, forces, faces(iterate))
    residual_zero = forces - stencil_apply(level_zero, faces(iterate))
    rhs_one = restrict(extend(residual_zero, 1, True), mid_shape)
    corr_one = OMEGA * rhs_one / level_one[13][None]
    corr_one = relax(level_one, corr_one, rhs_one, faces(corr_one))
    residual_one = rhs_one - stencil_apply(level_one, faces(corr_one))
    rhs_two = restrict(extend(residual_one, 1, True), low_shape)
    corr_two = OMEGA * rhs_two / level_two[13][None]
    for sweep in range(3):
        corr_two = relax(level_two, corr_two, rhs_two, faces(corr_two))
    corr_one = corr_one + prolong(extend(corr_two, 1, False), low_shape)
    for sweep in range(2):
        corr_one = relax(level_one, corr_one, rhs_one, faces(corr_one))
    iterate = iterate + prolong(extend(corr_one, 1, False), mid_shape)
    for sweep in range(2):
        iterate = relax(level_zero, iterate, forces, faces(iterate))
    return (iterate, level_one)


LANES = 128
ROWS = 8
TILE = (ROWS, LANES)
SNAKE = (0, 1, 3, 2)


def lane_roll(x, by):
    return pltpu.roll(x, by % LANES, x.ndim - 1)


def row_roll(x, by):
    return pltpu.roll(x, by % ROWS, x.ndim - 2)


def lane_ids(shape):
    return lax.broadcasted_iota(jnp.int32, shape, len(shape) - 1)


def row_ids(shape):
    return lax.broadcasted_iota(jnp.int32, shape, len(shape) - 2)


def x_below(x):
    return jnp.where(lane_ids(x.shape) >= 32, lane_roll(x, 32), 0.0)


def x_above(x):
    return jnp.where(lane_ids(x.shape) < 96, lane_roll(x, -32), 0.0)


def y_below(x):
    return jnp.where(row_ids(x.shape) >= 1, row_roll(x, 1), 0.0)


def y_above(x):
    return jnp.where(row_ids(x.shape) < ROWS - 1, row_roll(x, -1), 0.0)


def z_below(x):
    return lane_roll(x, 1)


def z_above(x):
    return lane_roll(x, -1)


def swap_groups(parts, unit):
    group = lane_ids(parts[0].shape) // unit
    parts = list(parts)
    for bit in (1, 2):
        low = (group & bit) == 0
        for i in range(4):
            if i & bit == 0:
                a, b = parts[i], parts[i + bit]
                parts[i] = jnp.where(low, a, lane_roll(b, unit * bit))
                parts[i + bit] = jnp.where(low, lane_roll(a, -unit * bit), b)
    return parts


def pick_lanes(x, source):
    return jnp.take_along_axis(x, jnp.broadcast_to(source, x.shape), axis=-1)


def slab_place(gx, gz):
    order = jnp.where(gx < 2, gx, 5 - gx)
    return jnp.where(lax.rem(gz, 2) == 0, order, 3 - order)


def owner_of(place, gz):
    order = jnp.where(lax.rem(gz, 2) == 0, place, 3 - place)
    return jnp.where(order < 2, order, 5 - order)


def slab_partners():
    gx, gz = lax.axis_index("gx"), lax.axis_index("gz")
    return [lax.bitwise_xor(gx, owner_of(t, gz)) for t in range(4)]


def pack_kernel(
    mod_ref, cw_ref, wg_ref, mat_ref, mass_ref, pin_ref, pos_ref, force_ref, out_0, out_1, out_2, out_3, out_ref,
):
    partners = slab_partners()
    material = mat_ref[...]
    lookup = jnp.zeros(material.shape, jnp.float32)
    for index in range(mod_ref.shape[0]):
        lookup = jnp.where(material == index, mod_ref[index], lookup)
    stiff = cw_ref[...] * jnp.exp(-LEARN_RATE * wg_ref[...]) * lookup
    mass = mass_ref[...] + PIN_WEIGHT * pin_ref[...].astype(jnp.float32)
    fields = [stiff, mass] + [pos_ref[c] for c in range(3)] + [force_ref[c] for c in range(3)]
    lane = lane_ids((16, LANES))
    source = (lane // 32) * 32 + (lane % 8) * 4 + (lane % 32) // 8
    for f, field in enumerate(fields):
        moved = swap_groups([pick_lanes(field[x], source) for x in range(4)], 32)
        for t in range(4):
            out_ref[partners[t], f] = moved[t]
    for j, ref in enumerate((out_0, out_1, out_2, out_3)):
        ref[...] = out_ref[j]


def unpack_kernel(own_ref, one_ref, two_ref, three_ref, iterate_ref, level_ref, hold):
    for j, ref in enumerate((own_ref, one_ref, two_ref, three_ref)):
        hold[j] = ref[...]
    blocks = slab_partners()
    lane = lane_ids((16, LANES))
    source = (lane // 32) * 32 + (lane % 4) * 8 + (lane % 32) // 4
    for c in range(3):
        moved = swap_groups([hold[j, 16 * c:16 * c + 16] for j in blocks], 32)
        for x in range(4):
            iterate_ref[c, x] = pick_lanes(moved[x], source)
    lane = lane_ids(TILE)
    source = ((lane % 64) // 16) * 32 + (lane % 2) * 8 + (lane % 16) // 2
    for g in range(7):
        moved = swap_groups([hold[j, 48 + 8 * g:56 + 8 * g] for j in blocks], 32)
        for o in range(4):
            if 4 * g + o < 27:
                for x in range(2):
                    level_ref[4 * g + o, x] = pick_lanes(moved[o], source + 16 * x)[:, :64]


def fill_low(ref, n):
    ref[0, 1:, 1:] = x_below(ref[n, 1:, 1:])
    ref[:, 0, 1:] = y_below(ref[:, n, 1:])
    ref[:, :, 0] = z_below(ref[:, :, n])


def fill_both(ref, n):
    mid = slice(1, n + 1)
    ref[0, mid, mid] = x_below(ref[n, mid, mid])
    ref[n + 1, mid, mid] = x_above(ref[1, mid, mid])
    ref[:, 0, mid] = y_below(ref[:, n, mid])
    ref[:, n + 1, mid] = y_above(ref[:, 1, mid])
    ref[:, :, 0] = z_below(ref[:, :, n])
    ref[:, :, n + 1] = z_above(ref[:, :, 1])


def add(*terms):
    total = None
    for term in terms:
        if term is not None:
            total = term if total is None else total + term
    return total


def coarsen(low, mid, high, before, count):
    def scaled(x, factor):
        return None if x is None else factor * x

    leads = []
    for i in range(count):
        half = scaled(mid(2 * i + 1), 0.5)
        leads.append((add(low(2 * i + 1), half), add(high(2 * i + 1), half)))
    wrapped = tuple(None if x is None else before(x) for x in leads[-1])
    out = []
    for i in range(count):
        to_low, to_high = leads[i]
        from_low, from_high = leads[i - 1] if i else wrapped
        here = add(scaled(mid(2 * i), 2.0), low(2 * i), high(2 * i), to_low, from_high)
        out.append((add(low(2 * i), from_low), here, add(high(2 * i), to_high)))
    return out


def triple_product(src, mid_a, mid_b, dst, n, faces):
    half = n // 2
    looped = n == 4

    def pass_x(j, y, skip):
        def part(f):
            return lambda i: None if f in skip else src[9 * f + j, i, y]

        for i, trio in enumerate(coarsen(part(0), part(1), part(2), x_below, half)):
            for c in range(3):
                mid_a[9 * c + j, i, y] = trio[c]

    def all_x(y, carry):
        for j in range(9):
            crossed = (j // 3 != 1) + (j % 3 != 1)
            skip = () if not faces or crossed == 2 else ((1,) if crossed == 1 else (0, 2))
            pass_x(j, y, skip)
        return carry

    lax.fori_loop(0, n, all_x, 0, unroll=not looped)

    def pass_y(j, carry):
        base = 9 * (j // 3) + j % 3

        def part(f):
            return lambda i: mid_a[base + 3 * f, :, i]

        for i, trio in enumerate(coarsen(part(0), part(1), part(2), y_below, half)):
            for c in range(3):
                mid_b[base + 3 * c, :, i] = trio[c]
        return carry

    lax.fori_loop(0, 9, pass_y, 0, unroll=not looped)

    def pass_z(j, carry):
        def part(f):
            return lambda i: mid_b[3 * j + f, :, :, i]

        for i, trio in enumerate(coarsen(part(0), part(1), part(2), z_below, half)):
            for c in range(3):
                dst[3 * j + c, :, :, i] = 0.125 * trio[c]
        return carry

    lax.fori_loop(0, 9, pass_z, 0, unroll=not looped)


def sweep(level, field, n, store):
    def body(step, carry):
        x, y = step // n, step % n
        sums = [[None] * n for _ in range(3)]
        for o0 in range(3):
            for o1 in range(3):
                columns = [[field[c, x + o0, y + o1, z] for z in range(n + 2)] for c in range(3)]
                for o2 in range(3):
                    for z in range(n):
                        coef = level[9 * o0 + 3 * o1 + o2, x, y, z]
                        for c in range(3):
                            term = coef * columns[c][z + o2]
                            sums[c][z] = term if sums[c][z] is None else sums[c][z] + term
        for c in range(3):
            for z in range(n):
                store(c, x, y, z, sums[c][z])
        return carry

    lax.fori_loop(0, n * n, body, 0, unroll=True)


def cell_sweep(parts, field, store):
    cells, edge_x, edge_y, edge_z, diag, sums = parts

    def gather(c, carry):
        for x in range(4):
            pair = [[field[c, 1 + x, 1 + y, 1 + z] + field[c, 2 + x, 1 + y, 1 + z] for z in range(5)] for y in range(5)]
            for y in range(4):
                quad = [pair[y][z] + pair[y + 1][z] for z in range(5)]
                for z in range(4):
                    sums[c, 1 + x, 1 + y, 1 + z] = cells[1 + x, 1 + y, 1 + z] * (quad[z] + quad[z + 1])
        fill_low(sums.at[c], 4)
        return carry

    lax.fori_loop(0, 3, gather, 0, unroll=True)

    for x in range(4):
        for y in range(4):
            for c in range(3):
                near = [
                    (sums[c, x, y, z] + sums[c, x, y + 1, z]) + (sums[c, x + 1, y, z] + sums[c, x + 1, y + 1, z])
                    for z in range(5)
                ]
                line = [field[c, 1 + x, 1 + y, z] for z in range(6)]
                for z in range(4):
                    value = diag[x, y, z] * line[1 + z] + (near[z] + near[z + 1])
                    value = value - edge_x[x, y, z] * field[c, x, 1 + y, 1 + z]
                    value = value - edge_x[x + 1, y, z] * field[c, x + 2, 1 + y, 1 + z]
                    value = value - edge_y[x, y, z] * field[c, 1 + x, y, 1 + z]
                    value = value - edge_y[x, y + 1, z] * field[c, 1 + x, y + 2, 1 + z]
                    value = value - edge_z[x, y, z] * line[z]
                    value = value - edge_z[x, y, z + 1] * line[z + 2]
                    store(c, x, y, z, value)


def apply_level(level, field, n, store):
    if n == 4:
        cell_sweep(level, field, store)
    else:
        sweep(level, field, n, store)


def relax_into(level, weight, rhs, src, dst, n):
    def store(c, x, y, z, value):
        dst[c, 1 + x, 1 + y, 1 + z] = src[c, 1 + x, 1 + y, 1 + z] + weight[x, y, z] * (rhs[c, x, y, z] - value)

    apply_level(level, src, n, store)


def residual_down(level, rhs, src, res, coarse_rhs, n):
    half = n // 2

    def store(c, x, y, z, value):
        res[c, 1 + x, 1 + y, 1 + z] = rhs[c, x, y, z] - value

    apply_level(level, src, n, store)

    def body(c, carry):
        fill_low(res.at[c], n)
        for i in range(half):
            part = 0.5 * (res[c, 2 * i] + res[c, 2 * i + 2]) + res[c, 2 * i + 1]
            for j in range(half):
                line = 0.5 * (part[2 * j] + part[2 * j + 2]) + part[2 * j + 1]
                for k in range(half):
                    coarse_rhs[c, i, j, k] = 0.5 * (line[2 * k] + line[2 * k + 2]) + line[2 * k + 1]
        return carry

    lax.fori_loop(0, 3, body, 0, unroll=n < 4)


def add_prolonged(coarse, fine, inside, half):
    def between(values):
        out = []
        for i in range(half):
            out += [values[i], 0.5 * (values[i] + values[i + 1])]
        return out

    def body(c, carry):
        planes = between([coarse[c, 1 + i, 1:, 1:] for i in range(half + 1)])
        for x, plane in enumerate(planes):
            for y, line in enumerate(between([plane[j] for j in range(half + 1)])):
                for z, value in enumerate(between([line[k] for k in range(half + 1)])):
                    fine[c, 1 + x, 1 + y, 1 + z] += jnp.where(inside, value, 0.0)
        return carry

    lax.fori_loop(0, 3, body, 0, unroll=half < 2)


def fill_all(ref, n):
    def body(c, carry):
        fill_both(ref.at[c], n)
        return carry

    lax.fori_loop(0, 3, body, 0, unroll=n < 4)


def cycle_kernel(
    prev_ref, own_ref, next_ref, out_own, out_one, out_two, out_three,
    fields, cells, level_a, weight_a, mid_a, mid_b, level_b, weight_b, mid_c, mid_d, level_c, weight_c,
    va, va2, vb, vb2, vc, vc2, res_a, res_b, rhs_b, rhs_c, out_ref,
    edge_x, edge_y, edge_z, diag, sums,
):
    gx_own, gz = lax.axis_index("gx"), lax.axis_index("gz")
    index = 4 * gz + slab_place(gx_own, gz)
    below, above = lax.max(index - 1, 0), lax.min(index + 1, 15)
    gx_prev = owner_of(lax.rem(below, 4), lax.div(below, 4))
    gx_next = owner_of(lax.rem(above, 4), lax.div(above, 4))
    slab = (lane_ids(TILE) // 8) % 4
    inside = (slab == 1) | ((slab == 0) & (index > 0)) | ((slab == 2) & (index < 15))

    def arrange(step, carry):
        f = step
        for yp in range(4):
            by_source = []
            for source in range(4):
                tiles = [
                    ref[lax.bitwise_xor(gx, source), f, pl.ds(yp, ROWS, stride=4), :]
                    for ref, gx in ((prev_ref, gx_prev), (own_ref, gx_own), (next_ref, gx_next))
                ]
                by_source.append(swap_groups(tiles + [jnp.zeros(TILE, jnp.float32)], 8))
            for zp in range(4):
                moved = swap_groups([by_source[source][zp] for source in range(4)], 32)
                for xp in range(4):
                    fields[f, xp, yp, zp] = moved[xp]
        return carry

    lax.fori_loop(0, 8, arrange, 0)

    for x in range(4):
        cells[1 + x, 1:, 1:] = fields[0, x] * ELEMENT_TERMS[3]
    fill_low(cells, 4)

    def build(step, carry):
        x, y = step // 4, step % 4
        near = [[[cells[x + 1 - s0, y + 1 - s1, z] for z in range(5)] for s1 in (0, 1)] for s0 in (0, 1)]
        for z in range(4):
            for slot, offset in enumerate(offset_list()):
                nonzero = sum(1 for part in offset if part != 0)
                if nonzero == 1:
                    continue
                total = None
                for s in corner_list():
                    if all(0 <= s[d] + offset[d] <= 1 for d in range(3)):
                        term = near[s[0]][s[1]][z + 1 - s[2]]
                        total = term if total is None else total + term
                if nonzero == 0:
                    mass = fields[1, x, y, z]
                    diag[x, y, z] = ((ELEMENT_TERMS[0] - ELEMENT_TERMS[3]) / ELEMENT_TERMS[3]) * total + mass
                    total = (ELEMENT_TERMS[0] / ELEMENT_TERMS[3]) * total + mass
                    weight_a[x, y, z] = jnp.where(inside, OMEGA / jnp.where(inside, total, 1.0), 0.0)
                level_a[slot, x, y, z] = total
        return carry

    lax.fori_loop(0, 16, build, 0)

    edge_z[...] = (cells[1:, 1:] + cells[:4, 1:]) + (cells[1:, :4] + cells[:4, :4])
    over_z = cells[:, :, 1:] + cells[:, :, :4]
    edge_x[...] = over_z[:, 1:] + over_z[:, :4]
    edge_y[...] = over_z[1:] + over_z[:4]
    fine = (cells, edge_x, edge_y, edge_z, diag, sums)

    triple_product(level_a, mid_a, mid_b, level_b, 4, True)
    weight_b[...] = jnp.where(inside, OMEGA / jnp.where(inside, level_b[13], 1.0), 0.0)
    triple_product(level_b, mid_c, mid_d, level_c, 2, False)
    weight_c[...] = jnp.where(inside, OMEGA / jnp.where(inside, level_c[13], 1.0), 0.0)

    position, force = fields.at[2:5], fields.at[5:8]

    def load(c, carry):
        for x in range(4):
            va[c, 1 + x, 1:5, 1:5] = position[c, x]
        return carry

    lax.fori_loop(0, 3, load, 0)
    fill_all(va, 4)
    relax_into(fine, weight_a, force, va, va2, 4)
    fill_all(va2, 4)
    relax_into(fine, weight_a, force, va2, va, 4)
    fill_all(va, 4)
    residual_down(fine, force, va, res_a, rhs_b, 4)

    for c in range(3):
        for x in range(2):
            vb[c, 1 + x, 1:3, 1:3] = weight_b[x] * rhs_b[c, x]
    fill_all(vb, 2)
    relax_into(level_b, weight_b, rhs_b, vb, vb2, 2)
    fill_all(vb2, 2)
    residual_down(level_b, rhs_b, vb2, res_b, rhs_c, 2)

    for c in range(3):
        vc[c, 1, 1, 1] = weight_c[0, 0, 0] * rhs_c[c, 0, 0, 0]
    fill_all(vc, 1)
    relax_into(level_c, weight_c, rhs_c, vc, vc2, 1)
    fill_all(vc2, 1)
    relax_into(level_c, weight_c, rhs_c, vc2, vc, 1)
    fill_all(vc, 1)
    relax_into(level_c, weight_c, rhs_c, vc, vc2, 1)
    fill_all(vc2, 1)

    add_prolonged(vc2, vb2, inside, 1)
    fill_all(vb2, 2)
    relax_into(level_b, weight_b, rhs_b, vb2, vb, 2)
    fill_all(vb, 2)
    relax_into(level_b, weight_b, rhs_b, vb, vb2, 2)
    fill_all(vb2, 2)

    add_prolonged(vb2, va, inside, 2)
    fill_all(va, 4)
    relax_into(fine, weight_a, force, va, va2, 4)
    fill_all(va2, 4)
    relax_into(fine, weight_a, force, va2, va, 4)

    def own_slab(tiles):
        total = None
        for group, tile in enumerate(tiles):
            moved = lane_roll(tile, 8 * group - 8)
            total = moved if total is None else jnp.where(slab == group, moved, total)
        return total

    def send_field(c, carry):
        for yp in range(4):
            lines = [own_slab([va[c, 1 + xp, 1 + yp, 1 + zp] for zp in range(4)]) for xp in range(4)]
            for dest, tile in enumerate(swap_groups(lines, 32)):
                out_ref[lax.bitwise_xor(gx_own, dest), pl.ds(32 * c + yp, ROWS, stride=4), :] = tile
        return carry

    lax.fori_loop(0, 3, send_field, 0)

    for g in range(7):
        for yp in range(2):
            lines = [
                own_slab([level_b[min(4 * g + o, 26), xp, yp, zp] for xp in range(2) for zp in range(2)])
                for o in range(4)
            ]
            for dest, tile in enumerate(swap_groups(lines, 32)):
                out_ref[lax.bitwise_xor(gx_own, dest), pl.ds(96 + 16 * g + yp, ROWS, stride=2), :] = tile

    side = lax.axis_index("gy")
    for j, ref in enumerate((out_own, out_one, out_two, out_three)):
        for c in range(3):
            ref[16 * c:16 * c + 16] = out_ref[j, pl.ds(pl.multiple_of(32 * c + 16 * side, 16), 16), :]
        for g in range(7):
            ref[48 + 8 * g:56 + 8 * g] = out_ref[j, pl.ds(pl.multiple_of(96 + 16 * g + 8 * side, 8), 8), :]


def slab_owner(place, gz):
    order = place if gz % 2 == 0 else 3 - place
    return SNAKE[order]


def vmem_specs(count):
    return [pl.BlockSpec(memory_space=pltpu.VMEM)] * count


def shards_by_slab(cell_weight, weight_grad, material, modulus, node_mass, pinned, positions, forces):
    smem = pl.BlockSpec(memory_space=pltpu.SMEM)
    gx, gy, gz = lax.axis_index("gx"), lax.axis_index("gy"), lax.axis_index("gz")
    f32 = jnp.float32
    index = 4 * gz + slab_place(gx, gz)
    packed = pl.pallas_call(
        pack_kernel,
        out_shape=[pltpu.VMEM((8, 16, LANES), f32)] * 4,
        in_specs=[smem] + vmem_specs(7),
        out_specs=vmem_specs(4),
        scratch_shapes=[pltpu.VMEM((4, 8, 16, LANES), f32)],
        name="pack",
    )(modulus, cell_weight, weight_grad, material, node_mass, pinned, positions, forces)

    mine = [packed[0]]
    for j in range(1, 4):
        mine.append(lax.ppermute(packed[j], "gx", [(i, i ^ j) for i in range(4)]))
    mine = jnp.stack(mine)

    def swap_in_chain(first):
        pairs = []
        for core in range(2):
            chain = [(slab_owner(at, z) * 2 + core) * 4 + z for z in range(4) for at in range(4)]
            for at in range(first, 15, 2):
                pairs += [(chain[at], chain[at + 1]), (chain[at + 1], chain[at])]
            if first:
                pairs += [(chain[end], chain[end] ^ 4) for end in (0, 15)]
        return lax.ppermute(mine, ("gx", "gy", "gz"), pairs)

    even, odd = swap_in_chain(0), swap_in_chain(1)

    def both_halves(half, present):
        other = lax.ppermute(half, "gy", [(0, 1), (1, 0)])
        rows = jnp.concatenate([jnp.where(gy == 0, half, other), jnp.where(gy == 0, other, half)], axis=2)
        return jnp.where(present, rows, 0.0)

    odd_place = index % 2 == 1
    own = both_halves(mine, True)
    even = both_halves(even, True)
    odd = both_halves(odd, (index > 0) & (index < 15))
    before = jnp.where(odd_place, even, odd)
    after = jnp.where(odd_place, odd, even)

    def buf(*dims):
        return pltpu.VMEM(tuple(dims) + TILE, f32)

    message = pl.pallas_call(
        cycle_kernel,
        out_shape=[pltpu.VMEM((104, LANES), f32)] * 4,
        in_specs=vmem_specs(3),
        out_specs=vmem_specs(4),
        scratch_shapes=[
            buf(8, 4, 4, 4), buf(5, 5, 5), buf(27, 4, 4, 4), buf(4, 4, 4),
            buf(27, 2, 4, 4), buf(27, 2, 2, 4), buf(27, 2, 2, 2), buf(2, 2, 2),
            buf(27, 1, 2, 2), buf(27, 1, 1, 2), buf(27, 1, 1, 1), buf(1, 1, 1),
            buf(3, 6, 6, 6), buf(3, 6, 6, 6), buf(3, 4, 4, 4), buf(3, 4, 4, 4), buf(3, 3, 3, 3), buf(3, 3, 3, 3),
            buf(3, 5, 5, 5), buf(3, 3, 3, 3), buf(3, 2, 2, 2), buf(3, 1, 1, 1),
            pltpu.VMEM((4, 208, LANES), f32),
            buf(5, 4, 4), buf(4, 5, 4), buf(4, 4, 5), buf(4, 4, 4), buf(3, 5, 5, 5),
        ],
        compiler_params=pltpu.CompilerParams(vmem_limit_bytes=48 * 1024 * 1024),
        name="cycle",
    )(before, own, after)

    back = [message[0]]
    for j in range(1, 4):
        back.append(lax.ppermute(message[j], "gx", [(i, i ^ j) for i in range(4)]))
    return pl.pallas_call(
        unpack_kernel,
        out_shape=[
            jax.ShapeDtypeStruct(positions.shape, f32),
            jax.ShapeDtypeStruct((27, 2, 8, 64), f32),
        ],
        in_specs=vmem_specs(4),
        out_specs=vmem_specs(2),
        scratch_shapes=[pltpu.VMEM((4, 104, LANES), f32)],
        name="unpack",
    )(*back)


def solution(mesh):
    placed = (
        P("gx", "gy", "gz"),
        P("gx", "gy", "gz"),
        P("gx", "gy", "gz"),
        P(),
        P("gx", "gy", "gz"),
        P("gx", "gy", "gz"),
        P(None, "gx", "gy", "gz"),
        P(None, "gx", "gy", "gz"),
    )
    sizes = tuple(mesh.shape[axis] for axis in ("gx", "gy", "gz"))

    def choose(cell_weight, *rest):
        fits = sizes == (4, 2, 4) and cell_weight.shape == (4, 16, 128)
        return (shards_by_slab if fits else shards)(cell_weight, *rest)

    return jax.shard_map(
        choose,
        mesh=mesh,
        in_specs=placed,
        out_specs=(P(None, "gx", "gy", "gz"), P(None, "gx", "gy", "gz")),
        check_vma=False,
    )
```

```python
import jax
import jax.numpy as jnp
import numpy as np
from jax import lax
from jax.experimental import pallas as pl
from jax.experimental.pallas import tpu as pltpu
from jax.sharding import PartitionSpec as P

OMEGA = 0.6
LEARN_RATE = 0.5
PIN_WEIGHT = 4.0
ELEMENT_TERMS = (1.0 / 3.0, 0.0, -1.0 / 12.0, -1.0 / 12.0)


def shifted(x, axis, by):
    peers = lax.axis_size(axis)
    pairs = [(i, i + by) for i in range(peers) if 0 <= i + by < peers]
    return lax.ppermute(x, axis, pairs)


def extended(block, sides, width):
    for axis, dim in sides:
        count = lax.axis_size(axis)
        forward = [(i, i + 1) for i in range(count - 1)]
        backward = [(target, source) for source, target in forward]
        low = lax.ppermute(
            lax.slice_in_dim(block, block.shape[dim] - width, None, axis=dim), axis, forward
        )
        high = lax.ppermute(lax.slice_in_dim(block, 0, width, axis=dim), axis, backward)
        block = jnp.concatenate([low, block, high], axis=dim)
    return block


def offset_list():
    return [
        (shift_x, shift_y, shift_z)
        for shift_x in (-1, 0, 1)
        for shift_y in (-1, 0, 1)
        for shift_z in (-1, 0, 1)
    ]


def corner_list():
    return [(bit_x, bit_y, bit_z) for bit_x in (0, 1) for bit_y in (0, 1) for bit_z in (0, 1)]


def hat_weight(distance):
    if distance == 0:
        return 1.0
    if abs(distance) == 1:
        return 0.5
    return 0.0


def galerkin_tables():
    offsets = offset_list()
    tables = np.zeros((27, 27, 27), np.float32)
    for slot_a, outer in enumerate(offsets):
        for slot_c, coarse in enumerate(offsets):
            for slot_f, inner in enumerate(offsets):
                factor = 1.0
                for axis_pos in range(3):
                    factor *= hat_weight(outer[axis_pos]) * hat_weight(
                        2 * coarse[axis_pos] - outer[axis_pos] - inner[axis_pos]
                    )
                tables[slot_a, slot_c, slot_f] = factor
    return tables


def stiffness_of(cell_weight, weight_grad, material, modulus):
    lookup = jnp.zeros(cell_weight.shape, jnp.float32)
    for index in range(modulus.shape[0]):
        lookup = lookup + jnp.where(material == index, modulus[index], 0.0)
    return cell_weight * jnp.exp(-LEARN_RATE * weight_grad) * lookup


def assemble(cell_rim, node_mass, pinned_weight):
    node_shape = node_mass.shape
    rows_out = []
    for offset in offset_list():
        total = jnp.zeros(node_shape, jnp.float32)
        for corner in corner_list():
            if all((0 <= corner[axis_pos] + offset[axis_pos] <= 1 for axis_pos in range(3))):
                total = (
                    total
                    + cell_rim[
                        1 - corner[0] : 1 - corner[0] + node_shape[0],
                        1 - corner[1] : 1 - corner[1] + node_shape[1],
                        1 - corner[2] : 1 - corner[2] + node_shape[2],
                    ]
                )
        nonzero = sum((1 for axis_pos in range(3) if offset[axis_pos] != 0))
        entry = ELEMENT_TERMS[nonzero] * total
        if nonzero == 0:
            entry = entry + node_mass + PIN_WEIGHT * pinned_weight
        rows_out.append(entry)
    return jnp.stack(rows_out)


def galerkin(op_rim, coarse_shape):
    tables = jnp.asarray(galerkin_tables())
    result = None
    for slot_a, outer in enumerate(offset_list()):
        piece = op_rim[
            :,
            outer[0] + 1 : outer[0] + 1 + 2 * coarse_shape[0] : 2,
            outer[1] + 1 : outer[1] + 1 + 2 * coarse_shape[1] : 2,
            outer[2] + 1 : outer[2] + 1 + 2 * coarse_shape[2] : 2,
        ]
        term = jnp.einsum("pk,kxyz->pxyz", tables[slot_a], piece, precision=lax.Precision.HIGHEST)
        result = term if result is None else result + term
    return result


def stencil_apply(stencil, padded):
    node_shape = stencil.shape[1:]
    result = None
    for slot, offset in enumerate(offset_list()):
        window = padded[
            :,
            1 + offset[0] : 1 + offset[0] + node_shape[0],
            1 + offset[1] : 1 + offset[1] + node_shape[1],
            1 + offset[2] : 1 + offset[2] + node_shape[2],
        ]
        term = stencil[slot][None] * window
        result = term if result is None else result + term
    return result


def relax(stencil, field, rhs_field, padded):
    return field + OMEGA * (rhs_field - stencil_apply(stencil, padded)) / stencil[13][None]


def restrict_axis(field, axis_pos, coarse_len):
    below = lax.slice_in_dim(field, 0, 2 * coarse_len - 1, 2, axis_pos)
    centre = lax.slice_in_dim(field, 1, 2 * coarse_len, 2, axis_pos)
    above = lax.slice_in_dim(field, 2, 2 * coarse_len + 1, 2, axis_pos)
    return 0.5 * below + centre + 0.5 * above


def restrict(rim_field, coarse_shape):
    field = rim_field
    for axis_pos in (1, 2, 3):
        field = restrict_axis(field, axis_pos, coarse_shape[axis_pos - 1])
    return field


def prolong_axis(field, axis_pos, coarse_len):
    lower = lax.slice_in_dim(field, 0, coarse_len, 1, axis_pos)
    upper = lax.slice_in_dim(field, 1, coarse_len + 1, 1, axis_pos)
    middle = 0.5 * (lower + upper)
    paired = jnp.stack([lower, middle], axis=axis_pos + 1)
    new_shape = list(lower.shape)
    new_shape[axis_pos] = 2 * coarse_len
    return paired.reshape(new_shape)


def prolong(rim_field, coarse_shape):
    field = rim_field
    for axis_pos in (1, 2, 3):
        field = prolong_axis(field, axis_pos, coarse_shape[axis_pos - 1])
    return field


def boundary_layer(field, axis_pos, forward):
    extent = field.shape[axis_pos]
    if forward:
        return lax.slice_in_dim(field, extent - 1, extent, 1, axis_pos)
    return lax.slice_in_dim(field, 0, 1, 1, axis_pos)


def attach(field, layer_in, axis_pos, forward):
    if forward:
        return jnp.concatenate([layer_in, field], axis=axis_pos)
    return jnp.concatenate([field, layer_in], axis=axis_pos)


def extend(field, leading, forward):
    step = 1 if forward else -1
    got_x = shifted(boundary_layer(field, leading, forward), "gx", step)
    field = attach(field, got_x, leading, forward)
    got_y = shifted(boundary_layer(field, leading + 1, forward), "gy", step)
    field = attach(field, got_y, leading + 1, forward)
    got_z = shifted(boundary_layer(field, leading + 2, forward), "gz", step)
    return attach(field, got_z, leading + 2, forward)


def faces(field):
    return extended(field, (("gx", 1), ("gy", 2), ("gz", 3)), 1)


def shards(cell_weight, weight_grad, material, modulus, node_mass, pinned, positions, forces):
    stiffness = stiffness_of(cell_weight, weight_grad, material, modulus)
    fine_shape = node_mass.shape
    mid_shape = tuple((extent // 2 for extent in fine_shape))
    low_shape = tuple((extent // 4 for extent in fine_shape))
    pinned_weight = pinned.astype(jnp.float32)
    level_zero = assemble(extend(stiffness, 0, True), node_mass, pinned_weight)
    zero_rim = extend(level_zero, 1, True)
    level_one = galerkin(zero_rim, mid_shape)
    level_two = galerkin(extend(level_one, 1, True), low_shape)
    iterate = positions
    for sweep in range(2):
        iterate = relax(level_zero, iterate, forces, faces(iterate))
    residual_zero = forces - stencil_apply(level_zero, faces(iterate))
    rhs_one = restrict(extend(residual_zero, 1, True), mid_shape)
    corr_one = OMEGA * rhs_one / level_one[13][None]
    corr_one = relax(level_one, corr_one, rhs_one, faces(corr_one))
    residual_one = rhs_one - stencil_apply(level_one, faces(corr_one))
    rhs_two = restrict(extend(residual_one, 1, True), low_shape)
    corr_two = OMEGA * rhs_two / level_two[13][None]
    for sweep in range(3):
        corr_two = relax(level_two, corr_two, rhs_two, faces(corr_two))
    corr_one = corr_one + prolong(extend(corr_two, 1, False), low_shape)
    for sweep in range(2):
        corr_one = relax(level_one, corr_one, rhs_one, faces(corr_one))
    iterate = iterate + prolong(extend(corr_one, 1, False), mid_shape)
    for sweep in range(2):
        iterate = relax(level_zero, iterate, forces, faces(iterate))
    return (iterate, level_one)


LANES = 128
ROWS = 8
TILE = (ROWS, LANES)
SNAKE = (0, 1, 3, 2)


def lane_roll(x, by):
    return pltpu.roll(x, by % LANES, x.ndim - 1)


def row_roll(x, by):
    return pltpu.roll(x, by % ROWS, x.ndim - 2)


def lane_ids(shape):
    return lax.broadcasted_iota(jnp.int32, shape, len(shape) - 1)


def row_ids(shape):
    return lax.broadcasted_iota(jnp.int32, shape, len(shape) - 2)


def x_below(x):
    return jnp.where(lane_ids(x.shape) >= 32, lane_roll(x, 32), 0.0)


def x_above(x):
    return jnp.where(lane_ids(x.shape) < 96, lane_roll(x, -32), 0.0)


def y_below(x):
    return jnp.where(row_ids(x.shape) >= 1, row_roll(x, 1), 0.0)


def y_above(x):
    return jnp.where(row_ids(x.shape) < ROWS - 1, row_roll(x, -1), 0.0)


def z_below(x):
    return lane_roll(x, 1)


def z_above(x):
    return lane_roll(x, -1)


def swap_groups(parts, unit):
    group = lane_ids(parts[0].shape) // unit
    parts = list(parts)
    for bit in (1, 2):
        low = (group & bit) == 0
        for i in range(4):
            if i & bit == 0:
                a, b = parts[i], parts[i + bit]
                parts[i] = jnp.where(low, a, lane_roll(b, unit * bit))
                parts[i + bit] = jnp.where(low, lane_roll(a, -unit * bit), b)
    return parts


def pick_lanes(x, source):
    return jnp.take_along_axis(x, jnp.broadcast_to(source, x.shape), axis=-1)


def slab_place(gx, gz):
    order = jnp.where(gx < 2, gx, 5 - gx)
    return jnp.where(lax.rem(gz, 2) == 0, order, 3 - order)


def owner_of(place, gz):
    order = jnp.where(lax.rem(gz, 2) == 0, place, 3 - place)
    return jnp.where(order < 2, order, 5 - order)


def slab_partners():
    gx, gz = lax.axis_index("gx"), lax.axis_index("gz")
    return [lax.bitwise_xor(gx, owner_of(t, gz)) for t in range(4)]


def pack_kernel(
    mod_ref, cw_ref, wg_ref, mat_ref, mass_ref, pin_ref, pos_ref, force_ref, out_0, out_1, out_2, out_3, out_ref,
):
    partners = slab_partners()
    material = mat_ref[...]
    lookup = jnp.zeros(material.shape, jnp.float32)
    for index in range(mod_ref.shape[0]):
        lookup = jnp.where(material == index, mod_ref[index], lookup)
    stiff = cw_ref[...] * jnp.exp(-LEARN_RATE * wg_ref[...]) * lookup
    mass = mass_ref[...] + PIN_WEIGHT * pin_ref[...].astype(jnp.float32)
    fields = [stiff, mass] + [pos_ref[c] for c in range(3)] + [force_ref[c] for c in range(3)]
    lane = lane_ids((16, LANES))
    source = (lane // 32) * 32 + (lane % 8) * 4 + (lane % 32) // 8
    for f, field in enumerate(fields):
        moved = swap_groups([pick_lanes(field[x], source) for x in range(4)], 32)
        for t in range(4):
            out_ref[partners[t], f] = moved[t]
    for j, ref in enumerate((out_0, out_1, out_2, out_3)):
        ref[...] = out_ref[j]


def unpack_kernel(own_ref, one_ref, two_ref, three_ref, iterate_ref, level_ref, hold):
    for j, ref in enumerate((own_ref, one_ref, two_ref, three_ref)):
        hold[j] = ref[...]
    blocks = slab_partners()
    lane = lane_ids((16, LANES))
    source = (lane // 32) * 32 + (lane % 4) * 8 + (lane % 32) // 4
    for c in range(3):
        moved = swap_groups([hold[j, 16 * c:16 * c + 16] for j in blocks], 32)
        for x in range(4):
            iterate_ref[c, x] = pick_lanes(moved[x], source)
    lane = lane_ids(TILE)
    source = ((lane % 64) // 16) * 32 + (lane % 2) * 8 + (lane % 16) // 2
    for g in range(7):
        moved = swap_groups([hold[j, 48 + 8 * g:56 + 8 * g] for j in blocks], 32)
        for o in range(4):
            if 4 * g + o < 27:
                for x in range(2):
                    level_ref[4 * g + o, x] = pick_lanes(moved[o], source + 16 * x)[:, :64]


def fill_low(ref, n):
    ref[0, 1:, 1:] = x_below(ref[n, 1:, 1:])
    ref[:, 0, 1:] = y_below(ref[:, n, 1:])
    ref[:, :, 0] = z_below(ref[:, :, n])


def fill_both(ref, n):
    mid = slice(1, n + 1)
    ref[0, mid, mid] = x_below(ref[n, mid, mid])
    ref[n + 1, mid, mid] = x_above(ref[1, mid, mid])
    ref[:, 0, mid] = y_below(ref[:, n, mid])
    ref[:, n + 1, mid] = y_above(ref[:, 1, mid])
    ref[:, :, 0] = z_below(ref[:, :, n])
    ref[:, :, n + 1] = z_above(ref[:, :, 1])


def add(*terms):
    total = None
    for term in terms:
        if term is not None:
            total = term if total is None else total + term
    return total


def coarsen(low, mid, high, before, count):
    def scaled(x, factor):
        return None if x is None else factor * x

    leads = []
    for i in range(count):
        half = scaled(mid(2 * i + 1), 0.5)
        leads.append((add(low(2 * i + 1), half), add(high(2 * i + 1), half)))
    wrapped = tuple(None if x is None else before(x) for x in leads[-1])
    out = []
    for i in range(count):
        to_low, to_high = leads[i]
        from_low, from_high = leads[i - 1] if i else wrapped
        here = add(scaled(mid(2 * i), 2.0), low(2 * i), high(2 * i), to_low, from_high)
        out.append((add(low(2 * i), from_low), here, add(high(2 * i), to_high)))
    return out


def triple_product(src, mid_a, mid_b, dst, n, faces):
    half = n // 2
    looped = n == 4

    def pass_x(j, y, skip):
        def part(f):
            return lambda i: None if f in skip else src[9 * f + j, i, y]

        for i, trio in enumerate(coarsen(part(0), part(1), part(2), x_below, half)):
            for c in range(3):
                mid_a[9 * c + j, i, y] = trio[c]

    def all_x(y, carry):
        for j in range(9):
            crossed = (j // 3 != 1) + (j % 3 != 1)
            skip = () if not faces or crossed == 2 else ((1,) if crossed == 1 else (0, 2))
            pass_x(j, y, skip)
        return carry

    lax.fori_loop(0, n, all_x, 0, unroll=not looped)

    def pass_y(j, carry):
        base = 9 * (j // 3) + j % 3

        def part(f):
            return lambda i: mid_a[base + 3 * f, :, i]

        for i, trio in enumerate(coarsen(part(0), part(1), part(2), y_below, half)):
            for c in range(3):
                mid_b[base + 3 * c, :, i] = trio[c]
        return carry

    lax.fori_loop(0, 9, pass_y, 0, unroll=not looped)

    def pass_z(j, carry):
        def part(f):
            return lambda i: mid_b[3 * j + f, :, :, i]

        for i, trio in enumerate(coarsen(part(0), part(1), part(2), z_below, half)):
            for c in range(3):
                dst[3 * j + c, :, :, i] = 0.125 * trio[c]
        return carry

    lax.fori_loop(0, 9, pass_z, 0, unroll=not looped)


def sweep(level, field, n, store):
    def body(step, carry):
        x, y = step // n, step % n
        sums = [[None] * n for _ in range(3)]
        for o0 in range(3):
            for o1 in range(3):
                columns = [[field[c, x + o0, y + o1, z] for z in range(n + 2)] for c in range(3)]
                for o2 in range(3):
                    for z in range(n):
                        coef = level[9 * o0 + 3 * o1 + o2, x, y, z]
                        for c in range(3):
                            term = coef * columns[c][z + o2]
                            sums[c][z] = term if sums[c][z] is None else sums[c][z] + term
        for c in range(3):
            for z in range(n):
                store(c, x, y, z, sums[c][z])
        return carry

    lax.fori_loop(0, n * n, body, 0, unroll=True)


def cell_sweep(parts, field, store):
    cells, edge_x, edge_y, edge_z, diag, sums = parts

    def gather(c, carry):
        for x in range(4):
            pair = [[field[c, 1 + x, 1 + y, 1 + z] + field[c, 2 + x, 1 + y, 1 + z] for z in range(5)] for y in range(5)]
            for y in range(4):
                quad = [pair[y][z] + pair[y + 1][z] for z in range(5)]
                for z in range(4):
                    sums[c, 1 + x, 1 + y, 1 + z] = cells[1 + x, 1 + y, 1 + z] * (quad[z] + quad[z + 1])
        fill_low(sums.at[c], 4)
        return carry

    lax.fori_loop(0, 3, gather, 0, unroll=True)

    for x in range(4):
        for y in range(4):
            for c in range(3):
                near = [
                    (sums[c, x, y, z] + sums[c, x, y + 1, z]) + (sums[c, x + 1, y, z] + sums[c, x + 1, y + 1, z])
                    for z in range(5)
                ]
                line = [field[c, 1 + x, 1 + y, z] for z in range(6)]
                for z in range(4):
                    value = diag[x, y, z] * line[1 + z] + (near[z] + near[z + 1])
                    value = value - edge_x[x, y, z] * field[c, x, 1 + y, 1 + z]
                    value = value - edge_x[x + 1, y, z] * field[c, x + 2, 1 + y, 1 + z]
                    value = value - edge_y[x, y, z] * field[c, 1 + x, y, 1 + z]
                    value = value - edge_y[x, y + 1, z] * field[c, 1 + x, y + 2, 1 + z]
                    value = value - edge_z[x, y, z] * line[z]
                    value = value - edge_z[x, y, z + 1] * line[z + 2]
                    store(c, x, y, z, value)


def apply_level(level, field, n, store):
    if n == 4:
        cell_sweep(level, field, store)
    else:
        sweep(level, field, n, store)


def relax_into(level, weight, rhs, src, dst, n):
    def store(c, x, y, z, value):
        dst[c, 1 + x, 1 + y, 1 + z] = src[c, 1 + x, 1 + y, 1 + z] + weight[x, y, z] * (rhs[c, x, y, z] - value)

    apply_level(level, src, n, store)


def residual_down(level, rhs, src, res, coarse_rhs, n):
    half = n // 2

    def store(c, x, y, z, value):
        res[c, 1 + x, 1 + y, 1 + z] = rhs[c, x, y, z] - value

    apply_level(level, src, n, store)

    def body(c, carry):
        fill_low(res.at[c], n)
        for i in range(half):
            part = 0.5 * (res[c, 2 * i] + res[c, 2 * i + 2]) + res[c, 2 * i + 1]
            for j in range(half):
                line = 0.5 * (part[2 * j] + part[2 * j + 2]) + part[2 * j + 1]
                for k in range(half):
                    coarse_rhs[c, i, j, k] = 0.5 * (line[2 * k] + line[2 * k + 2]) + line[2 * k + 1]
        return carry

    lax.fori_loop(0, 3, body, 0, unroll=n < 4)


def add_prolonged(coarse, fine, inside, half):
    def between(values):
        out = []
        for i in range(half):
            out += [values[i], 0.5 * (values[i] + values[i + 1])]
        return out

    def body(c, carry):
        planes = between([coarse[c, 1 + i, 1:, 1:] for i in range(half + 1)])
        for x, plane in enumerate(planes):
            for y, line in enumerate(between([plane[j] for j in range(half + 1)])):
                for z, value in enumerate(between([line[k] for k in range(half + 1)])):
                    fine[c, 1 + x, 1 + y, 1 + z] += jnp.where(inside, value, 0.0)
        return carry

    lax.fori_loop(0, 3, body, 0, unroll=half < 2)


def fill_all(ref, n):
    def body(c, carry):
        fill_both(ref.at[c], n)
        return carry

    lax.fori_loop(0, 3, body, 0, unroll=n < 4)


def cycle_kernel(
    prev_ref, own_ref, next_ref, out_own, out_one, out_two, out_three,
    fields, cells, level_a, weight_a, mid_a, mid_b, level_b, weight_b, mid_c, mid_d, level_c, weight_c,
    va, va2, vb, vb2, vc, vc2, res_a, res_b, rhs_b, rhs_c, out_ref,
    edge_x, edge_y, edge_z, diag, sums,
):
    gx_own, gz = lax.axis_index("gx"), lax.axis_index("gz")
    index = 4 * gz + slab_place(gx_own, gz)
    below, above = lax.max(index - 1, 0), lax.min(index + 1, 15)
    gx_prev = owner_of(lax.rem(below, 4), lax.div(below, 4))
    gx_next = owner_of(lax.rem(above, 4), lax.div(above, 4))
    slab = (lane_ids(TILE) // 8) % 4
    inside = (slab == 1) | ((slab == 0) & (index > 0)) | ((slab == 2) & (index < 15))

    def arrange(step, carry):
        f = step
        for yp in range(4):
            by_source = []
            for source in range(4):
                tiles = [
                    ref[lax.bitwise_xor(gx, source), f, pl.ds(yp, ROWS, stride=4), :]
                    for ref, gx in ((prev_ref, gx_prev), (own_ref, gx_own), (next_ref, gx_next))
                ]
                by_source.append(swap_groups(tiles + [jnp.zeros(TILE, jnp.float32)], 8))
            for zp in range(4):
                moved = swap_groups([by_source[source][zp] for source in range(4)], 32)
                for xp in range(4):
                    fields[f, xp, yp, zp] = moved[xp]
        return carry

    lax.fori_loop(0, 8, arrange, 0)

    for x in range(4):
        cells[1 + x, 1:, 1:] = fields[0, x] * ELEMENT_TERMS[3]
    fill_low(cells, 4)

    def build(step, carry):
        x, y = step // 4, step % 4
        near = [[[cells[x + 1 - s0, y + 1 - s1, z] for z in range(5)] for s1 in (0, 1)] for s0 in (0, 1)]
        for z in range(4):
            for slot, offset in enumerate(offset_list()):
                nonzero = sum(1 for part in offset if part != 0)
                if nonzero == 1:
                    continue
                total = None
                for s in corner_list():
                    if all(0 <= s[d] + offset[d] <= 1 for d in range(3)):
                        term = near[s[0]][s[1]][z + 1 - s[2]]
                        total = term if total is None else total + term
                if nonzero == 0:
                    mass = fields[1, x, y, z]
                    diag[x, y, z] = ((ELEMENT_TERMS[0] - ELEMENT_TERMS[3]) / ELEMENT_TERMS[3]) * total + mass
                    total = (ELEMENT_TERMS[0] / ELEMENT_TERMS[3]) * total + mass
                    weight_a[x, y, z] = jnp.where(inside, OMEGA / jnp.where(inside, total, 1.0), 0.0)
                level_a[slot, x, y, z] = total
        return carry

    lax.fori_loop(0, 16, build, 0)

    edge_z[...] = (cells[1:, 1:] + cells[:4, 1:]) + (cells[1:, :4] + cells[:4, :4])
    over_z = cells[:, :, 1:] + cells[:, :, :4]
    edge_x[...] = over_z[:, 1:] + over_z[:, :4]
    edge_y[...] = over_z[1:] + over_z[:4]
    fine = (cells, edge_x, edge_y, edge_z, diag, sums)

    triple_product(level_a, mid_a, mid_b, level_b, 4, True)
    weight_b[...] = jnp.where(inside, OMEGA / jnp.where(inside, level_b[13], 1.0), 0.0)
    triple_product(level_b, mid_c, mid_d, level_c, 2, False)
    weight_c[...] = jnp.where(inside, OMEGA / jnp.where(inside, level_c[13], 1.0), 0.0)

    position, force = fields.at[2:5], fields.at[5:8]

    def load(c, carry):
        for x in range(4):
            va[c, 1 + x, 1:5, 1:5] = position[c, x]
        return carry

    lax.fori_loop(0, 3, load, 0)
    fill_all(va, 4)
    relax_into(fine, weight_a, force, va, va2, 4)
    fill_all(va2, 4)
    relax_into(fine, weight_a, force, va2, va, 4)
    fill_all(va, 4)
    residual_down(fine, force, va, res_a, rhs_b, 4)

    for c in range(3):
        for x in range(2):
            vb[c, 1 + x, 1:3, 1:3] = weight_b[x] * rhs_b[c, x]
    fill_all(vb, 2)
    relax_into(level_b, weight_b, rhs_b, vb, vb2, 2)
    fill_all(vb2, 2)
    residual_down(level_b, rhs_b, vb2, res_b, rhs_c, 2)

    for c in range(3):
        vc[c, 1, 1, 1] = weight_c[0, 0, 0] * rhs_c[c, 0, 0, 0]
    fill_all(vc, 1)
    relax_into(level_c, weight_c, rhs_c, vc, vc2, 1)
    fill_all(vc2, 1)
    relax_into(level_c, weight_c, rhs_c, vc2, vc, 1)
    fill_all(vc, 1)
    relax_into(level_c, weight_c, rhs_c, vc, vc2, 1)
    fill_all(vc2, 1)

    add_prolonged(vc2, vb2, inside, 1)
    fill_all(vb2, 2)
    relax_into(level_b, weight_b, rhs_b, vb2, vb, 2)
    fill_all(vb, 2)
    relax_into(level_b, weight_b, rhs_b, vb, vb2, 2)
    fill_all(vb2, 2)

    add_prolonged(vb2, va, inside, 2)
    fill_all(va, 4)
    relax_into(fine, weight_a, force, va, va2, 4)
    fill_all(va2, 4)
    relax_into(fine, weight_a, force, va2, va, 4)

    def own_slab(tiles):
        total = None
        for group, tile in enumerate(tiles):
            moved = lane_roll(tile, 8 * group - 8)
            total = moved if total is None else jnp.where(slab == group, moved, total)
        return total

    def send_field(c, carry):
        for yp in range(4):
            lines = [own_slab([va[c, 1 + xp, 1 + yp, 1 + zp] for zp in range(4)]) for xp in range(4)]
            for dest, tile in enumerate(swap_groups(lines, 32)):
                out_ref[lax.bitwise_xor(gx_own, dest), pl.ds(32 * c + yp, ROWS, stride=4), :] = tile
        return carry

    lax.fori_loop(0, 3, send_field, 0)

    for g in range(7):
        for yp in range(2):
            lines = [
                own_slab([level_b[min(4 * g + o, 26), xp, yp, zp] for xp in range(2) for zp in range(2)])
                for o in range(4)
            ]
            for dest, tile in enumerate(swap_groups(lines, 32)):
                out_ref[lax.bitwise_xor(gx_own, dest), pl.ds(96 + 16 * g + yp, ROWS, stride=2), :] = tile

    side = lax.axis_index("gy")
    for j, ref in enumerate((out_own, out_one, out_two, out_three)):
        for c in range(3):
            ref[16 * c:16 * c + 16] = out_ref[j, pl.ds(pl.multiple_of(32 * c + 16 * side, 16), 16), :]
        for g in range(7):
            ref[48 + 8 * g:56 + 8 * g] = out_ref[j, pl.ds(pl.multiple_of(96 + 16 * g + 8 * side, 8), 8), :]


def slab_owner(place, gz):
    order = place if gz % 2 == 0 else 3 - place
    return SNAKE[order]


def vmem_specs(count):
    return [pl.BlockSpec(memory_space=pltpu.VMEM)] * count


def shards_by_slab(cell_weight, weight_grad, material, modulus, node_mass, pinned, positions, forces):
    smem = pl.BlockSpec(memory_space=pltpu.SMEM)
    gx, gy, gz = lax.axis_index("gx"), lax.axis_index("gy"), lax.axis_index("gz")
    f32 = jnp.float32
    index = 4 * gz + slab_place(gx, gz)
    packed = pl.pallas_call(
        pack_kernel,
        out_shape=[pltpu.VMEM((8, 16, LANES), f32)] * 4,
        in_specs=[smem] + vmem_specs(7),
        out_specs=vmem_specs(4),
        scratch_shapes=[pltpu.VMEM((4, 8, 16, LANES), f32)],
        name="pack",
    )(modulus, cell_weight, weight_grad, material, node_mass, pinned, positions, forces)

    mine = [packed[0]]
    for j in range(1, 4):
        mine.append(lax.ppermute(packed[j], "gx", [(i, i ^ j) for i in range(4)]))
    mine = jnp.stack(mine)

    def swap_in_chain(first):
        pairs = []
        for core in range(2):
            chain = [(slab_owner(at, z) * 2 + core) * 4 + z for z in range(4) for at in range(4)]
            for at in range(first, 15, 2):
                pairs += [(chain[at], chain[at + 1]), (chain[at + 1], chain[at])]
            if first:
                pairs += [(chain[end], chain[end] ^ 4) for end in (0, 15)]
        return lax.ppermute(mine, ("gx", "gy", "gz"), pairs)

    even, odd = swap_in_chain(0), swap_in_chain(1)

    def both_halves(half, present):
        other = lax.ppermute(half, "gy", [(0, 1), (1, 0)])
        rows = jnp.concatenate([jnp.where(gy == 0, half, other), jnp.where(gy == 0, other, half)], axis=2)
        return jnp.where(present, rows, 0.0)

    odd_place = index % 2 == 1
    own = both_halves(mine, True)
    even = both_halves(even, True)
    odd = both_halves(odd, (index > 0) & (index < 15))
    before = jnp.where(odd_place, even, odd)
    after = jnp.where(odd_place, odd, even)

    def buf(*dims):
        return pltpu.VMEM(tuple(dims) + TILE, f32)

    message = pl.pallas_call(
        cycle_kernel,
        out_shape=[pltpu.VMEM((104, LANES), f32)] * 4,
        in_specs=vmem_specs(3),
        out_specs=vmem_specs(4),
        scratch_shapes=[
            buf(8, 4, 4, 4), buf(5, 5, 5), buf(27, 4, 4, 4), buf(4, 4, 4),
            buf(27, 2, 4, 4), buf(27, 2, 2, 4), buf(27, 2, 2, 2), buf(2, 2, 2),
            buf(27, 1, 2, 2), buf(27, 1, 1, 2), buf(27, 1, 1, 1), buf(1, 1, 1),
            buf(3, 6, 6, 6), buf(3, 6, 6, 6), buf(3, 4, 4, 4), buf(3, 4, 4, 4), buf(3, 3, 3, 3), buf(3, 3, 3, 3),
            buf(3, 5, 5, 5), buf(3, 3, 3, 3), buf(3, 2, 2, 2), buf(3, 1, 1, 1),
            pltpu.VMEM((4, 208, LANES), f32),
            buf(5, 4, 4), buf(4, 5, 4), buf(4, 4, 5), buf(4, 4, 4), buf(3, 5, 5, 5),
        ],
        compiler_params=pltpu.CompilerParams(vmem_limit_bytes=48 * 1024 * 1024),
        name="cycle",
    )(before, own, after)

    back = [message[0]]
    for j in range(1, 4):
        back.append(lax.ppermute(message[j], "gx", [(i, i ^ j) for i in range(4)]))
    return pl.pallas_call(
        unpack_kernel,
        out_shape=[
            jax.ShapeDtypeStruct(positions.shape, f32),
            jax.ShapeDtypeStruct((27, 2, 8, 64), f32),
        ],
        in_specs=vmem_specs(4),
        out_specs=vmem_specs(2),
        scratch_shapes=[pltpu.VMEM((4, 104, LANES), f32)],
        compiler_params=pltpu.CompilerParams(vmem_limit_bytes=8 * 1024 * 1024),
        name="unpack",
    )(*back)


def solution(mesh):
    placed = (
        P("gx", "gy", "gz"),
        P("gx", "gy", "gz"),
        P("gx", "gy", "gz"),
        P(),
        P("gx", "gy", "gz"),
        P("gx", "gy", "gz"),
        P(None, "gx", "gy", "gz"),
        P(None, "gx", "gy", "gz"),
    )
    sizes = tuple(mesh.shape[axis] for axis in ("gx", "gy", "gz"))

    def choose(cell_weight, *rest):
        fits = sizes == (4, 2, 4) and cell_weight.shape == (4, 16, 128)
        return (shards_by_slab if fits else shards)(cell_weight, *rest)

    return jax.shard_map(
        choose,
        mesh=mesh,
        in_specs=placed,
        out_specs=(P(None, "gx", "gy", "gz"), P(None, "gx", "gy", "gz")),
        check_vma=False,
    )
```

```python
import jax
import jax.numpy as jnp
import numpy as np
from jax import lax
from jax.experimental import pallas as pl
from jax.experimental.pallas import tpu as pltpu
from jax.sharding import PartitionSpec as P

OMEGA = 0.6
LEARN_RATE = 0.5
PIN_WEIGHT = 4.0
ELEMENT_TERMS = (1.0 / 3.0, 0.0, -1.0 / 12.0, -1.0 / 12.0)


def shifted(x, axis, by):
    peers = lax.axis_size(axis)
    pairs = [(i, i + by) for i in range(peers) if 0 <= i + by < peers]
    return lax.ppermute(x, axis, pairs)


def extended(block, sides, width):
    for axis, dim in sides:
        count = lax.axis_size(axis)
        forward = [(i, i + 1) for i in range(count - 1)]
        backward = [(target, source) for source, target in forward]
        low = lax.ppermute(
            lax.slice_in_dim(block, block.shape[dim] - width, None, axis=dim), axis, forward
        )
        high = lax.ppermute(lax.slice_in_dim(block, 0, width, axis=dim), axis, backward)
        block = jnp.concatenate([low, block, high], axis=dim)
    return block


def offset_list():
    return [
        (shift_x, shift_y, shift_z)
        for shift_x in (-1, 0, 1)
        for shift_y in (-1, 0, 1)
        for shift_z in (-1, 0, 1)
    ]


def corner_list():
    return [(bit_x, bit_y, bit_z) for bit_x in (0, 1) for bit_y in (0, 1) for bit_z in (0, 1)]


def hat_weight(distance):
    if distance == 0:
        return 1.0
    if abs(distance) == 1:
        return 0.5
    return 0.0


def galerkin_tables():
    offsets = offset_list()
    tables = np.zeros((27, 27, 27), np.float32)
    for slot_a, outer in enumerate(offsets):
        for slot_c, coarse in enumerate(offsets):
            for slot_f, inner in enumerate(offsets):
                factor = 1.0
                for axis_pos in range(3):
                    factor *= hat_weight(outer[axis_pos]) * hat_weight(
                        2 * coarse[axis_pos] - outer[axis_pos] - inner[axis_pos]
                    )
                tables[slot_a, slot_c, slot_f] = factor
    return tables


def stiffness_of(cell_weight, weight_grad, material, modulus):
    lookup = jnp.zeros(cell_weight.shape, jnp.float32)
    for index in range(modulus.shape[0]):
        lookup = lookup + jnp.where(material == index, modulus[index], 0.0)
    return cell_weight * jnp.exp(-LEARN_RATE * weight_grad) * lookup


def assemble(cell_rim, node_mass, pinned_weight):
    node_shape = node_mass.shape
    rows_out = []
    for offset in offset_list():
        total = jnp.zeros(node_shape, jnp.float32)
        for corner in corner_list():
            if all((0 <= corner[axis_pos] + offset[axis_pos] <= 1 for axis_pos in range(3))):
                total = (
                    total
                    + cell_rim[
                        1 - corner[0] : 1 - corner[0] + node_shape[0],
                        1 - corner[1] : 1 - corner[1] + node_shape[1],
                        1 - corner[2] : 1 - corner[2] + node_shape[2],
                    ]
                )
        nonzero = sum((1 for axis_pos in range(3) if offset[axis_pos] != 0))
        entry = ELEMENT_TERMS[nonzero] * total
        if nonzero == 0:
            entry = entry + node_mass + PIN_WEIGHT * pinned_weight
        rows_out.append(entry)
    return jnp.stack(rows_out)


def galerkin(op_rim, coarse_shape):
    tables = jnp.asarray(galerkin_tables())
    result = None
    for slot_a, outer in enumerate(offset_list()):
        piece = op_rim[
            :,
            outer[0] + 1 : outer[0] + 1 + 2 * coarse_shape[0] : 2,
            outer[1] + 1 : outer[1] + 1 + 2 * coarse_shape[1] : 2,
            outer[2] + 1 : outer[2] + 1 + 2 * coarse_shape[2] : 2,
        ]
        term = jnp.einsum("pk,kxyz->pxyz", tables[slot_a], piece, precision=lax.Precision.HIGHEST)
        result = term if result is None else result + term
    return result


def stencil_apply(stencil, padded):
    node_shape = stencil.shape[1:]
    result = None
    for slot, offset in enumerate(offset_list()):
        window = padded[
            :,
            1 + offset[0] : 1 + offset[0] + node_shape[0],
            1 + offset[1] : 1 + offset[1] + node_shape[1],
            1 + offset[2] : 1 + offset[2] + node_shape[2],
        ]
        term = stencil[slot][None] * window
        result = term if result is None else result + term
    return result


def relax(stencil, field, rhs_field, padded):
    return field + OMEGA * (rhs_field - stencil_apply(stencil, padded)) / stencil[13][None]


def restrict_axis(field, axis_pos, coarse_len):
    below = lax.slice_in_dim(field, 0, 2 * coarse_len - 1, 2, axis_pos)
    centre = lax.slice_in_dim(field, 1, 2 * coarse_len, 2, axis_pos)
    above = lax.slice_in_dim(field, 2, 2 * coarse_len + 1, 2, axis_pos)
    return 0.5 * below + centre + 0.5 * above


def restrict(rim_field, coarse_shape):
    field = rim_field
    for axis_pos in (1, 2, 3):
        field = restrict_axis(field, axis_pos, coarse_shape[axis_pos - 1])
    return field


def prolong_axis(field, axis_pos, coarse_len):
    lower = lax.slice_in_dim(field, 0, coarse_len, 1, axis_pos)
    upper = lax.slice_in_dim(field, 1, coarse_len + 1, 1, axis_pos)
    middle = 0.5 * (lower + upper)
    paired = jnp.stack([lower, middle], axis=axis_pos + 1)
    new_shape = list(lower.shape)
    new_shape[axis_pos] = 2 * coarse_len
    return paired.reshape(new_shape)


def prolong(rim_field, coarse_shape):
    field = rim_field
    for axis_pos in (1, 2, 3):
        field = prolong_axis(field, axis_pos, coarse_shape[axis_pos - 1])
    return field


def boundary_layer(field, axis_pos, forward):
    extent = field.shape[axis_pos]
    if forward:
        return lax.slice_in_dim(field, extent - 1, extent, 1, axis_pos)
    return lax.slice_in_dim(field, 0, 1, 1, axis_pos)


def attach(field, layer_in, axis_pos, forward):
    if forward:
        return jnp.concatenate([layer_in, field], axis=axis_pos)
    return jnp.concatenate([field, layer_in], axis=axis_pos)


def extend(field, leading, forward):
    step = 1 if forward else -1
    got_x = shifted(boundary_layer(field, leading, forward), "gx", step)
    field = attach(field, got_x, leading, forward)
    got_y = shifted(boundary_layer(field, leading + 1, forward), "gy", step)
    field = attach(field, got_y, leading + 1, forward)
    got_z = shifted(boundary_layer(field, leading + 2, forward), "gz", step)
    return attach(field, got_z, leading + 2, forward)


def faces(field):
    return extended(field, (("gx", 1), ("gy", 2), ("gz", 3)), 1)


def shards(cell_weight, weight_grad, material, modulus, node_mass, pinned, positions, forces):
    stiffness = stiffness_of(cell_weight, weight_grad, material, modulus)
    fine_shape = node_mass.shape
    mid_shape = tuple((extent // 2 for extent in fine_shape))
    low_shape = tuple((extent // 4 for extent in fine_shape))
    pinned_weight = pinned.astype(jnp.float32)
    level_zero = assemble(extend(stiffness, 0, True), node_mass, pinned_weight)
    zero_rim = extend(level_zero, 1, True)
    level_one = galerkin(zero_rim, mid_shape)
    level_two = galerkin(extend(level_one, 1, True), low_shape)
    iterate = positions
    for sweep in range(2):
        iterate = relax(level_zero, iterate, forces, faces(iterate))
    residual_zero = forces - stencil_apply(level_zero, faces(iterate))
    rhs_one = restrict(extend(residual_zero, 1, True), mid_shape)
    corr_one = OMEGA * rhs_one / level_one[13][None]
    corr_one = relax(level_one, corr_one, rhs_one, faces(corr_one))
    residual_one = rhs_one - stencil_apply(level_one, faces(corr_one))
    rhs_two = restrict(extend(residual_one, 1, True), low_shape)
    corr_two = OMEGA * rhs_two / level_two[13][None]
    for sweep in range(3):
        corr_two = relax(level_two, corr_two, rhs_two, faces(corr_two))
    corr_one = corr_one + prolong(extend(corr_two, 1, False), low_shape)
    for sweep in range(2):
        corr_one = relax(level_one, corr_one, rhs_one, faces(corr_one))
    iterate = iterate + prolong(extend(corr_one, 1, False), mid_shape)
    for sweep in range(2):
        iterate = relax(level_zero, iterate, forces, faces(iterate))
    return (iterate, level_one)


LANES = 128
ROWS = 8
TILE = (ROWS, LANES)
SNAKE = (0, 1, 3, 2)


def lane_roll(x, by):
    return pltpu.roll(x, by % LANES, x.ndim - 1)


def row_roll(x, by):
    return pltpu.roll(x, by % ROWS, x.ndim - 2)


def lane_ids(shape):
    return lax.broadcasted_iota(jnp.int32, shape, len(shape) - 1)


def row_ids(shape):
    return lax.broadcasted_iota(jnp.int32, shape, len(shape) - 2)


def x_below(x):
    return jnp.where(lane_ids(x.shape) >= 32, lane_roll(x, 32), 0.0)


def x_above(x):
    return jnp.where(lane_ids(x.shape) < 96, lane_roll(x, -32), 0.0)


def y_below(x):
    return jnp.where(row_ids(x.shape) >= 1, row_roll(x, 1), 0.0)


def y_above(x):
    return jnp.where(row_ids(x.shape) < ROWS - 1, row_roll(x, -1), 0.0)


def z_below(x):
    return lane_roll(x, 1)


def z_above(x):
    return lane_roll(x, -1)


def swap_groups(parts, unit):
    group = lane_ids(parts[0].shape) // unit
    parts = list(parts)
    for bit in (1, 2):
        low = (group & bit) == 0
        for i in range(4):
            if i & bit == 0:
                a, b = parts[i], parts[i + bit]
                parts[i] = jnp.where(low, a, lane_roll(b, unit * bit))
                parts[i + bit] = jnp.where(low, lane_roll(a, -unit * bit), b)
    return parts


def pick_lanes(x, source):
    return jnp.take_along_axis(x, jnp.broadcast_to(source, x.shape), axis=-1)


def slab_place(gx, gz):
    order = jnp.where(gx < 2, gx, 5 - gx)
    return jnp.where(lax.rem(gz, 2) == 0, order, 3 - order)


def owner_of(place, gz):
    order = jnp.where(lax.rem(gz, 2) == 0, place, 3 - place)
    return jnp.where(order < 2, order, 5 - order)


def slab_partners():
    gx, gz = lax.axis_index("gx"), lax.axis_index("gz")
    return [lax.bitwise_xor(gx, owner_of(t, gz)) for t in range(4)]


def pack_kernel(
    mod_ref, cw_ref, wg_ref, mat_ref, mass_ref, pin_ref, pos_ref, force_ref, out_0, out_1, out_2, out_3, out_ref,
):
    partners = slab_partners()
    material = mat_ref[...]
    lookup = jnp.zeros(material.shape, jnp.float32)
    for index in range(mod_ref.shape[0]):
        lookup = jnp.where(material == index, mod_ref[index], lookup)
    stiff = cw_ref[...] * jnp.exp(-LEARN_RATE * wg_ref[...]) * lookup
    mass = mass_ref[...] + PIN_WEIGHT * pin_ref[...].astype(jnp.float32)
    fields = [stiff, mass] + [pos_ref[c] for c in range(3)] + [force_ref[c] for c in range(3)]
    lane = lane_ids((16, LANES))
    source = (lane // 32) * 32 + (lane % 8) * 4 + (lane % 32) // 8
    for f, field in enumerate(fields):
        moved = swap_groups([pick_lanes(field[x], source) for x in range(4)], 32)
        for t in range(4):
            out_ref[partners[t], f] = moved[t]
    for j, ref in enumerate((out_0, out_1, out_2, out_3)):
        ref[...] = out_ref[j]


def unpack_kernel(own_ref, one_ref, two_ref, three_ref, iterate_ref, level_ref, hold):
    for j, ref in enumerate((own_ref, one_ref, two_ref, three_ref)):
        hold[j] = ref[...]
    blocks = slab_partners()
    lane = lane_ids((16, LANES))
    source = (lane // 32) * 32 + (lane % 4) * 8 + (lane % 32) // 4
    for c in range(3):
        moved = swap_groups([hold[j, 16 * c:16 * c + 16] for j in blocks], 32)
        for x in range(4):
            iterate_ref[c, x] = pick_lanes(moved[x], source)
    lane = lane_ids(TILE)
    source = ((lane % 64) // 16) * 32 + (lane % 2) * 8 + (lane % 16) // 2
    for g in range(7):
        moved = swap_groups([hold[j, 48 + 8 * g:56 + 8 * g] for j in blocks], 32)
        for o in range(4):
            if 4 * g + o < 27:
                for x in range(2):
                    level_ref[4 * g + o, x] = pick_lanes(moved[o], source + 16 * x)[:, :64]


def fill_low(ref, n):
    ref[0, 1:, 1:] = x_below(ref[n, 1:, 1:])
    ref[:, 0, 1:] = y_below(ref[:, n, 1:])
    ref[:, :, 0] = z_below(ref[:, :, n])


def fill_both(ref, n):
    mid = slice(1, n + 1)
    ref[0, mid, mid] = x_below(ref[n, mid, mid])
    ref[n + 1, mid, mid] = x_above(ref[1, mid, mid])
    ref[:, 0, mid] = y_below(ref[:, n, mid])
    ref[:, n + 1, mid] = y_above(ref[:, 1, mid])
    ref[:, :, 0] = z_below(ref[:, :, n])
    ref[:, :, n + 1] = z_above(ref[:, :, 1])


def add(*terms):
    total = None
    for term in terms:
        if term is not None:
            total = term if total is None else total + term
    return total


def coarsen(low, mid, high, before, count):
    def scaled(x, factor):
        return None if x is None else factor * x

    leads = []
    for i in range(count):
        half = scaled(mid(2 * i + 1), 0.5)
        leads.append((add(low(2 * i + 1), half), add(high(2 * i + 1), half)))
    wrapped = tuple(None if x is None else before(x) for x in leads[-1])
    out = []
    for i in range(count):
        to_low, to_high = leads[i]
        from_low, from_high = leads[i - 1] if i else wrapped
        here = add(scaled(mid(2 * i), 2.0), low(2 * i), high(2 * i), to_low, from_high)
        out.append((add(low(2 * i), from_low), here, add(high(2 * i), to_high)))
    return out


def triple_product(src, mid_a, mid_b, dst, n, faces):
    half = n // 2
    looped = n == 4

    def pass_x(j, y, skip):
        def part(f):
            return lambda i: None if f in skip else src[9 * f + j, i, y]

        for i, trio in enumerate(coarsen(part(0), part(1), part(2), x_below, half)):
            for c in range(3):
                mid_a[9 * c + j, i, y] = trio[c]

    def all_x(y, carry):
        for j in range(9):
            crossed = (j // 3 != 1) + (j % 3 != 1)
            skip = () if not faces or crossed == 2 else ((1,) if crossed == 1 else (0, 2))
            pass_x(j, y, skip)
        return carry

    lax.fori_loop(0, n, all_x, 0, unroll=not looped)

    def pass_y(j, carry):
        base = 9 * (j // 3) + j % 3

        def part(f):
            return lambda i: mid_a[base + 3 * f, :, i]

        for i, trio in enumerate(coarsen(part(0), part(1), part(2), y_below, half)):
            for c in range(3):
                mid_b[base + 3 * c, :, i] = trio[c]
        return carry

    lax.fori_loop(0, 9, pass_y, 0, unroll=not looped)

    def pass_z(j, carry):
        def part(f):
            return lambda i: mid_b[3 * j + f, :, :, i]

        for i, trio in enumerate(coarsen(part(0), part(1), part(2), z_below, half)):
            for c in range(3):
                dst[3 * j + c, :, :, i] = 0.125 * trio[c]
        return carry

    lax.fori_loop(0, 9, pass_z, 0, unroll=not looped)


def sweep(level, field, n, store):
    def body(step, carry):
        x, y = step // n, step % n
        sums = [[None] * n for _ in range(3)]
        for o0 in range(3):
            for o1 in range(3):
                columns = [[field[c, x + o0, y + o1, z] for z in range(n + 2)] for c in range(3)]
                for o2 in range(3):
                    for z in range(n):
                        coef = level[9 * o0 + 3 * o1 + o2, x, y, z]
                        for c in range(3):
                            term = coef * columns[c][z + o2]
                            sums[c][z] = term if sums[c][z] is None else sums[c][z] + term
        for c in range(3):
            for z in range(n):
                store(c, x, y, z, sums[c][z])
        return carry

    lax.fori_loop(0, n * n, body, 0, unroll=True)


def cell_sweep(parts, field, store):
    cells, edge_x, edge_y, edge_z, diag, sums = parts

    def gather(c, carry):
        for x in range(4):
            pair = [[field[c, 1 + x, 1 + y, 1 + z] + field[c, 2 + x, 1 + y, 1 + z] for z in range(5)] for y in range(5)]
            for y in range(4):
                quad = [pair[y][z] + pair[y + 1][z] for z in range(5)]
                for z in range(4):
                    sums[c, 1 + x, 1 + y, 1 + z] = cells[1 + x, 1 + y, 1 + z] * (quad[z] + quad[z + 1])
        fill_low(sums.at[c], 4)
        return carry

    lax.fori_loop(0, 3, gather, 0, unroll=True)

    for x in range(4):
        for y in range(4):
            for c in range(3):
                near = [
                    (sums[c, x, y, z] + sums[c, x, y + 1, z]) + (sums[c, x + 1, y, z] + sums[c, x + 1, y + 1, z])
                    for z in range(5)
                ]
                line = [field[c, 1 + x, 1 + y, z] for z in range(6)]
                for z in range(4):
                    value = diag[x, y, z] * line[1 + z] + (near[z] + near[z + 1])
                    value = value - edge_x[x, y, z] * field[c, x, 1 + y, 1 + z]
                    value = value - edge_x[x + 1, y, z] * field[c, x + 2, 1 + y, 1 + z]
                    value = value - edge_y[x, y, z] * field[c, 1 + x, y, 1 + z]
                    value = value - edge_y[x, y + 1, z] * field[c, 1 + x, y + 2, 1 + z]
                    value = value - edge_z[x, y, z] * line[z]
                    value = value - edge_z[x, y, z + 1] * line[z + 2]
                    store(c, x, y, z, value)


def apply_level(level, field, n, store):
    if n == 4:
        cell_sweep(level, field, store)
    else:
        sweep(level, field, n, store)


def relax_into(level, weight, rhs, src, dst, n):
    def store(c, x, y, z, value):
        dst[c, 1 + x, 1 + y, 1 + z] = src[c, 1 + x, 1 + y, 1 + z] + weight[x, y, z] * (rhs[c, x, y, z] - value)

    apply_level(level, src, n, store)


def residual_down(level, rhs, src, res, coarse_rhs, n):
    half = n // 2

    def store(c, x, y, z, value):
        res[c, 1 + x, 1 + y, 1 + z] = rhs[c, x, y, z] - value

    apply_level(level, src, n, store)

    def body(c, carry):
        fill_low(res.at[c], n)
        for i in range(half):
            part = 0.5 * (res[c, 2 * i] + res[c, 2 * i + 2]) + res[c, 2 * i + 1]
            for j in range(half):
                line = 0.5 * (part[2 * j] + part[2 * j + 2]) + part[2 * j + 1]
                for k in range(half):
                    coarse_rhs[c, i, j, k] = 0.5 * (line[2 * k] + line[2 * k + 2]) + line[2 * k + 1]
        return carry

    lax.fori_loop(0, 3, body, 0, unroll=True)


def add_prolonged(coarse, fine, inside, half):
    def between(values):
        out = []
        for i in range(half):
            out += [values[i], 0.5 * (values[i] + values[i + 1])]
        return out

    def body(c, carry):
        planes = between([coarse[c, 1 + i, 1:, 1:] for i in range(half + 1)])
        for x, plane in enumerate(planes):
            for y, line in enumerate(between([plane[j] for j in range(half + 1)])):
                for z, value in enumerate(between([line[k] for k in range(half + 1)])):
                    fine[c, 1 + x, 1 + y, 1 + z] += jnp.where(inside, value, 0.0)
        return carry

    lax.fori_loop(0, 3, body, 0, unroll=half < 2)


def fill_all(ref, n):
    def body(c, carry):
        fill_both(ref.at[c], n)
        return carry

    lax.fori_loop(0, 3, body, 0, unroll=True)


def cycle_kernel(
    prev_ref, own_ref, next_ref, out_own, out_one, out_two, out_three,
    fields, cells, level_a, weight_a, mid_a, mid_b, level_b, weight_b, mid_c, mid_d, level_c, weight_c,
    va, va2, vb, vb2, vc, vc2, res_a, res_b, rhs_b, rhs_c, out_ref,
    edge_x, edge_y, edge_z, diag, sums,
):
    gx_own, gz = lax.axis_index("gx"), lax.axis_index("gz")
    index = 4 * gz + slab_place(gx_own, gz)
    below, above = lax.max(index - 1, 0), lax.min(index + 1, 15)
    gx_prev = owner_of(lax.rem(below, 4), lax.div(below, 4))
    gx_next = owner_of(lax.rem(above, 4), lax.div(above, 4))
    slab = (lane_ids(TILE) // 8) % 4
    inside = (slab == 1) | ((slab == 0) & (index > 0)) | ((slab == 2) & (index < 15))

    def arrange(step, carry):
        f = step
        for yp in range(4):
            by_source = []
            for source in range(4):
                tiles = [
                    ref[lax.bitwise_xor(gx, source), f, pl.ds(yp, ROWS, stride=4), :]
                    for ref, gx in ((prev_ref, gx_prev), (own_ref, gx_own), (next_ref, gx_next))
                ]
                by_source.append(swap_groups(tiles + [jnp.zeros(TILE, jnp.float32)], 8))
            for zp in range(4):
                moved = swap_groups([by_source[source][zp] for source in range(4)], 32)
                for xp in range(4):
                    fields[f, xp, yp, zp] = moved[xp]
        return carry

    lax.fori_loop(0, 8, arrange, 0)

    for x in range(4):
        cells[1 + x, 1:, 1:] = fields[0, x] * ELEMENT_TERMS[3]
    fill_low(cells, 4)

    def build(step, carry):
        x, y = step // 4, step % 4
        near = [[[cells[x + 1 - s0, y + 1 - s1, z] for z in range(5)] for s1 in (0, 1)] for s0 in (0, 1)]
        for z in range(4):
            for slot, offset in enumerate(offset_list()):
                nonzero = sum(1 for part in offset if part != 0)
                if nonzero == 1:
                    continue
                total = None
                for s in corner_list():
                    if all(0 <= s[d] + offset[d] <= 1 for d in range(3)):
                        term = near[s[0]][s[1]][z + 1 - s[2]]
                        total = term if total is None else total + term
                if nonzero == 0:
                    mass = fields[1, x, y, z]
                    diag[x, y, z] = ((ELEMENT_TERMS[0] - ELEMENT_TERMS[3]) / ELEMENT_TERMS[3]) * total + mass
                    total = (ELEMENT_TERMS[0] / ELEMENT_TERMS[3]) * total + mass
                    weight_a[x, y, z] = jnp.where(inside, OMEGA / jnp.where(inside, total, 1.0), 0.0)
                level_a[slot, x, y, z] = total
        return carry

    lax.fori_loop(0, 16, build, 0)

    edge_z[...] = (cells[1:, 1:] + cells[:4, 1:]) + (cells[1:, :4] + cells[:4, :4])
    over_z = cells[:, :, 1:] + cells[:, :, :4]
    edge_x[...] = over_z[:, 1:] + over_z[:, :4]
    edge_y[...] = over_z[1:] + over_z[:4]
    fine = (cells, edge_x, edge_y, edge_z, diag, sums)

    triple_product(level_a, mid_a, mid_b, level_b, 4, True)
    weight_b[...] = jnp.where(inside, OMEGA / jnp.where(inside, level_b[13], 1.0), 0.0)
    triple_product(level_b, mid_c, mid_d, level_c, 2, False)
    weight_c[...] = jnp.where(inside, OMEGA / jnp.where(inside, level_c[13], 1.0), 0.0)

    position, force = fields.at[2:5], fields.at[5:8]

    def load(c, carry):
        for x in range(4):
            va[c, 1 + x, 1:5, 1:5] = position[c, x]
        return carry

    lax.fori_loop(0, 3, load, 0)
    fill_all(va, 4)
    relax_into(fine, weight_a, force, va, va2, 4)
    fill_all(va2, 4)
    relax_into(fine, weight_a, force, va2, va, 4)
    fill_all(va, 4)
    residual_down(fine, force, va, res_a, rhs_b, 4)

    for c in range(3):
        for x in range(2):
            vb[c, 1 + x, 1:3, 1:3] = weight_b[x] * rhs_b[c, x]
    fill_all(vb, 2)
    relax_into(level_b, weight_b, rhs_b, vb, vb2, 2)
    fill_all(vb2, 2)
    residual_down(level_b, rhs_b, vb2, res_b, rhs_c, 2)

    for c in range(3):
        vc[c, 1, 1, 1] = weight_c[0, 0, 0] * rhs_c[c, 0, 0, 0]
    fill_all(vc, 1)
    relax_into(level_c, weight_c, rhs_c, vc, vc2, 1)
    fill_all(vc2, 1)
    relax_into(level_c, weight_c, rhs_c, vc2, vc, 1)
    fill_all(vc, 1)
    relax_into(level_c, weight_c, rhs_c, vc, vc2, 1)
    fill_all(vc2, 1)

    add_prolonged(vc2, vb2, inside, 1)
    fill_all(vb2, 2)
    relax_into(level_b, weight_b, rhs_b, vb2, vb, 2)
    fill_all(vb, 2)
    relax_into(level_b, weight_b, rhs_b, vb, vb2, 2)
    fill_all(vb2, 2)

    add_prolonged(vb2, va, inside, 2)
    fill_all(va, 4)
    relax_into(fine, weight_a, force, va, va2, 4)
    fill_all(va2, 4)
    relax_into(fine, weight_a, force, va2, va, 4)

    def own_slab(tiles):
        total = None
        for group, tile in enumerate(tiles):
            moved = lane_roll(tile, 8 * group - 8)
            total = moved if total is None else jnp.where(slab == group, moved, total)
        return total

    def send_field(c, carry):
        for yp in range(4):
            lines = [own_slab([va[c, 1 + xp, 1 + yp, 1 + zp] for zp in range(4)]) for xp in range(4)]
            for dest, tile in enumerate(swap_groups(lines, 32)):
                out_ref[lax.bitwise_xor(gx_own, dest), pl.ds(32 * c + yp, ROWS, stride=4), :] = tile
        return carry

    lax.fori_loop(0, 3, send_field, 0)

    for g in range(7):
        for yp in range(2):
            lines = [
                own_slab([level_b[min(4 * g + o, 26), xp, yp, zp] for xp in range(2) for zp in range(2)])
                for o in range(4)
            ]
            for dest, tile in enumerate(swap_groups(lines, 32)):
                out_ref[lax.bitwise_xor(gx_own, dest), pl.ds(96 + 16 * g + yp, ROWS, stride=2), :] = tile

    side = lax.axis_index("gy")
    for j, ref in enumerate((out_own, out_one, out_two, out_three)):
        for c in range(3):
            ref[16 * c:16 * c + 16] = out_ref[j, pl.ds(pl.multiple_of(32 * c + 16 * side, 16), 16), :]
        for g in range(7):
            ref[48 + 8 * g:56 + 8 * g] = out_ref[j, pl.ds(pl.multiple_of(96 + 16 * g + 8 * side, 8), 8), :]


def slab_owner(place, gz):
    order = place if gz % 2 == 0 else 3 - place
    return SNAKE[order]


def vmem_specs(count):
    return [pl.BlockSpec(memory_space=pltpu.VMEM)] * count


def shards_by_slab(cell_weight, weight_grad, material, modulus, node_mass, pinned, positions, forces):
    smem = pl.BlockSpec(memory_space=pltpu.SMEM)
    gx, gy, gz = lax.axis_index("gx"), lax.axis_index("gy"), lax.axis_index("gz")
    f32 = jnp.float32
    index = 4 * gz + slab_place(gx, gz)
    packed = pl.pallas_call(
        pack_kernel,
        out_shape=[pltpu.VMEM((8, 16, LANES), f32)] * 4,
        in_specs=[smem] + vmem_specs(7),
        out_specs=vmem_specs(4),
        scratch_shapes=[pltpu.VMEM((4, 8, 16, LANES), f32)],
        name="pack",
    )(modulus, cell_weight, weight_grad, material, node_mass, pinned, positions, forces)

    mine = [packed[0]]
    for j in range(1, 4):
        mine.append(lax.ppermute(packed[j], "gx", [(i, i ^ j) for i in range(4)]))
    mine = jnp.stack(mine)

    def swap_in_chain(first):
        pairs = []
        for core in range(2):
            chain = [(slab_owner(at, z) * 2 + core) * 4 + z for z in range(4) for at in range(4)]
            for at in range(first, 15, 2):
                pairs += [(chain[at], chain[at + 1]), (chain[at + 1], chain[at])]
            if first:
                pairs += [(chain[end], chain[end] ^ 4) for end in (0, 15)]
        return lax.ppermute(mine, ("gx", "gy", "gz"), pairs)

    even, odd = swap_in_chain(0), swap_in_chain(1)

    def both_halves(half, present):
        other = lax.ppermute(half, "gy", [(0, 1), (1, 0)])
        rows = jnp.concatenate([jnp.where(gy == 0, half, other), jnp.where(gy == 0, other, half)], axis=2)
        return jnp.where(present, rows, 0.0)

    odd_place = index % 2 == 1
    own = both_halves(mine, True)
    even = both_halves(even, True)
    odd = both_halves(odd, (index > 0) & (index < 15))
    before = jnp.where(odd_place, even, odd)
    after = jnp.where(odd_place, odd, even)

    def buf(*dims):
        return pltpu.VMEM(tuple(dims) + TILE, f32)

    message = pl.pallas_call(
        cycle_kernel,
        out_shape=[pltpu.VMEM((104, LANES), f32)] * 4,
        in_specs=vmem_specs(3),
        out_specs=vmem_specs(4),
        scratch_shapes=[
            buf(8, 4, 4, 4), buf(5, 5, 5), buf(27, 4, 4, 4), buf(4, 4, 4),
            buf(27, 2, 4, 4), buf(27, 2, 2, 4), buf(27, 2, 2, 2), buf(2, 2, 2),
            buf(27, 1, 2, 2), buf(27, 1, 1, 2), buf(27, 1, 1, 1), buf(1, 1, 1),
            buf(3, 6, 6, 6), buf(3, 6, 6, 6), buf(3, 4, 4, 4), buf(3, 4, 4, 4), buf(3, 3, 3, 3), buf(3, 3, 3, 3),
            buf(3, 5, 5, 5), buf(3, 3, 3, 3), buf(3, 2, 2, 2), buf(3, 1, 1, 1),
            pltpu.VMEM((4, 208, LANES), f32),
            buf(5, 4, 4), buf(4, 5, 4), buf(4, 4, 5), buf(4, 4, 4), buf(3, 5, 5, 5),
        ],
        compiler_params=pltpu.CompilerParams(vmem_limit_bytes=48 * 1024 * 1024),
        name="cycle",
    )(before, own, after)

    back = [message[0]]
    for j in range(1, 4):
        back.append(lax.ppermute(message[j], "gx", [(i, i ^ j) for i in range(4)]))
    return pl.pallas_call(
        unpack_kernel,
        out_shape=[
            jax.ShapeDtypeStruct(positions.shape, f32),
            jax.ShapeDtypeStruct((27, 2, 8, 64), f32),
        ],
        in_specs=vmem_specs(4),
        out_specs=vmem_specs(2),
        scratch_shapes=[pltpu.VMEM((4, 104, LANES), f32)],
        compiler_params=pltpu.CompilerParams(vmem_limit_bytes=8 * 1024 * 1024),
        name="unpack",
    )(*back)


def solution(mesh):
    placed = (
        P("gx", "gy", "gz"),
        P("gx", "gy", "gz"),
        P("gx", "gy", "gz"),
        P(),
        P("gx", "gy", "gz"),
        P("gx", "gy", "gz"),
        P(None, "gx", "gy", "gz"),
        P(None, "gx", "gy", "gz"),
    )
    sizes = tuple(mesh.shape[axis] for axis in ("gx", "gy", "gz"))

    def choose(cell_weight, *rest):
        fits = sizes == (4, 2, 4) and cell_weight.shape == (4, 16, 128)
        return (shards_by_slab if fits else shards)(cell_weight, *rest)

    return jax.shard_map(
        choose,
        mesh=mesh,
        in_specs=placed,
        out_specs=(P(None, "gx", "gy", "gz"), P(None, "gx", "gy", "gz")),
        check_vma=False,
    )
```
